32 devices in a mesh: dp: 2 (over y), ctx: 4 (over z), tensor: 4 (over x, core).
Axes of the slice: x: 2, y: 2, z: 4, core: 2. Of those that a mesh axis runs over, the one named last changes fastest.
Arguments:
- hidden: bfloat16 [2, 2048, 2048], P('dp', 'ctx'), may hold values from -17 to 17
- cotangent: bfloat16 [2, 2048, 2048], P('dp', 'ctx'), may hold values from -6 to 6
- norm1_gain: float32 [2048], replicated, may hold values from 0.5 to 1.5
- ssm_in: bfloat16 [2048, 2, 3072], P(None, None, 'tensor'), may hold values from -0.125 to 0.125
- ssm_bc: bfloat16 [2048, 2, 256], replicated, may hold values from -0.125 to 0.125
- ssm_dt: bfloat16 [2048, 48], P(None, 'tensor'), may hold values from -0.125 to 0.125
- dt_bias: float32 [48], P('tensor'), may hold values from -7 to -5
- a_log: float32 [48], P('tensor'), may hold values from -4.6 to 2.3
- d_skip: float32 [48], P('tensor'), may hold values from 0.5 to 2
- ssm_out: bfloat16 [3072, 2048], P('tensor'), may hold values from -0.109375 to 0.109375
- attn_q: bfloat16 [2048, 1024], P(None, 'tensor'), may hold values from -0.125 to 0.125
- attn_kv: bfloat16 [2048, 2, 256], replicated, may hold values from -0.125 to 0.125
- attn_out: bfloat16 [1024, 2048], P('tensor'), may hold values from -4 to 4
- norm2_gain: float32 [2048], replicated, may hold values from 0.5 to 1.5
- mlp_gate_up: bfloat16 [2048, 2, 4096], P(None, None, 'tensor'), may hold values from -0.125 to 0.125
- mlp_down: bfloat16 [4096, 2048], P('tensor'), may hold values from -0.09375 to 0.09375
Outputs:
- output: bfloat16 [2, 2048, 2048], P('dp', 'ctx')
- grad_hidden: bfloat16 [2, 2048, 2048], P('dp', 'ctx')
- grad_norm1_gain: float32 [2048], P(('dp', 'ctx'))
- grad_ssm_in: float32 [2048, 2, 3072], P(('dp', 'ctx'), None, 'tensor')
- grad_ssm_bc: float32 [2048, 2, 256], P(('dp', 'ctx'))
- grad_ssm_dt: float32 [2048, 48], P(('dp', 'ctx'), 'tensor')
- grad_dt_bias: float32 [48], P('tensor')
- grad_a_log: float32 [48], P('tensor')
- grad_d_skip: float32 [48], P('tensor')
- grad_ssm_out: float32 [3072, 2048], P('tensor', ('dp', 'ctx'))
- grad_attn_q: float32 [2048, 1024], P(('dp', 'ctx'), 'tensor')
- grad_attn_kv: float32 [2048, 2, 256], P(('dp', 'ctx', 'tensor'))
- grad_attn_out: float32 [1024, 2048], P('tensor', ('dp', 'ctx'))
- grad_norm2_gain: float32 [2048], P(('dp', 'ctx'))
- grad_mlp_gate_up: float32 [2048, 2, 4096], P(('dp', 'ctx'), None, 'tensor')
- grad_mlp_down: float32 [4096, 2048], P('tensor', ('dp', 'ctx'))
- branch_rms: float32 [3], replicated
The draws below stay inside these ranges and needn't reach their ends.
All inputs are finite; a program needn't handle non-finite values.
Results may differ from the reference program's by a relative error of at most 0.013.
The reference program's roundings to bfloat16 on the way count: a program that leaves them out, or rounds other values in their place, can miss the bound.
Values may be sent and summed in bfloat16 or wider, within the bound.
No kernel may reach another device: no remote copies, remote signals or barrier semaphores. Data moves between devices by JAX's collectives and lax.ppermute only.
A program may use at most 320 MiB of HBM per device.

```python
import math
import jax
import jax.numpy as jnp
from jax import lax

D = 2048
MHEADS = 48
HEADDIM = 64
STATE = 256
AHEADS = 8
KVHEADS = 2
AHEAD_DIM = 128
FF = 4096
SCAN_BLOCK = 256
QBLOCK = 512
MINNER = 3072
SEQS = 2
LEN = 2048


def draw_hidden(key, part):
    key = jax.random.fold_in(key, 11)
    row_total = SEQS * LEN
    order = jnp.arange(row_total, dtype=jnp.float32).reshape(SEQS, LEN, 1) / row_total
    ramp = jnp.exp(order * math.log(3.0))
    jitter = jax.random.uniform(jax.random.fold_in(key, 1), (SEQS, LEN, 1), jnp.float32, 0.7, 1.4)
    base = jnp.clip(jax.random.normal(jax.random.fold_in(key, 2), (SEQS, LEN, D), jnp.float32), -4.0, 4.0)
    return (base * ramp * jitter).astype(jnp.bfloat16)


def steps_of(stream_key, shape, shards, low, high):
    def one(axis_at, parts):
        heights = jax.random.uniform(jax.random.fold_in(jax.random.fold_in(stream_key, 6), axis_at), (parts,), jnp.float32, low / len(shards), high / len(shards))
        return jnp.repeat(jnp.exp(heights), shape[axis_at] // parts).reshape((-1,) + (1,) * (len(shape) - axis_at - 1))

    level = one(*shards[0])
    for cut in shards[1:]:
        level = level * one(*cut)
    return level


def normal_values(own_key, shape, scale, bound, cuts=(), kind=jnp.bfloat16):
    drawn = scale * jax.random.normal(own_key, shape, jnp.float32)
    if cuts:
        drawn = drawn * steps_of(own_key, shape, cuts, -0.22, 0.18)
    return jnp.clip(drawn, -bound, bound).astype(kind)


def setup_inputs(seed: int = 0) -> dict:
    splits = jax.random.split(jax.random.key(seed), 17)
    return {
        "hidden": draw_hidden(jax.random.fold_in(splits[16], 71), 0),
        "cotangent": normal_values(splits[1], (SEQS, LEN, D), 1.0, 6.0, ((0, 2), (1, 4))),
        "norm1_gain": jnp.clip(1.0 + 0.1 * jax.random.normal(splits[2], (D,), jnp.float32), 0.5, 1.5),
        "ssm_in": normal_values(splits[3], (D, 2, MINNER), D ** -0.5, 0.125, ((2, 4),)),
        "ssm_bc": normal_values(splits[4], (D, 2, STATE), D ** -0.5, 0.125),
        "ssm_dt": normal_values(splits[5], (D, MHEADS), D ** -0.5, 0.125, ((1, 4),)),
        "dt_bias": jnp.clip(-7.0 + 2.0 * jax.random.uniform(splits[6], (MHEADS,), jnp.float32) ** steps_of(splits[6], (MHEADS,), ((0, 4),), -0.2, 0.2), -7.0, -5.0),
        "a_log": jnp.clip(-4.6 + 6.8999998569488525 * jax.random.uniform(splits[7], (MHEADS,), jnp.float32) ** steps_of(splits[7], (MHEADS,), ((0, 4),), -0.2, 0.2), -4.6, 2.3),
        "d_skip": jnp.clip(0.5 + 1.5 * jax.random.uniform(splits[8], (MHEADS,), jnp.float32) ** steps_of(splits[8], (MHEADS,), ((0, 4),), -0.2, 0.2), 0.5, 2.0),
        "ssm_out": normal_values(splits[9], (MINNER, D), MINNER ** -0.5, 0.109375, ((0, 4),)),
        "attn_q": normal_values(splits[10], (D, AHEADS * AHEAD_DIM), D ** -0.5, 0.125, ((1, 4),)),
        "attn_kv": normal_values(splits[11], (D, 2, KVHEADS * AHEAD_DIM), D ** -0.5, 0.125),
        "attn_out": normal_values(splits[12], (AHEADS * AHEAD_DIM, D), (max(1, AHEADS * AHEAD_DIM * 4 // LEN)) ** -0.5, 4.0, ((0, 4),)),
        "norm2_gain": jnp.clip(1.0 + 0.1 * jax.random.normal(splits[13], (D,), jnp.float32), 0.5, 1.5),
        "mlp_gate_up": normal_values(splits[14], (D, 2, FF), D ** -0.5, 0.125, ((2, 4),)),
        "mlp_down": normal_values(splits[15], (FF, D), FF ** -0.5, 0.09375, ((0, 4),)),
    }


EPSILON = 1e-05
NEG_FILL = -1e+30
PRECISE = lax.Precision.HIGHEST

@jax.custom_vjp
def low(v):
    return lax.optimization_barrier(v.astype(jnp.bfloat16)).astype(jnp.float32)

@jax.custom_vjp
def low_back(v):
    return v

def low_keep(v):
    return (low(v), None)

def low_pass(kept, grad):
    return (grad,)

def back_keep(v):
    return (v, None)

def back_low(kept, grad):
    return (low(grad),)
low.defvjp(low_keep, low_pass)
low_back.defvjp(back_keep, back_low)

def matmul_high(former, latter):
    return jnp.dot(former, latter, precision=PRECISE)

def rms_normed(source, gain):
    return source * lax.rsqrt(lax.optimization_barrier(jnp.mean(source * source, axis=-1, keepdims=True)) + EPSILON) * gain

def ssd_block(states, pieces, decay_rate, skip_gain):
    source_block, write_block, read_block, step_block = pieces
    increments = step_block * decay_rate
    running = jnp.cumsum(increments, axis=0)
    block_len = increments.shape[0]
    lower_mask = jnp.arange(block_len, dtype=jnp.int32)[:, None] >= jnp.arange(block_len, dtype=jnp.int32)[None, :]
    differences = running[:, None, :] - running[None, :, :]
    decays = jnp.exp(jnp.where(lower_mask[:, :, None], differences, NEG_FILL))
    intersection = jnp.dot(read_block, write_block.T, precision=PRECISE)
    mixing = decays * intersection[:, :, None] * step_block[None, :, :]
    within = jnp.einsum('tsh,shp->thp', mixing, source_block, precision=PRECISE)
    carried = jnp.einsum('tn,hpn->thp', read_block, states, precision=PRECISE) * jnp.exp(running)[:, :, None]
    result = within + carried + skip_gain[None, :, None] * source_block
    tailing = jnp.exp(running[-1][None, :] - running) * step_block
    incoming = jnp.einsum('sh,shp,sn->hpn', tailing, source_block, write_block, precision=PRECISE)
    states = states * jnp.exp(running[-1])[:, None, None] + incoming
    return (states, result)

def run_ssd(source_heads, write_rows, read_rows, step_rows, a_log, d_skip, entering, block_len):
    row_total = source_heads.shape[0]
    block_count = row_total // block_len
    decay_rate = -jnp.exp(a_log)

    def blocked(source):
        return source.reshape((block_count, block_len) + source.shape[1:])

    def stepper(states, pieces):
        return ssd_block(states, pieces, decay_rate, d_skip)
    closing, outputs = lax.scan(jax.checkpoint(stepper), entering, (blocked(source_heads), blocked(write_rows), blocked(read_rows), blocked(step_rows)))
    return (outputs.reshape(source_heads.shape), closing)

def attention(queries, key_value):
    length = queries.shape[0]
    group_size = AHEADS // KVHEADS
    kv_split = KVHEADS * AHEAD_DIM
    key_rows = key_value[:, :kv_split].reshape(length, KVHEADS, AHEAD_DIM)
    value_rows = key_value[:, kv_split:].reshape(length, KVHEADS, AHEAD_DIM)
    block_rows = min(QBLOCK, length)
    factor = 1.0 / math.sqrt(AHEAD_DIM)
    key_place = jnp.arange(length, dtype=jnp.int32)

    def attend(offset):
        query_rows = lax.dynamic_slice_in_dim(queries, offset, block_rows, 0).reshape(block_rows, KVHEADS, group_size, AHEAD_DIM)
        scores = low_back(jnp.einsum('qkgd,tkd->kgqt', query_rows, key_rows, precision=PRECISE) * factor)
        positions = offset + jnp.arange(block_rows, dtype=jnp.int32)
        allowed = key_place[None, :] <= positions[:, None]
        masked = jnp.where(allowed, scores, NEG_FILL)
        maxima = lax.optimization_barrier(jnp.max(masked, axis=-1, keepdims=True))
        weights = jnp.exp(masked - maxima)
        probability = low(weights / lax.optimization_barrier(jnp.sum(weights, axis=-1, keepdims=True)))
        mixed_rows = jnp.einsum('kgqt,tkd->qkgd', probability, value_rows, precision=PRECISE)
        return low(low_back(mixed_rows.reshape(block_rows, AHEADS * AHEAD_DIM)))
    starts = jnp.arange(length // block_rows, dtype=jnp.int32) * block_rows
    return lax.map(jax.checkpoint(attend), starts).reshape(length, AHEADS * AHEAD_DIM)

def layer_forward(source, weights):
    norm1_gain, ssm_in, ssm_bc, ssm_dt, dt_bias, a_log, d_skip, ssm_out, attn_q, attn_kv, attn_out, norm2_gain, mlp_gate_up, mlp_down = weights
    length = source.shape[0]
    input_one = low(rms_normed(source, norm1_gain))
    zx_proj = low_back(matmul_high(input_one, ssm_in.reshape(D, 2 * MINNER)))
    gate_ssm = zx_proj[:, :MINNER]
    source_ssm = low(zx_proj[:, MINNER:])
    bc_rows = low(low_back(matmul_high(input_one, ssm_bc.reshape(D, 2 * STATE))))
    dt_rows = jax.nn.softplus(low_back(matmul_high(input_one, ssm_dt)) + dt_bias)
    entering = jnp.zeros((MHEADS, HEADDIM, STATE), jnp.float32)
    ssm_values, closing = run_ssd(source_ssm.reshape(length, MHEADS, HEADDIM), bc_rows[:, :STATE], bc_rows[:, STATE:], dt_rows, a_log, d_skip, entering, SCAN_BLOCK)
    ssm_values = low_back(ssm_values.reshape(length, MINNER))
    gated_rows = low(ssm_values * jax.nn.silu(gate_ssm))
    ssm_branch = matmul_high(gated_rows, ssm_out)
    queries = low(low_back(matmul_high(input_one, attn_q)))
    key_value = low(low_back(matmul_high(input_one, attn_kv.reshape(D, 2 * KVHEADS * AHEAD_DIM))))
    attended = attention(queries, key_value)
    attn_branch = matmul_high(attended, attn_out)
    mixer_total = low_back(ssm_branch + attn_branch)
    middle = source + mixer_total
    input_two = low(rms_normed(middle, norm2_gain))
    gate_up = low_back(matmul_high(input_two, mlp_gate_up.reshape(D, 2 * FF)))
    activated = low(jax.nn.silu(gate_up[:, :FF]) * gate_up[:, FF:])
    mlp_total = low_back(matmul_high(activated, mlp_down))
    block_out = middle + mlp_total
    statistics = jnp.stack([jnp.sum(mixer_total * mixer_total), jnp.sum(mlp_total * mlp_total), jnp.sum(block_out * block_out)])
    return (block_out, statistics)

def reference(hidden, cotangent, norm1_gain, ssm_in, ssm_bc, ssm_dt, dt_bias, a_log, d_skip, ssm_out, attn_q, attn_kv, attn_out, norm2_gain, mlp_gate_up, mlp_down):
    weights = tuple((argument.astype(jnp.float32) for argument in (norm1_gain, ssm_in, ssm_bc, ssm_dt, dt_bias, a_log, d_skip, ssm_out, attn_q, attn_kv, attn_out, norm2_gain, mlp_gate_up, mlp_down)))
    zero_grads = jax.tree.map(jnp.zeros_like, weights)

    def per_sequence(running_sums, pieces):
        grad_sums, square_sums = running_sums
        source, upstream = pieces
        result, back_fn, statistics = jax.vjp(layer_forward, source.astype(jnp.float32), weights, has_aux=True)
        grad_source, grad_weights = back_fn(upstream.astype(jnp.float32))
        grad_sums = jax.tree.map(jnp.add, grad_sums, grad_weights)
        return ((grad_sums, square_sums + statistics), (result.astype(jnp.bfloat16), grad_source.astype(jnp.bfloat16)))
    (grad_sums, square_sums), (output, grad_hidden) = lax.scan(per_sequence, (zero_grads, jnp.zeros((3,), jnp.float32)), (hidden, cotangent))
    branch_rms = jnp.sqrt(square_sums / (SEQS * LEN * D))
    return (output, grad_hidden, grad_sums[0], grad_sums[1], grad_sums[2], grad_sums[3], grad_sums[4], grad_sums[5], grad_sums[6], grad_sums[7], grad_sums[8], grad_sums[9], grad_sums[10], grad_sums[11], grad_sums[12], grad_sums[13], branch_rms)
```

```python
from functools import partial
import math

import jax
import jax.numpy as jnp
from jax import lax
from jax.sharding import PartitionSpec as P

KVHEADS = 2
AHEAD_DIM = 128
SCAN_BLOCK = 256
QBLOCK = 512


EPSILON = 1e-05
NEG_FILL = -1e30
PRECISE = lax.Precision.HIGHEST

CORE, CHIP = (1, 2)


def pairs_of(stride):
    return [(source, source ^ stride) for source in range(4)]


def partner(value, stride):
    return lax.ppermute(value, "tensor", pairs_of(stride))


def shifted(value, axis, shift):
    count = lax.axis_size(axis)
    return lax.ppermute(value, axis, [(i, (i + shift) % count) for i in range(count)])


def moved(value, axis, shift):
    count = lax.axis_size(axis)
    pairs = [(i, i + shift) for i in range(count) if 0 <= i + shift < count]
    return lax.ppermute(value, axis, pairs)


def cut(value, index, size, axis):
    return lax.dynamic_slice_in_dim(value, index * size, size, axis)


def paired_rows(mine, other, core):
    first = jnp.where(core == 0, mine, other)
    second = jnp.where(core == 0, other, mine)
    return jnp.concatenate([first, second], axis=0)


def gather_rows(mine, core):
    return paired_rows(mine, partner(mine, CORE), core)


def sum_rows(make, core):
    sent = partner(make(1 - core).astype(jnp.bfloat16), CORE)
    mine = (make(core) + sent.astype(jnp.float32)).astype(jnp.bfloat16)
    return mine.astype(jnp.float32) + partner(mine, CHIP).astype(jnp.float32)


def dp_columns(value, core):
    count, mine = (lax.axis_size("dp"), lax.axis_index("dp"))
    share = value.shape[1] // count
    half = value.shape[0] // 2
    pieces = [cut(value, mine, share, 1)]
    rows = cut(value, core, half, 0)
    for shift in range(1, count):
        sent = shifted(cut(rows, (mine + shift) % count, share, 1), "dp", shift)
        pieces.append(gather_rows(sent, core))
    return jnp.concatenate(pieces, axis=0)


def dp_rows(value):
    pieces = [value] + [shifted(value, "dp", shift) for shift in range(1, lax.axis_size("dp"))]
    return jnp.concatenate(pieces, axis=0)


def weight_grad(former, latter):
    local = inner_rows(former, latter).astype(jnp.bfloat16)
    return lax.psum_scatter(local, "ctx", scatter_dimension=0, tiled=True).astype(jnp.float32)


def all_sum(value, axis):
    count, mine = (lax.axis_size(axis), lax.axis_index(axis))
    pieces = jnp.stack([value] + [shifted(value, axis, shift) for shift in range(1, count)])
    total = jnp.zeros_like(value)
    for rank in range(count):
        total = total + lax.dynamic_index_in_dim(pieces, (mine - rank) % count, 0, keepdims=False)
    return total


def scatter_sum(value, axis):
    count, mine = (lax.axis_size(axis), lax.axis_index(axis))
    share = value.shape[0] // count
    total = cut(value, mine, share, 0)
    for shift in range(1, count):
        total = total + shifted(cut(value, (mine + shift) % count, share, 0), axis, shift)
    return total


def chained(state, log_decay, axis, direction):
    count = lax.axis_size(axis)
    total = jnp.zeros_like(state)
    between = jnp.zeros_like(log_decay)
    for shift in range(1, count):
        arrived = moved(state.astype(jnp.bfloat16), axis, direction * shift).astype(jnp.float32)
        total = total + arrived * jnp.exp(between)[:, None, None]
        between = between + moved(log_decay, axis, direction * shift)
    return total


def matmul_low(former, latter):
    return jnp.dot(former, latter, preferred_element_type=jnp.float32)


def inner_rows(former, latter):
    return lax.dot_general(
        former, latter, (((0,), (0,)), ((), ())), preferred_element_type=jnp.float32
    )


def times_back(former, latter):
    return lax.dot_general(
        former, latter, (((1,), (1,)), ((), ())), preferred_element_type=jnp.float32
    )


def round_keep(values):
    return lax.optimization_barrier(values.astype(jnp.bfloat16)).astype(jnp.float32)


def silu_slope(values):
    logistic = jax.nn.sigmoid(values)
    return logistic * (1.0 + values * (1.0 - logistic))


def norm_back(grad_normed, source, scale_rows, gain):
    weighted = grad_normed * gain
    cubed = scale_rows * scale_rows * scale_rows
    grad_source = scale_rows * weighted - source * cubed * jnp.mean(
        weighted * source, axis=-1, keepdims=True
    )
    grad_gain = jnp.sum(grad_normed * source * scale_rows, axis=0)
    return (grad_source, grad_gain)


def ssd_block(states, pieces, decay_rate, skip_gain):
    source_block, write_block, read_block, step_block = pieces
    increments = step_block * decay_rate
    running = jnp.cumsum(increments, axis=0)
    block_len = increments.shape[0]
    lower_mask = (
        jnp.arange(block_len, dtype=jnp.int32)[:, None]
        >= jnp.arange(block_len, dtype=jnp.int32)[None, :]
    )
    differences = running[:, None, :] - running[None, :, :]
    decays = jnp.exp(jnp.where(lower_mask[:, :, None], differences, NEG_FILL))
    intersection = jnp.dot(read_block, write_block.T, precision=PRECISE)
    mixing = decays * intersection[:, :, None] * step_block[None, :, :]
    within = jnp.einsum("tsh,shp->thp", mixing, source_block, precision=PRECISE)
    carried = (
        jnp.einsum("tn,hpn->thp", read_block, states, precision=PRECISE)
        * jnp.exp(running)[:, :, None]
    )
    result = within + carried + skip_gain[None, :, None] * source_block
    tailing = jnp.exp(running[-1][None, :] - running) * step_block
    incoming = jnp.einsum("sh,shp,sn->hpn", tailing, source_block, write_block, precision=PRECISE)
    states = states * jnp.exp(running[-1])[:, None, None] + incoming
    return (states, result)


def run_ssd(source_heads, write_rows, read_rows, step_rows, a_log, d_skip, entering, block_len):
    row_total = source_heads.shape[0]
    block_count = row_total // block_len
    decay_rate = -jnp.exp(a_log)

    def blocked(source):
        return source.reshape((block_count, block_len) + source.shape[1:])

    def stepper(states, pieces):
        return ssd_block(states, pieces, decay_rate, d_skip)

    closing, outputs = lax.scan(
        jax.checkpoint(stepper),
        entering,
        (blocked(source_heads), blocked(write_rows), blocked(read_rows), blocked(step_rows)),
    )
    return (outputs.reshape(source_heads.shape), closing)


def body(
    hidden,
    cotangent,
    norm1_gain,
    ssm_in,
    ssm_bc,
    ssm_dt,
    dt_bias,
    a_log,
    d_skip,
    ssm_out,
    attn_q,
    attn_kv,
    attn_out,
    norm2_gain,
    mlp_gate_up,
    mlp_down,
):
    ctx_rank = lax.axis_index("ctx")
    ctx_count = lax.axis_size("ctx")
    tensor_rank = lax.axis_index("tensor")
    core = tensor_rank % 2
    chip = tensor_rank // 2
    hidden_rows = hidden[0]
    grad_low = cotangent[0]
    source = hidden_rows.astype(jnp.float32)
    tokens = source.shape[0]
    half = tokens // 2
    model_width = source.shape[1]
    inner_local = ssm_in.shape[2]
    heads_local = ssm_dt.shape[1]
    head_width = inner_local // heads_local
    state_width = ssm_bc.shape[2]
    in_matrix = ssm_in.reshape(model_width, 2 * inner_local)
    bc_matrix = ssm_bc.reshape(model_width, 2 * state_width)
    bc_share = 2 * state_width // 4
    bc_columns = cut(bc_matrix, tensor_rank, bc_share, 1)
    heads_query = attn_q.shape[1] // AHEAD_DIM
    kv_pair = cut(attn_kv, chip, AHEAD_DIM, 2)
    kv_matrix = kv_pair.reshape(model_width, 2 * AHEAD_DIM)
    kv_columns = lax.dynamic_index_in_dim(kv_pair, core, 1, keepdims=False)
    ff_local = mlp_down.shape[0]
    gu_matrix = mlp_gate_up.reshape(model_width, 2 * ff_local)
    factor = 1.0 / math.sqrt(AHEAD_DIM)

    scale_one = lax.rsqrt(jnp.mean(source * source, axis=-1, keepdims=True) + EPSILON)
    input_one = (source * scale_one * norm1_gain).astype(jnp.bfloat16)

    key_value = matmul_low(input_one, kv_matrix).astype(jnp.bfloat16)
    kv_sent = cut(key_value, core, AHEAD_DIM, 1)
    kv_got = [kv_sent] + [moved(kv_sent, "ctx", shift) for shift in range(1, ctx_count)]
    kv_mine = jnp.concatenate(kv_got, axis=0)
    kv_other = partner(kv_mine, CORE)
    key_rows = jnp.where(core == 0, kv_mine, kv_other)
    value_rows = jnp.where(core == 0, kv_other, kv_mine)

    cot_columns = dp_columns(grad_low, core)
    one_columns = dp_columns(input_one, core)

    zx_proj = matmul_low(input_one, in_matrix)
    gate_ssm = zx_proj[:, :inner_local]
    source_heads = round_keep(zx_proj[:, inner_local:]).reshape(tokens, heads_local, head_width)
    bc_rows = round_keep(matmul_low(input_one, bc_matrix))
    write_rows = bc_rows[:, :state_width]
    read_rows = bc_rows[:, state_width:]
    dt_pre = matmul_low(input_one, ssm_dt) + dt_bias
    dt_rows = jax.nn.softplus(dt_pre)
    decay_rate = -jnp.exp(a_log)
    running = jnp.cumsum(dt_rows * decay_rate, axis=0)
    to_end = jnp.exp(running[-1][None, :] - running) * dt_rows
    own_state = jnp.einsum("th,thp,tn->hpn", to_end, source_heads, write_rows, precision=PRECISE)
    entering = chained(own_state, running[-1], "ctx", 1)
    ssm_pair, ssm_back = jax.vjp(
        partial(run_ssd, block_len=SCAN_BLOCK),
        source_heads,
        write_rows,
        read_rows,
        dt_rows,
        a_log,
        d_skip,
        entering,
    )
    ssm_values = ssm_pair[0].reshape(tokens, inner_local)
    gate_act = jax.nn.silu(gate_ssm)
    gated_rows = (ssm_values * gate_act).astype(jnp.bfloat16)

    queries = matmul_low(input_one, attn_q).astype(jnp.bfloat16)
    query_rows = queries.reshape(tokens, heads_query, AHEAD_DIM)
    row_place = jnp.arange(tokens, dtype=jnp.int32)
    key_block = jnp.arange(ctx_count * tokens, dtype=jnp.int32) // tokens
    key_place = jnp.arange(ctx_count * tokens, dtype=jnp.int32) % tokens
    allowed = jnp.where(
        key_block[None, :] == 0,
        key_place[None, :] <= row_place[:, None],
        key_block[None, :] <= ctx_rank,
    )
    scores = (
        jnp.einsum("qhd,kd->hqk", query_rows, key_rows, preferred_element_type=jnp.float32) * factor
    )
    masked = jnp.where(allowed[None], scores, NEG_FILL)
    maxima = jnp.max(masked, axis=-1, keepdims=True)
    weights = jnp.exp(masked - maxima)
    probability = weights / jnp.sum(weights, axis=-1, keepdims=True)
    prob_low = probability.astype(jnp.bfloat16)
    mixed_rows = jnp.einsum("hqk,kd->qhd", prob_low, value_rows, preferred_element_type=jnp.float32)
    attended = mixed_rows.reshape(tokens, heads_query * AHEAD_DIM).astype(jnp.bfloat16)

    def mixer_share(index):
        return matmul_low(cut(gated_rows, index, half, 0), ssm_out) + matmul_low(
            cut(attended, index, half, 0), attn_out
        )

    mixer_total = sum_rows(mixer_share, core)
    middle = cut(hidden_rows, core, half, 0).astype(jnp.float32) + mixer_total
    scale_two = lax.rsqrt(jnp.mean(middle * middle, axis=-1, keepdims=True) + EPSILON)
    two_mine = (middle * scale_two * norm2_gain).astype(jnp.bfloat16)
    input_two = gather_rows(two_mine, core)
    gate_up = matmul_low(input_two, gu_matrix)
    gate_rows = gate_up[:, :ff_local]
    up_rows = gate_up[:, ff_local:]
    gate_silu = jax.nn.silu(gate_rows)
    activated = (gate_silu * up_rows).astype(jnp.bfloat16)
    grad_act = times_back(grad_low, mlp_down)
    grad_gu = jnp.concatenate(
        [grad_act * up_rows * silu_slope(gate_rows), grad_act * gate_silu], axis=1
    ).astype(jnp.bfloat16)
    grad_normed_two = sum_rows(lambda index: times_back(cut(grad_gu, index, half, 0), gu_matrix), core)

    mlp_total = sum_rows(lambda index: matmul_low(cut(activated, index, half, 0), mlp_down), core)
    block_out = middle + mlp_total
    output = gather_rows(block_out.astype(jnp.bfloat16), core)
    squares = jnp.stack(
        [
            jnp.sum(mixer_total * mixer_total),
            jnp.sum(mlp_total * mlp_total),
            jnp.sum(block_out * block_out),
        ]
    )
    two_columns = dp_columns(input_two, core)
    grad_gate_up = weight_grad(two_columns, dp_rows(grad_gu))
    grad_down = weight_grad(cot_columns, dp_rows(activated))

    grad_middle, grad_gain_two = norm_back(grad_normed_two, middle, scale_two, norm2_gain)
    grad_middle = cut(grad_low, core, half, 0).astype(jnp.float32) + grad_middle
    grad_mix = gather_rows(grad_middle.astype(jnp.bfloat16), core)
    mix_columns = dp_columns(grad_mix, core)
    grad_outs = weight_grad(
        mix_columns, dp_rows(jnp.concatenate([gated_rows, attended], axis=1))
    )
    grad_gated = times_back(grad_mix, ssm_out)
    grad_values = round_keep(grad_gated * gate_act).reshape(tokens, heads_local, head_width)
    grad_gate_ssm = (grad_gated * ssm_values * silu_slope(gate_ssm)).astype(jnp.bfloat16)
    grad_attended = times_back(grad_mix, attn_out).astype(jnp.bfloat16)
    from_start = jnp.exp(running)
    own_grad = jnp.einsum("th,thp,tn->hpn", from_start, grad_values, read_rows, precision=PRECISE)
    leaving = chained(own_grad, running[-1], "ctx", -1)

    grad_rows = grad_attended.reshape(tokens, heads_query, AHEAD_DIM)
    grad_value = jnp.einsum("hqk,qhd->kd", prob_low, grad_rows, preferred_element_type=jnp.float32)
    grad_prob = jnp.einsum("qhd,kd->hqk", grad_rows, value_rows, preferred_element_type=jnp.float32)
    centre = jnp.sum(probability * grad_prob, axis=-1, keepdims=True)
    grad_score = (probability * (grad_prob - centre)).astype(jnp.bfloat16)
    grad_query = (
        jnp.einsum("hqk,kd->qhd", grad_score, key_rows, preferred_element_type=jnp.float32) * factor
    )
    grad_query_low = grad_query.reshape(tokens, heads_query * AHEAD_DIM).astype(jnp.bfloat16)
    grad_key = (
        jnp.einsum("hqk,qhd->kd", grad_score, query_rows, preferred_element_type=jnp.float32) * factor
    )
    kv_kept = jnp.where(core == 0, grad_key, grad_value)
    kv_given = jnp.where(core == 0, grad_value, grad_key).astype(jnp.bfloat16)
    kv_paired = (kv_kept + partner(kv_given, CORE).astype(jnp.float32)).reshape(
        ctx_count, tokens, AHEAD_DIM
    )
    kv_sum = kv_paired[0]
    for shift in range(1, ctx_count):
        kv_sum = kv_sum + moved(kv_paired[shift].astype(jnp.bfloat16), "ctx", -shift).astype(
            jnp.float32
        )
    grad_kv_low = kv_sum.astype(jnp.bfloat16)

    ssm_grads = ssm_back((grad_values, leaving))
    grad_dt_pre = ssm_grads[3] * jax.nn.sigmoid(dt_pre)
    grad_dt_bias = jnp.sum(grad_dt_pre, axis=0)
    grad_dt_low = grad_dt_pre.astype(jnp.bfloat16)
    grad_source_low = ssm_grads[0].reshape(tokens, inner_local).astype(jnp.bfloat16)
    grad_bc = jnp.concatenate([ssm_grads[1], ssm_grads[2]], axis=1)
    bc_pair = 2 * bc_share
    bc_sent = partner(cut(grad_bc, 1 - chip, bc_pair, 1).astype(jnp.bfloat16), CHIP)
    bc_mine = cut(grad_bc, chip, bc_pair, 1) + bc_sent.astype(jnp.float32)
    bc_given = partner(cut(bc_mine, 1 - core, bc_share, 1).astype(jnp.bfloat16), CORE)
    grad_bc_low = (cut(bc_mine, core, bc_share, 1) + bc_given.astype(jnp.float32)).astype(jnp.bfloat16)

    pad = -heads_local % AHEAD_DIM
    grad_all = jnp.concatenate(
        [
            grad_gate_ssm,
            grad_source_low,
            grad_query_low,
            grad_kv_low,
            grad_bc_low,
            jnp.pad(grad_dt_low, ((0, 0), (0, pad))),
        ],
        axis=1,
    )
    weight_all = jnp.concatenate(
        [in_matrix, attn_q, kv_columns, bc_columns, jnp.pad(ssm_dt, ((0, 0), (0, pad)))], axis=1
    )
    grad_normed_one = sum_rows(lambda index: times_back(cut(grad_all, index, half, 0), weight_all), core)
    source_mine = cut(hidden_rows, core, half, 0).astype(jnp.float32)
    grad_source, grad_gain_one = norm_back(
        grad_normed_one, source_mine, cut(scale_one, core, half, 0), norm1_gain
    )
    grad_hidden = gather_rows((grad_middle + grad_source).astype(jnp.bfloat16), core)
    grad_ins = weight_grad(one_columns, dp_rows(grad_all))

    at = 2 * inner_local
    grad_ssm_in = grad_ins[:, :at].reshape(-1, 2, inner_local)
    grad_attn_q = grad_ins[:, at : at + heads_query * AHEAD_DIM]
    at = at + heads_query * AHEAD_DIM
    kv_part = grad_ins[:, at : at + AHEAD_DIM]
    at = at + AHEAD_DIM
    bc_part = grad_ins[:, at : at + bc_share]
    at = at + bc_share
    grad_ssm_dt = grad_ins[:, at : at + heads_local]

    share = kv_part.shape[0] // 4
    blocks = [cut(kv_part, tensor_rank, share, 0)]
    for stride in range(1, 4):
        blocks.append(partner(cut(kv_part, tensor_rank ^ stride, share, 0), stride))
    blocks = jnp.stack(blocks)

    def of_rank(pieces, rank):
        return lax.dynamic_index_in_dim(pieces, tensor_rank ^ rank, 0, keepdims=False)

    grad_attn_kv = jnp.stack(
        [
            jnp.concatenate([of_rank(blocks, kind), of_rank(blocks, 2 + kind)], axis=1)
            for kind in range(2)
        ],
        axis=1,
    )
    bc_blocks = jnp.stack([bc_part] + [partner(bc_part, stride) for stride in range(1, 4)])
    grad_ssm_bc = jnp.concatenate([of_rank(bc_blocks, rank) for rank in range(4)], axis=1).reshape(
        -1, 2, state_width
    )

    both = jnp.concatenate([grad_gain_one, grad_gain_two, jnp.pad(squares, (0, 125))])
    both = both + partner(both, CORE)
    gains = scatter_sum(
        scatter_sum(jnp.stack([both[:model_width], both[model_width : 2 * model_width]], axis=1), "dp"),
        "ctx",
    )
    small = jnp.concatenate(
        [
            grad_dt_bias,
            ssm_grads[4],
            ssm_grads[5],
            both[2 * model_width : 2 * model_width + 3],
        ]
    )
    small = all_sum(all_sum(small, "dp"), "ctx")
    counted = tokens * model_width * lax.axis_size("dp") * ctx_count
    branch_rms = jnp.sqrt(small[3 * heads_local :] / counted)
    return (
        output[None],
        grad_hidden[None],
        gains[:, 0],
        grad_ssm_in,
        grad_ssm_bc,
        grad_ssm_dt,
        small[:heads_local],
        small[heads_local : 2 * heads_local],
        small[2 * heads_local : 3 * heads_local],
        grad_outs[:, :inner_local].T,
        grad_attn_q,
        grad_attn_kv,
        grad_outs[:, inner_local:].T,
        gains[:, 1],
        grad_gate_up.reshape(-1, 2, ff_local),
        grad_down.T,
        branch_rms,
    )


def solution(mesh):
    return jax.shard_map(
        body,
        mesh=mesh,
        in_specs=(
            P("dp", "ctx", None),
            P("dp", "ctx", None),
            P(),
            P(None, None, "tensor"),
            P(),
            P(None, "tensor"),
            P("tensor"),
            P("tensor"),
            P("tensor"),
            P("tensor", None),
            P(None, "tensor"),
            P(),
            P("tensor", None),
            P(),
            P(None, None, "tensor"),
            P("tensor", None),
        ),
        out_specs=(
            P("dp", "ctx", None),
            P("dp", "ctx", None),
            P(("dp", "ctx")),
            P(("dp", "ctx"), None, "tensor"),
            P(("dp", "ctx"), None, None),
            P(("dp", "ctx"), "tensor"),
            P("tensor"),
            P("tensor"),
            P("tensor"),
            P("tensor", ("dp", "ctx")),
            P(("dp", "ctx"), "tensor"),
            P(("dp", "ctx", "tensor"), None, None),
            P("tensor", ("dp", "ctx")),
            P(("dp", "ctx")),
            P(("dp", "ctx"), None, "tensor"),
            P("tensor", ("dp", "ctx")),
            P(),
        ),
        check_vma=False,
    )
```

```python
from functools import partial
import math

import jax
import jax.numpy as jnp
from jax import lax
from jax.experimental import pallas as pl
from jax.experimental.pallas import tpu as pltpu
from jax.sharding import PartitionSpec as P

AHEAD_DIM = 128
SCAN_BLOCK = 256


EPSILON = 1e-05
NEG_FILL = -1e30

CORE, CHIP = (1, 2)


def pairs_of(stride):
    return [(source, source ^ stride) for source in range(4)]


def partner(value, stride):
    return lax.ppermute(value, "tensor", pairs_of(stride))


def shifted(value, axis, shift):
    count = lax.axis_size(axis)
    return lax.ppermute(value, axis, [(i, (i + shift) % count) for i in range(count)])


def moved(value, axis, shift):
    count = lax.axis_size(axis)
    pairs = [(i, i + shift) for i in range(count) if 0 <= i + shift < count]
    return lax.ppermute(value, axis, pairs)


def cut(value, index, size, axis):
    return lax.dynamic_slice_in_dim(value, index * size, size, axis)


def paired_rows(mine, other, core):
    first = jnp.where(core == 0, mine, other)
    second = jnp.where(core == 0, other, mine)
    return jnp.concatenate([first, second], axis=0)


def gather_rows(mine, core):
    return paired_rows(mine, partner(mine, CORE), core)


def sum_rows(make, core):
    sent = partner(make(1 - core).astype(jnp.bfloat16), CORE)
    mine = (make(core) + sent.astype(jnp.float32)).astype(jnp.bfloat16)
    return mine.astype(jnp.float32) + partner(mine, CHIP).astype(jnp.float32)


def dp_columns(value, core):
    count, mine = (lax.axis_size("dp"), lax.axis_index("dp"))
    share = value.shape[1] // count
    half = value.shape[0] // 2
    pieces = [cut(value, mine, share, 1)]
    rows = cut(value, core, half, 0)
    for shift in range(1, count):
        sent = shifted(cut(rows, (mine + shift) % count, share, 1), "dp", shift)
        pieces.append(gather_rows(sent, core))
    return jnp.concatenate(pieces, axis=0)


def dp_rows(value):
    pieces = [value] + [shifted(value, "dp", shift) for shift in range(1, lax.axis_size("dp"))]
    return jnp.concatenate(pieces, axis=0)


def weight_grad(former, latter):
    local = inner_rows(former, latter).astype(jnp.bfloat16)
    return lax.psum_scatter(local, "ctx", scatter_dimension=0, tiled=True).astype(jnp.float32)


def all_sum(value, axis):
    count, mine = (lax.axis_size(axis), lax.axis_index(axis))
    pieces = jnp.stack([value] + [shifted(value, axis, shift) for shift in range(1, count)])
    total = jnp.zeros_like(value)
    for rank in range(count):
        total = total + lax.dynamic_index_in_dim(pieces, (mine - rank) % count, 0, keepdims=False)
    return total


def scatter_sum(value, axis):
    count, mine = (lax.axis_size(axis), lax.axis_index(axis))
    share = value.shape[0] // count
    total = cut(value, mine, share, 0)
    for shift in range(1, count):
        total = total + shifted(cut(value, (mine + shift) % count, share, 0), axis, shift)
    return total


def chained(state, log_decay, axis, direction):
    count = lax.axis_size(axis)
    width = state.shape[1]
    total = jnp.zeros((log_decay.shape[0], state.shape[0] // log_decay.shape[0], width), jnp.float32)
    between = jnp.zeros_like(log_decay)
    for shift in range(1, count):
        arrived = moved(state, axis, direction * shift).astype(jnp.float32).reshape(total.shape)
        total = total + arrived * jnp.exp(between)[:, None, None]
        between = between + moved(log_decay, axis, direction * shift)
    return total.astype(jnp.bfloat16).reshape(state.shape)


def matmul_low(former, latter):
    return jnp.dot(former, latter, preferred_element_type=jnp.float32)


def inner_rows(former, latter):
    return lax.dot_general(
        former, latter, (((0,), (0,)), ((), ())), preferred_element_type=jnp.float32
    )


def times_back(former, latter):
    return lax.dot_general(
        former, latter, (((1,), (1,)), ((), ())), preferred_element_type=jnp.float32
    )


def silu_slope(values):
    logistic = jax.nn.sigmoid(values)
    return logistic * (1.0 + values * (1.0 - logistic))


def norm_back(grad_normed, source, scale_rows, gain):
    weighted = grad_normed * gain
    cubed = scale_rows * scale_rows * scale_rows
    grad_source = scale_rows * weighted - source * cubed * jnp.mean(
        weighted * source, axis=-1, keepdims=True
    )
    grad_gain = jnp.sum(grad_normed * source * scale_rows, axis=0)
    return (grad_source, grad_gain)


def split_lanes(first, second, shape):
    lane = lax.broadcasted_iota(jnp.int32, shape, 1)
    return jnp.where(lane < shape[1] // 2, first, second)


def lane_sums(values):
    width = values.shape[1] // 2
    lane = lax.broadcasted_iota(jnp.int32, values.shape, 1)
    first = jnp.sum(jnp.where(lane < width, values, 0.0), axis=1, keepdims=True)
    second = jnp.sum(jnp.where(lane < width, 0.0, values), axis=1, keepdims=True)
    return (first, second)


def wide(values):
    return values.astype(jnp.float32)


def narrow(values):
    return values.astype(jnp.bfloat16)


def state_kernel(u_ref, small_ref, b_ref, state_ref, *, to_end):
    rows = small_ref[0]
    if to_end:
        last = rows[0:2, rows.shape[1] - 1 :]
        weights = jnp.exp(last - rows[0:2]) * rows[2:4]
    else:
        weights = jnp.exp(rows[0:2])
    cols = jnp.concatenate([weights, rows[2:8]], axis=0).T
    u = wide(u_ref[...])
    weighted = narrow(u * split_lanes(cols[:, 0:1], cols[:, 1:2], u.shape))
    state_ref[...] = narrow(inner_rows(weighted, b_ref[...]))


def scan_kernel(u_ref, small_ref, b_ref, c_ref, y_ref, cb_ref):
    size = SCAN_BLOCK
    count = u_ref.shape[0] // size
    block = [slice(i * size, (i + 1) * size) for i in range(count)]

    @pl.when(pl.program_id(0) == 0)
    def _():
        for i in range(count):
            for j in range(i + 1):
                cb_ref[block[i], block[j]] = times_back(c_ref[block[i], :], b_ref[block[j], :])

    rows = small_ref[0]
    cols = rows.T
    lower = lax.broadcasted_iota(jnp.int32, (size, size), 0) >= lax.broadcasted_iota(
        jnp.int32, (size, size), 1
    )
    for i in range(count):
        parts = []
        for h in range(2):
            total = jnp.zeros((size, u_ref.shape[1]), jnp.float32)
            for j in range(i + 1):
                difference = cols[block[i], h : h + 1] - rows[h : h + 1, block[j]]
                if i == j:
                    difference = jnp.where(lower, difference, NEG_FILL)
                mixing = jnp.exp(difference) * cb_ref[block[i], block[j]] * rows[2 + h : 3 + h, block[j]]
                total = total + matmul_low(narrow(mixing), u_ref[block[j], :])
            parts.append(total)
        skip = split_lanes(cols[block[i], 4:5], cols[block[i], 5:6], parts[0].shape)
        y_ref[block[i], :] = split_lanes(*parts, parts[0].shape) + skip * wide(u_ref[block[i], :])


def carry_kernel(y_ref, z_ref, small_ref, c_ref, state_ref, out_ref, gated_ref):
    cols = jnp.exp(small_ref[0][0:8]).T
    carried = times_back(c_ref[...], state_ref[...])
    values = y_ref[...] + carried * split_lanes(cols[:, 0:1], cols[:, 1:2], carried.shape)
    out_ref[...] = values
    gate = z_ref[...]
    gated_ref[...] = narrow(values * (gate * jax.nn.sigmoid(gate)))


def scan_back_kernel(u_ref, dy_ref, small_ref, b_ref, c_ref, dw_ref, sums_ref, db_ref, dc_ref, cb_ref, mix_ref):
    size = SCAN_BLOCK
    count = u_ref.shape[0] // size
    width = u_ref.shape[1]
    block = [slice(i * size, (i + 1) * size) for i in range(count)]

    @pl.when(pl.program_id(0) == 0)
    def _():
        mix_ref[...] = jnp.zeros_like(mix_ref)
        for i in range(count):
            for j in range(i, count):
                cb_ref[block[i], block[j]] = times_back(b_ref[block[i], :], c_ref[block[j], :])

    rows = small_ref[0]
    cols = rows.T
    upper = lax.broadcasted_iota(jnp.int32, (size, size), 0) <= lax.broadcasted_iota(
        jnp.int32, (size, size), 1
    )
    lane = lax.broadcasted_iota(jnp.int32, (size, width), 1)
    read_sums = [[jnp.zeros((1, size), jnp.float32) for _ in range(count)] for _ in range(2)]
    write_sums = [[], []]
    for i in range(count):
        parts = []
        for h in range(2):
            total = jnp.zeros((size, width), jnp.float32)
            write_sum = jnp.zeros((size, 1), jnp.float32)
            step = cols[block[i], 2 + h : 3 + h]
            for j in range(i, count):
                difference = rows[h : h + 1, block[j]] - cols[block[i], h : h + 1]
                if i == j:
                    difference = jnp.where(upper, difference, NEG_FILL)
                decay = jnp.exp(difference)
                dy = dy_ref[block[j], :]
                dy_head = jnp.where((lane < width // 2) == (h == 0), dy, jnp.zeros_like(dy))
                product = decay * times_back(u_ref[block[i], :], dy_head)
                crossing = cb_ref[block[i], block[j]]
                total = total + matmul_low(narrow(decay * crossing), dy)
                weighted = product * step
                mix_ref[block[i], block[j]] += weighted
                write_sum = write_sum + jnp.sum(product * crossing, axis=1, keepdims=True)
                read_sums[h][j] = read_sums[h][j] + jnp.sum(weighted * crossing, axis=0, keepdims=True)
            parts.append(total)
            write_sums[h].append(write_sum)
        dw_ref[block[i], :] = split_lanes(*parts, parts[0].shape)
    both = [jnp.concatenate(write_sums[h], axis=0) for h in range(2)]
    column = lax.broadcasted_iota(jnp.int32, (u_ref.shape[0], 8), 1)
    packed = jnp.where(column == 0, both[0], jnp.where(column == 1, both[1], 0.0)).T
    skip = jnp.sum(wide(u_ref[...]) * wide(dy_ref[...]), axis=0, keepdims=True)
    skip = jnp.concatenate([skip, jnp.zeros((1, u_ref.shape[0] - width), jnp.float32)], axis=1)
    reads = [jnp.concatenate(read_sums[h], axis=1) for h in range(2)]
    sums_ref[0] = jnp.concatenate([reads[0], reads[1], packed[0:2], skip, packed[2:5]], axis=0)

    @pl.when(pl.program_id(0) == pl.num_programs(0) - 1)
    def _():
        for i in range(count):
            total = jnp.zeros((size, b_ref.shape[1]), jnp.float32)
            for j in range(i, count):
                total = total + matmul_low(narrow(mix_ref[block[i], block[j]]), c_ref[block[j], :])
            db_ref[block[i], :] = total
        for j in range(count):
            total = jnp.zeros((size, b_ref.shape[1]), jnp.float32)
            for i in range(j + 1):
                total = total + inner_rows(narrow(mix_ref[block[i], block[j]]), b_ref[block[i], :])
            dc_ref[block[j], :] = total


def carry_back_kernel(
    u_ref, dy_ref, small_ref, sums_ref, dw_ref, b_ref, c_ref, state_ref, grad_ref, db_in_ref, dc_in_ref,
    du_ref, steps_ref, db_ref, dc_ref,
):
    rows = small_ref[0]
    tokens = rows.shape[1]
    last = rows[0:2, tokens - 1 :]
    from_start = jnp.exp(rows[0:2])
    to_end = jnp.exp(last - rows[0:2])
    cols = jnp.concatenate([from_start, to_end, rows[2:6]], axis=0).T
    u = wide(u_ref[...])
    dy = wide(dy_ref[...])

    def spread(at):
        return split_lanes(cols[:, at : at + 1], cols[:, at + 1 : at + 2], u.shape)

    @pl.when(pl.program_id(0) == 0)
    def _():
        db_ref[...] = db_in_ref[...]
        dc_ref[...] = dc_in_ref[...]

    state = state_ref[...]
    grad = grad_ref[...]
    started = spread(0) * dy
    ended = spread(2) * u
    step = spread(4)
    dw = dw_ref[...] + spread(2) * times_back(b_ref[...], grad)
    du_ref[...] = narrow(step * dw + spread(6) * dy)
    dc_ref[...] += matmul_low(narrow(started), state)
    db_ref[...] += matmul_low(narrow(ended * step), grad)
    reads = lane_sums(started * times_back(c_ref[...], state))
    writes = lane_sums(ended * times_back(b_ref[...], grad))
    column = lax.broadcasted_iota(jnp.int32, (tokens, 8), 1)
    packed = jnp.zeros((tokens, 8), jnp.float32)
    for at, values in enumerate(reads + writes):
        packed = jnp.where(column == at, values, packed)
    packed = packed.T
    sums = sums_ref[0]
    written = sums[2:4] + packed[2:4]
    slope = sums[0:2] + packed[0:2] - rows[2:4] * written
    products = jnp.sum(wide(state) * wide(grad), axis=1, keepdims=True)
    height = products.shape[0] // 2
    across = jnp.concatenate(
        [
            jnp.sum(products[:height], axis=0, keepdims=True),
            jnp.sum(products[height:], axis=0, keepdims=True),
        ],
        axis=0,
    ) * jnp.exp(last)
    across = across + jnp.sum(rows[2:4] * packed[2:4], axis=1, keepdims=True)
    held = jnp.concatenate([slope, jnp.zeros((6, tokens), jnp.float32)], axis=0)
    place = lax.broadcasted_iota(jnp.int32, held.shape, 1)
    reach = 1
    while reach < tokens:
        held = held + jnp.where(place < tokens - reach, pltpu.roll(held, tokens - reach, 1), 0.0)
        reach = 2 * reach
    flow = held[0:2] + across
    steps_ref[0] = jnp.concatenate([written + rows[6:8] * flow, flow, held[2:6]], axis=0)


def attend_scores(rank_ref, k_ref, q_ref, own, factor):
    scores = times_back(k_ref[...], q_ref[...]) * factor
    keys, queries = scores.shape
    row = lax.broadcasted_iota(jnp.int32, (own, queries), 0)
    column = lax.broadcasted_iota(jnp.int32, (own, queries), 1) + pl.program_id(1) * queries
    near = jnp.where(row <= column, scores[:own], NEG_FILL)
    if keys == own:
        return near
    far_row = lax.broadcasted_iota(jnp.int32, (keys - own, queries), 0)
    far = jnp.where(far_row < rank_ref[0] * own, scores[own:], NEG_FILL)
    return jnp.concatenate([near, far], axis=0)


def attend_kernel(rank_ref, q_ref, k_ref, v_ref, out_ref, log_ref, flat_ref, *, own, factor):
    @pl.when((pl.program_id(0) == 0) & (pl.program_id(1) == 0))
    def _():
        flat_ref[...] = v_ref[...].T

    scores = attend_scores(rank_ref, k_ref, q_ref, own, factor)
    maxima = jnp.max(scores, axis=0, keepdims=True)
    weights = jnp.exp(scores - maxima)
    totals = jnp.sum(weights, axis=0, keepdims=True)
    probability = narrow(weights * (1.0 / totals))
    out_ref[...] = narrow(matmul_low(flat_ref[...], probability).T)
    log_ref[0] = jnp.broadcast_to(maxima + jnp.log(totals), log_ref.shape[1:])


def attend_back_kernel(
    rank_ref, q_ref, do_ref, log_ref, k_ref, v_ref, dq_ref, dk_ref, dv_ref, flat_ref, *, own, factor
):
    @pl.when((pl.program_id(0) == 0) & (pl.program_id(1) == 0))
    def _():
        flat_ref[...] = k_ref[...].T
        dk_ref[...] = jnp.zeros_like(dk_ref)
        dv_ref[...] = jnp.zeros_like(dv_ref)

    scores = attend_scores(rank_ref, k_ref, q_ref, own, factor)
    probability = jnp.exp(scores - log_ref[0][0:1])
    dv_ref[...] += matmul_low(narrow(probability), do_ref[...])
    grad_prob = times_back(v_ref[...], do_ref[...])
    centre = jnp.sum(probability * grad_prob, axis=0, keepdims=True)
    grad_score = narrow(probability * (grad_prob - centre))
    dk_ref[...] += matmul_low(grad_score, q_ref[...]) * factor
    dq_ref[...] = narrow((matmul_low(flat_ref[...], grad_score) * factor).T)


def sizes(*values):
    return sum(v.size * v.dtype.itemsize for v in values)


def call(name, kernel, grid, specs, args, outs, scratch=(), flops=0):
    cost = pl.CostEstimate(
        flops=int(flops),
        bytes_accessed=int(sizes(*args) + sizes(*[out for out, _ in outs])),
        transcendentals=0,
    )
    return pl.pallas_call(
        kernel,
        name=name,
        grid=grid,
        in_specs=specs,
        out_specs=[spec for _, spec in outs],
        out_shape=[out for out, _ in outs],
        scratch_shapes=list(scratch),
        cost_estimate=cost,
        compiler_params=pltpu.CompilerParams(vmem_limit_bytes=48 * 1024 * 1024),
    )(*args)


def like(shape, kind):
    return jax.ShapeDtypeStruct(shape, kind)


class Scan:
    def __init__(self, tokens, inner, state):
        self.tokens, self.inner, self.state = (tokens, inner, state)
        self.pairs = inner // 128
        self.tile = pl.BlockSpec((tokens, 128), lambda p: (0, p))
        self.small = pl.BlockSpec((1, 8, tokens), lambda p: (p, 0, 0))
        self.shared = pl.BlockSpec((tokens, state), lambda p: (0, 0))
        self.states = pl.BlockSpec((128, state), lambda p: (p, 0))
        self.small_like = like((self.pairs, 8, tokens), jnp.float32)
        self.work = 2 * tokens * inner * state

    def rows_like(self, kind):
        return like((self.tokens, self.inner), kind)

    def own_state(self, u, small, b, to_end):
        return call(
            "own_state",
            partial(state_kernel, to_end=to_end),
            (self.pairs,),
            [self.tile, self.small, self.shared],
            (u, small, b),
            [(like((self.inner, self.state), jnp.bfloat16), self.states)],
            flops=self.work,
        )[0]

    def within(self, u, small, b, c):
        return call(
            "scan",
            scan_kernel,
            (self.pairs,),
            [self.tile, self.small, self.shared, self.shared],
            (u, small, b, c),
            [(self.rows_like(jnp.float32), self.tile)],
            [pltpu.VMEM((self.tokens, self.tokens), jnp.float32)],
            flops=8 * self.work,
        )[0]

    def carried(self, y, z, small, c, state):
        return call(
            "carry",
            carry_kernel,
            (self.pairs,),
            [self.tile, self.tile, self.small, self.shared, self.states],
            (y, z, small, c, state),
            [(self.rows_like(jnp.float32), self.tile), (self.rows_like(jnp.bfloat16), self.tile)],
            flops=self.work,
        )

    def within_back(self, u, dy, small, b, c):
        shared = like((self.tokens, self.state), jnp.float32)
        square = pltpu.VMEM((self.tokens, self.tokens), jnp.float32)
        return call(
            "scan_back",
            scan_back_kernel,
            (self.pairs,),
            [self.tile, self.tile, self.small, self.shared, self.shared],
            (u, dy, small, b, c),
            [
                (self.rows_like(jnp.float32), self.tile),
                (self.small_like, self.small),
                (shared, self.shared),
                (shared, self.shared),
            ],
            [square, square],
            flops=20 * self.work,
        )

    def carried_back(self, u, dy, small, sums, dw, b, c, state, grad, db, dc):
        shared = like((self.tokens, self.state), jnp.float32)
        return call(
            "carry_back",
            carry_back_kernel,
            (self.pairs,),
            [self.tile, self.tile, self.small, self.small, self.tile]
            + [self.shared, self.shared, self.states, self.states, self.shared, self.shared],
            (u, dy, small, sums, dw, b, c, state, grad, db, dc),
            [
                (self.rows_like(jnp.bfloat16), self.tile),
                (self.small_like, self.small),
                (shared, self.shared),
                (shared, self.shared),
            ],
            flops=6 * self.work,
        )


class Attend:
    def __init__(self, tokens, keys, heads):
        self.tokens, self.keys, self.heads = (tokens, keys, heads)
        size = min(256, tokens)
        self.grid = (heads, tokens // size)
        self.factor = 1.0 / math.sqrt(AHEAD_DIM)
        self.rank = pl.BlockSpec(memory_space=pltpu.SMEM)
        self.tile = pl.BlockSpec((size, AHEAD_DIM), lambda h, q: (q, h))
        self.log = pl.BlockSpec((1, 8, size), lambda h, q: (h, 0, q))
        self.whole = pl.BlockSpec((keys, AHEAD_DIM), lambda h, q: (0, 0))
        self.rows_like = like((tokens, heads * AHEAD_DIM), jnp.bfloat16)
        self.flat = pltpu.VMEM((AHEAD_DIM, keys), jnp.bfloat16)
        self.work = 2 * tokens * heads * AHEAD_DIM * keys

    def forward(self, rank, q, k, v):
        return call(
            "attend",
            partial(attend_kernel, own=self.tokens, factor=self.factor),
            self.grid,
            [self.rank, self.tile, self.whole, self.whole],
            (rank, q, k, v),
            [(self.rows_like, self.tile), (like((self.heads, 8, self.tokens), jnp.float32), self.log)],
            [self.flat],
            flops=4 * self.work,
        )

    def back(self, rank, q, do, log, k, v):
        whole = like((self.keys, AHEAD_DIM), jnp.float32)
        return call(
            "attend_back",
            partial(attend_back_kernel, own=self.tokens, factor=self.factor),
            self.grid,
            [self.rank, self.tile, self.tile, self.log, self.whole, self.whole],
            (rank, q, do, log, k, v),
            [(self.rows_like, self.tile), (whole, self.whole), (whole, self.whole)],
            [self.flat],
            flops=10 * self.work,
        )


def body(
    hidden,
    cotangent,
    norm1_gain,
    ssm_in,
    ssm_bc,
    ssm_dt,
    dt_bias,
    a_log,
    d_skip,
    ssm_out,
    attn_q,
    attn_kv,
    attn_out,
    norm2_gain,
    mlp_gate_up,
    mlp_down,
):
    ctx_rank = lax.axis_index("ctx")
    ctx_count = lax.axis_size("ctx")
    tensor_rank = lax.axis_index("tensor")
    core = tensor_rank % 2
    chip = tensor_rank // 2
    hidden_rows = hidden[0]
    grad_low = cotangent[0]
    source = hidden_rows.astype(jnp.float32)
    tokens = source.shape[0]
    half = tokens // 2
    model_width = source.shape[1]
    inner_local = ssm_in.shape[2]
    heads_local = ssm_dt.shape[1]
    head_width = inner_local // heads_local
    state_width = ssm_bc.shape[2]
    in_matrix = ssm_in.reshape(model_width, 2 * inner_local)
    bc_matrix = ssm_bc.reshape(model_width, 2 * state_width)
    bc_share = 2 * state_width // 4
    bc_columns = cut(bc_matrix, tensor_rank, bc_share, 1)
    heads_query = attn_q.shape[1] // AHEAD_DIM
    kv_pair = cut(attn_kv, chip, AHEAD_DIM, 2)
    kv_matrix = kv_pair.reshape(model_width, 2 * AHEAD_DIM)
    kv_columns = lax.dynamic_index_in_dim(kv_pair, core, 1, keepdims=False)
    ff_local = mlp_down.shape[0]
    gu_matrix = mlp_gate_up.reshape(model_width, 2 * ff_local)
    factor = 1.0 / math.sqrt(AHEAD_DIM)

    scale_one = lax.rsqrt(jnp.mean(source * source, axis=-1, keepdims=True) + EPSILON)
    input_one = (source * scale_one * norm1_gain).astype(jnp.bfloat16)

    key_value = matmul_low(input_one, kv_matrix).astype(jnp.bfloat16)
    kv_sent = cut(key_value, core, AHEAD_DIM, 1)
    kv_got = [kv_sent] + [moved(kv_sent, "ctx", shift) for shift in range(1, ctx_count)]
    kv_mine = jnp.concatenate(kv_got, axis=0)
    kv_other = partner(kv_mine, CORE)
    key_rows = jnp.where(core == 0, kv_mine, kv_other)
    value_rows = jnp.where(core == 0, kv_other, kv_mine)

    cot_columns = dp_columns(grad_low, core)
    one_columns = dp_columns(input_one, core)

    zx_proj = matmul_low(input_one, in_matrix)
    gate_ssm = zx_proj[:, :inner_local]
    source_rows = zx_proj[:, inner_local:].astype(jnp.bfloat16)
    bc_rows = matmul_low(input_one, bc_matrix).astype(jnp.bfloat16)
    write_rows = bc_rows[:, :state_width]
    read_rows = bc_rows[:, state_width:]
    dt_pre = lax.dot_general(
        ssm_dt, input_one, (((0,), (1,)), ((), ())), preferred_element_type=jnp.float32
    ) + dt_bias[:, None]
    dt_rows = jax.nn.softplus(dt_pre)
    decay_rate = -jnp.exp(a_log)
    running = jnp.cumsum(dt_rows * decay_rate[:, None], axis=1)
    head_pairs = heads_local // 2

    def by_head(value):
        return jnp.broadcast_to(value[:, None], (heads_local, tokens))

    small_rows = jnp.stack([running, dt_rows, by_head(d_skip), by_head(decay_rate)], axis=1)
    small_rows = small_rows.reshape(head_pairs, 2, 4, tokens).transpose(0, 2, 1, 3)
    small_rows = small_rows.reshape(head_pairs, 8, tokens)
    scan = Scan(tokens, inner_local, state_width)
    own_state = scan.own_state(source_rows, small_rows, write_rows, True)
    entering = chained(own_state, running[:, -1], "ctx", 1)
    within_rows = scan.within(source_rows, small_rows, write_rows, read_rows)
    queries = matmul_low(input_one, attn_q).astype(jnp.bfloat16)
    attend = Attend(tokens, ctx_count * tokens, heads_query)
    rank = ctx_rank.astype(jnp.int32)[None]
    attended, log_rows = attend.forward(rank, queries, key_rows, value_rows)
    ssm_values, gated_rows = scan.carried(within_rows, gate_ssm, small_rows, read_rows, entering)

    def mixer_share(index):
        return matmul_low(cut(gated_rows, index, half, 0), ssm_out) + matmul_low(
            cut(attended, index, half, 0), attn_out
        )

    mixer_total = sum_rows(mixer_share, core)
    middle = cut(hidden_rows, core, half, 0).astype(jnp.float32) + mixer_total
    scale_two = lax.rsqrt(jnp.mean(middle * middle, axis=-1, keepdims=True) + EPSILON)
    two_mine = (middle * scale_two * norm2_gain).astype(jnp.bfloat16)
    input_two = gather_rows(two_mine, core)
    gate_up = matmul_low(input_two, gu_matrix)
    gate_rows = gate_up[:, :ff_local]
    up_rows = gate_up[:, ff_local:]
    gate_silu = jax.nn.silu(gate_rows)
    activated = (gate_silu * up_rows).astype(jnp.bfloat16)
    grad_act = times_back(grad_low, mlp_down)
    grad_gu = jnp.concatenate(
        [grad_act * up_rows * silu_slope(gate_rows), grad_act * gate_silu], axis=1
    ).astype(jnp.bfloat16)
    grad_normed_two = sum_rows(lambda index: times_back(cut(grad_gu, index, half, 0), gu_matrix), core)

    mlp_total = sum_rows(lambda index: matmul_low(cut(activated, index, half, 0), mlp_down), core)
    block_out = middle + mlp_total
    output = gather_rows(block_out.astype(jnp.bfloat16), core)
    squares = jnp.stack(
        [
            jnp.sum(mixer_total * mixer_total),
            jnp.sum(mlp_total * mlp_total),
            jnp.sum(block_out * block_out),
        ]
    )
    two_columns = dp_columns(input_two, core)
    grad_gate_up = weight_grad(two_columns, dp_rows(grad_gu))
    grad_down = weight_grad(cot_columns, dp_rows(activated))

    grad_middle, grad_gain_two = norm_back(grad_normed_two, middle, scale_two, norm2_gain)
    grad_middle = cut(grad_low, core, half, 0).astype(jnp.float32) + grad_middle
    grad_mix = gather_rows(grad_middle.astype(jnp.bfloat16), core)
    mix_columns = dp_columns(grad_mix, core)
    grad_outs = weight_grad(
        mix_columns, dp_rows(jnp.concatenate([gated_rows, attended], axis=1))
    )
    grad_gated = times_back(grad_mix, ssm_out)
    grad_values = (grad_gated * jax.nn.silu(gate_ssm)).astype(jnp.bfloat16)
    grad_gate_ssm = (grad_gated * ssm_values * silu_slope(gate_ssm)).astype(jnp.bfloat16)
    grad_attended = times_back(grad_mix, attn_out).astype(jnp.bfloat16)
    own_grad = scan.own_state(grad_values, small_rows, read_rows, False)
    leaving = chained(own_grad, running[:, -1], "ctx", -1)
    grad_query_low, grad_key, grad_value = attend.back(
        rank, queries, grad_attended, log_rows, key_rows, value_rows
    )
    kv_kept = jnp.where(core == 0, grad_key, grad_value)
    kv_given = jnp.where(core == 0, grad_value, grad_key).astype(jnp.bfloat16)
    kv_paired = (kv_kept + partner(kv_given, CORE).astype(jnp.float32)).reshape(
        ctx_count, tokens, AHEAD_DIM
    )
    kv_sum = kv_paired[0]
    for shift in range(1, ctx_count):
        kv_sum = kv_sum + moved(kv_paired[shift].astype(jnp.bfloat16), "ctx", -shift).astype(
            jnp.float32
        )
    grad_kv_low = kv_sum.astype(jnp.bfloat16)

    grad_written, scan_sums, grad_b, grad_c = scan.within_back(
        source_rows, grad_values, small_rows, write_rows, read_rows
    )
    grad_source_low, steps, grad_b, grad_c = scan.carried_back(
        source_rows, grad_values, small_rows, scan_sums, grad_written,
        write_rows, read_rows, entering, leaving, grad_b, grad_c,
    )
    grad_dt_pre = steps[:, 0:2].reshape(heads_local, tokens) * jax.nn.sigmoid(dt_pre)
    flow_rows = steps[:, 2:4].reshape(heads_local, tokens)
    grad_dt_bias = jnp.sum(grad_dt_pre, axis=1)
    grad_a_log = decay_rate * jnp.sum(dt_rows * flow_rows, axis=1)
    grad_d_skip = jnp.sum(scan_sums[:, 4, : 2 * head_width].reshape(heads_local, head_width), axis=1)
    grad_dt_low = grad_dt_pre.astype(jnp.bfloat16).T
    grad_bc = jnp.concatenate([grad_b, grad_c], axis=1)
    bc_pair = 2 * bc_share
    bc_sent = partner(cut(grad_bc, 1 - chip, bc_pair, 1).astype(jnp.bfloat16), CHIP)
    bc_mine = cut(grad_bc, chip, bc_pair, 1) + bc_sent.astype(jnp.float32)
    bc_given = partner(cut(bc_mine, 1 - core, bc_share, 1).astype(jnp.bfloat16), CORE)
    grad_bc_low = (cut(bc_mine, core, bc_share, 1) + bc_given.astype(jnp.float32)).astype(jnp.bfloat16)

    pad = -heads_local % AHEAD_DIM
    grad_all = jnp.concatenate(
        [
            grad_gate_ssm,
            grad_source_low,
            grad_query_low,
            grad_kv_low,
            grad_bc_low,
            jnp.pad(grad_dt_low, ((0, 0), (0, pad))),
        ],
        axis=1,
    )
    weight_all = jnp.concatenate(
        [in_matrix, attn_q, kv_columns, bc_columns, jnp.pad(ssm_dt, ((0, 0), (0, pad)))], axis=1
    )
    grad_normed_one = sum_rows(lambda index: times_back(cut(grad_all, index, half, 0), weight_all), core)
    source_mine = cut(hidden_rows, core, half, 0).astype(jnp.float32)
    grad_source, grad_gain_one = norm_back(
        grad_normed_one, source_mine, cut(scale_one, core, half, 0), norm1_gain
    )
    grad_hidden = gather_rows((grad_middle + grad_source).astype(jnp.bfloat16), core)
    grad_ins = weight_grad(one_columns, dp_rows(grad_all))

    at = 2 * inner_local
    grad_ssm_in = grad_ins[:, :at].reshape(-1, 2, inner_local)
    grad_attn_q = grad_ins[:, at : at + heads_query * AHEAD_DIM]
    at = at + heads_query * AHEAD_DIM
    kv_part = grad_ins[:, at : at + AHEAD_DIM]
    at = at + AHEAD_DIM
    bc_part = grad_ins[:, at : at + bc_share]
    at = at + bc_share
    grad_ssm_dt = grad_ins[:, at : at + heads_local]

    share = kv_part.shape[0] // 4
    blocks = [cut(kv_part, tensor_rank, share, 0)]
    for stride in range(1, 4):
        blocks.append(partner(cut(kv_part, tensor_rank ^ stride, share, 0), stride))
    blocks = jnp.stack(blocks)

    def of_rank(pieces, rank):
        return lax.dynamic_index_in_dim(pieces, tensor_rank ^ rank, 0, keepdims=False)

    grad_attn_kv = jnp.stack(
        [
            jnp.concatenate([of_rank(blocks, kind), of_rank(blocks, 2 + kind)], axis=1)
            for kind in range(2)
        ],
        axis=1,
    )
    bc_blocks = jnp.stack([bc_part] + [partner(bc_part, stride) for stride in range(1, 4)])
    grad_ssm_bc = jnp.concatenate([of_rank(bc_blocks, rank) for rank in range(4)], axis=1).reshape(
        -1, 2, state_width
    )

    both = jnp.concatenate([grad_gain_one, grad_gain_two, jnp.pad(squares, (0, 125))])
    both = both + partner(both, CORE)
    gains = scatter_sum(
        scatter_sum(jnp.stack([both[:model_width], both[model_width : 2 * model_width]], axis=1), "dp"),
        "ctx",
    )
    small = jnp.concatenate(
        [
            grad_dt_bias,
            grad_a_log,
            grad_d_skip,
            both[2 * model_width : 2 * model_width + 3],
        ]
    )
    small = all_sum(all_sum(small, "dp"), "ctx")
    counted = tokens * model_width * lax.axis_size("dp") * ctx_count
    branch_rms = jnp.sqrt(small[3 * heads_local :] / counted)
    return (
        output[None],
        grad_hidden[None],
        gains[:, 0],
        grad_ssm_in,
        grad_ssm_bc,
        grad_ssm_dt,
        small[:heads_local],
        small[heads_local : 2 * heads_local],
        small[2 * heads_local : 3 * heads_local],
        grad_outs[:, :inner_local].T,
        grad_attn_q,
        grad_attn_kv,
        grad_outs[:, inner_local:].T,
        gains[:, 1],
        grad_gate_up.reshape(-1, 2, ff_local),
        grad_down.T,
        branch_rms,
    )


def solution(mesh):
    return jax.shard_map(
        body,
        mesh=mesh,
        in_specs=(
            P("dp", "ctx", None),
            P("dp", "ctx", None),
            P(),
            P(None, None, "tensor"),
            P(),
            P(None, "tensor"),
            P("tensor"),
            P("tensor"),
            P("tensor"),
            P("tensor", None),
            P(None, "tensor"),
            P(),
            P("tensor", None),
            P(),
            P(None, None, "tensor"),
            P("tensor", None),
        ),
        out_specs=(
            P("dp", "ctx", None),
            P("dp", "ctx", None),
            P(("dp", "ctx")),
            P(("dp", "ctx"), None, "tensor"),
            P(("dp", "ctx"), None, None),
            P(("dp", "ctx"), "tensor"),
            P("tensor"),
            P("tensor"),
            P("tensor"),
            P("tensor", ("dp", "ctx")),
            P(("dp", "ctx"), "tensor"),
            P(("dp", "ctx", "tensor"), None, None),
            P("tensor", ("dp", "ctx")),
            P(("dp", "ctx")),
            P(("dp", "ctx"), None, "tensor"),
            P("tensor", ("dp", "ctx")),
            P(),
        ),
        check_vma=False,
    )
```

```python
from functools import partial
import math

import jax
import jax.numpy as jnp
from jax import lax
from jax.experimental import pallas as pl
from jax.experimental.pallas import tpu as pltpu
from jax.sharding import PartitionSpec as P

AHEAD_DIM = 128
SCAN_BLOCK = 256


EPSILON = 1e-05
NEG_FILL = -1e30

CORE, CHIP = (1, 2)


def partner(value, stride):
    return lax.ppermute(value, "tensor", [(rank, rank ^ stride) for rank in range(4)])


def shifted(value, axis, shift):
    count = lax.axis_size(axis)
    return lax.ppermute(value, axis, [(i, (i + shift) % count) for i in range(count)])


def moved(value, axis, shift):
    count = lax.axis_size(axis)
    pairs = [(i, i + shift) for i in range(count) if 0 <= i + shift < count]
    return lax.ppermute(value, axis, pairs)


def after(value, *others):
    return lax.optimization_barrier((value,) + others)[0]


def cut(value, index, size, axis):
    return lax.dynamic_slice_in_dim(value, index * size, size, axis)


def paired_rows(mine, other, core):
    first = jnp.where(core == 0, mine, other)
    second = jnp.where(core == 0, other, mine)
    return jnp.concatenate([first, second], axis=0)


def gather_rows(mine, core):
    return paired_rows(mine, partner(mine, CORE), core)


def send_columns(rows):
    count, mine = (lax.axis_size("dp"), lax.axis_index("dp"))
    share = rows.shape[1] // count
    return [
        shifted(cut(rows, (mine + shift) % count, share, 1), "dp", shift) for shift in range(1, count)
    ]


def both_halves(arrived):
    return [(part, partner(part, CORE)) for part in arrived]


def send_rows(value):
    return [shifted(value, "dp", shift) for shift in range(1, lax.axis_size("dp"))]


def ctx_sum(value):
    return lax.psum_scatter(value, "ctx", scatter_dimension=0, tiled=True).astype(jnp.float32)


def all_sum(value, axis):
    count, mine = (lax.axis_size(axis), lax.axis_index(axis))
    pieces = jnp.stack([value] + [shifted(value, axis, shift) for shift in range(1, count)])
    total = jnp.zeros_like(value)
    for rank in range(count):
        total = total + lax.dynamic_index_in_dim(pieces, (mine - rank) % count, 0, keepdims=False)
    return total


def scatter_sum(value, axis):
    count, mine = (lax.axis_size(axis), lax.axis_index(axis))
    share = value.shape[0] // count
    total = cut(value, mine, share, 0)
    for shift in range(1, count):
        total = total + shifted(cut(value, (mine + shift) % count, share, 0), axis, shift)
    return total


def chained(state, log_decay, forward, fillers):
    count = lax.axis_size("ctx")
    decay = jnp.exp(log_decay)[:, None, None]
    per_head = (decay.shape[0], state.shape[0] // decay.shape[0], state.shape[1])
    own = state.reshape(per_head)
    sent = state
    entering = None
    for step in range(1, count):
        pair = (step - 1, step) if forward else (count - step, count - step - 1)
        arrived = lax.ppermute(sent, "ctx", [pair])
        if step <= len(fillers):
            arrived = after(arrived, *fillers[step - 1](sent))
        entering = arrived if entering is None else entering + arrived
        if step < count - 1:
            total = own.astype(jnp.float32) + decay * arrived.reshape(per_head).astype(jnp.float32)
            sent = total.astype(jnp.bfloat16).reshape(state.shape)
    return entering


def matmul_low(former, latter):
    return jnp.dot(former, latter, preferred_element_type=jnp.float32)


def inner_rows(former, latter):
    return lax.dot_general(
        former, latter, (((0,), (0,)), ((), ())), preferred_element_type=jnp.float32
    )


def times_back(former, latter):
    return lax.dot_general(
        former, latter, (((1,), (1,)), ((), ())), preferred_element_type=jnp.float32
    )


def silu_slope(values):
    logistic = jax.nn.sigmoid(values)
    return logistic * (1.0 + values * (1.0 - logistic))


def split_lanes(first, second, shape):
    lane = lax.broadcasted_iota(jnp.int32, shape, 1)
    return jnp.where(lane < shape[1] // 2, first, second)


def wide(values):
    return values.astype(jnp.float32)


def narrow(values):
    return values.astype(jnp.bfloat16)


def in_two(values):
    high = narrow(values)
    return (high, narrow(values - wide(high)))


def spread(rows, shape):
    rows = jnp.concatenate([rows, jnp.zeros((6, rows.shape[1]), jnp.float32)], axis=0)
    place = lax.broadcasted_iota(jnp.int32, (8, shape[1]), 0)
    lane = lax.broadcasted_iota(jnp.int32, (8, shape[1]), 1)
    chosen = narrow(jnp.where(place == lane // (shape[1] // 2), 1.0, 0.0))
    high, low = in_two(rows.T)
    return matmul_low(high, chosen) + matmul_low(low, chosen)


def lane_sums(values):
    place = lax.broadcasted_iota(jnp.int32, (8, values.shape[1]), 0)
    lane = lax.broadcasted_iota(jnp.int32, (8, values.shape[1]), 1)
    chosen = narrow(jnp.where(place == lane // (values.shape[1] // 2), 1.0, 0.0))
    high, low = in_two(values)
    return times_back(chosen, high) + times_back(chosen, low)


def lanes_of(ref):
    return [slice(at, at + 128) for at in range(0, ref.shape[1], 128)]


def state_kernel(u_ref, small_ref, b_ref, state_ref, *, to_end):
    for pair, lanes in enumerate(lanes_of(u_ref)):
        rows = small_ref[pair]
        if to_end:
            last = rows[0:2, rows.shape[1] - 1 :]
            weights = jnp.exp(last - rows[0:2]) * rows[2:4]
        else:
            weights = jnp.exp(rows[0:2])
        u = wide(u_ref[:, lanes])
        weighted = narrow(u * spread(weights, u.shape))
        state_ref[lanes, :] = narrow(inner_rows(weighted, b_ref[...]))


def scan_kernel(u_ref, small_ref, b_ref, c_ref, y_ref, cb_ref):
    size = SCAN_BLOCK
    count = u_ref.shape[0] // size
    block = [slice(i * size, (i + 1) * size) for i in range(count)]

    @pl.when(pl.program_id(0) == 0)
    def _():
        for i in range(count):
            for j in range(i + 1):
                cb_ref[block[i], block[j]] = times_back(c_ref[block[i], :], b_ref[block[j], :])

    lower = lax.broadcasted_iota(jnp.int32, (size, size), 0) >= lax.broadcasted_iota(
        jnp.int32, (size, size), 1
    )
    for pair, lanes in enumerate(lanes_of(u_ref)):
        rows = small_ref[pair]
        cols = rows.T
        for i in range(count):
            parts = []
            for h in range(2):
                total = jnp.zeros((size, 128), jnp.float32)
                for j in range(i + 1):
                    difference = cols[block[i], h : h + 1] - rows[h : h + 1, block[j]]
                    if i == j:
                        difference = jnp.where(lower, difference, NEG_FILL)
                    weights = cb_ref[block[i], block[j]] * rows[2 + h : 3 + h, block[j]]
                    mixing = narrow(jnp.exp(difference) * weights)
                    total = total + matmul_low(mixing, u_ref[block[j], lanes])
                parts.append(total)
            skip = split_lanes(cols[block[i], 4:5], cols[block[i], 5:6], parts[0].shape)
            values = split_lanes(*parts, parts[0].shape) + skip * wide(u_ref[block[i], lanes])
            y_ref[block[i], lanes] = values


def carry_kernel(y_ref, z_ref, small_ref, c_ref, state_ref, out_ref, gated_ref):
    for pair, lanes in enumerate(lanes_of(y_ref)):
        carried = times_back(c_ref[...], state_ref[lanes, :])
        decay = spread(jnp.exp(small_ref[pair][0:2]), carried.shape)
        values = y_ref[:, lanes] + carried * decay
        out_ref[:, lanes] = values
        gate = z_ref[:, lanes]
        gated_ref[:, lanes] = narrow(values * (gate * jax.nn.sigmoid(gate)))


def scan_back_kernel(u_ref, dy_ref, small_ref, b_ref, c_ref, dw_ref, sums_ref, db_ref, dc_ref, cb_ref, mix_ref):
    size = SCAN_BLOCK
    count = u_ref.shape[0] // size
    width = u_ref.shape[1]
    block = [slice(i * size, (i + 1) * size) for i in range(count)]

    @pl.when(pl.program_id(0) == 0)
    def _():
        mix_ref[...] = jnp.zeros_like(mix_ref)
        for i in range(count):
            for j in range(i, count):
                cb_ref[block[i], block[j]] = times_back(b_ref[block[i], :], c_ref[block[j], :])

    rows = small_ref[0]
    cols = rows.T
    upper = lax.broadcasted_iota(jnp.int32, (size, size), 0) <= lax.broadcasted_iota(
        jnp.int32, (size, size), 1
    )
    lane = lax.broadcasted_iota(jnp.int32, (size, width), 1)
    read_sums = [[jnp.zeros((1, size), jnp.float32) for _ in range(count)] for _ in range(2)]
    write_sums = [[], []]
    ones = jnp.ones((8, size), jnp.bfloat16)
    for i in range(count):
        parts = []
        for h in range(2):
            total = jnp.zeros((size, width), jnp.float32)
            write_sum = jnp.zeros((8, size), jnp.float32)
            step = cols[block[i], 2 + h : 3 + h]
            for j in range(i, count):
                difference = rows[h : h + 1, block[j]] - cols[block[i], h : h + 1]
                if i == j:
                    difference = jnp.where(upper, difference, NEG_FILL)
                decay = jnp.exp(difference)
                dy = dy_ref[block[j], :]
                dy_head = jnp.where((lane < width // 2) == (h == 0), dy, jnp.zeros_like(dy))
                product = decay * times_back(u_ref[block[i], :], dy_head)
                crossing = cb_ref[block[i], block[j]]
                total = total + matmul_low(narrow(decay * crossing), dy)
                weighted = product * step
                mix_ref[block[i], block[j]] += weighted
                high, low = in_two(product * crossing)
                write_sum = write_sum + times_back(ones, high) + times_back(ones, low)
                read_sums[h][j] = read_sums[h][j] + jnp.sum(weighted * crossing, axis=0, keepdims=True)
            parts.append(total)
            write_sums[h].append(write_sum)
        dw_ref[block[i], :] = split_lanes(*parts, parts[0].shape)
    writes = [jnp.concatenate(write_sums[h], axis=1)[0:1] for h in range(2)]
    skip = jnp.sum(wide(u_ref[...]) * wide(dy_ref[...]), axis=0, keepdims=True)
    skip = jnp.concatenate([skip, jnp.zeros((1, u_ref.shape[0] - width), jnp.float32)], axis=1)
    reads = [jnp.concatenate(read_sums[h], axis=1) for h in range(2)]
    sums_ref[0] = jnp.concatenate(reads + writes + [skip, jnp.zeros_like(skip)] + reads, axis=0)

    @pl.when(pl.program_id(0) == pl.num_programs(0) - 1)
    def _():
        for i in range(count):
            total = jnp.zeros((size, b_ref.shape[1]), jnp.float32)
            for j in range(i, count):
                total = total + matmul_low(narrow(mix_ref[block[i], block[j]]), c_ref[block[j], :])
            db_ref[block[i], :] = total
        for j in range(count):
            total = jnp.zeros((size, b_ref.shape[1]), jnp.float32)
            for i in range(j + 1):
                total = total + inner_rows(narrow(mix_ref[block[i], block[j]]), b_ref[block[i], :])
            dc_ref[block[j], :] = total


def carry_back_kernel(
    u_ref, dy_ref, small_ref, sums_ref, dw_ref, b_ref, c_ref, state_ref, grad_ref, db_in_ref, dc_in_ref,
    du_ref, steps_ref, db_ref, dc_ref,
):
    tokens = u_ref.shape[0]

    @pl.when(pl.program_id(0) == 0)
    def _():
        db_ref[...] = db_in_ref[...]
        dc_ref[...] = dc_in_ref[...]

    all_started, all_ended = ([], [])
    for pair, lanes in enumerate(lanes_of(u_ref)):
        rows = small_ref[pair]
        last = rows[0:2, tokens - 1 :]
        u = wide(u_ref[:, lanes])
        dy = wide(dy_ref[:, lanes])
        state = state_ref[lanes, :]
        grad = grad_ref[lanes, :]
        started = spread(jnp.exp(rows[0:2]), u.shape) * dy
        tail = spread(jnp.exp(last - rows[0:2]), u.shape)
        ended = tail * u
        step = spread(rows[2:4], u.shape)
        left = times_back(b_ref[...], grad)
        dw = dw_ref[:, lanes] + tail * left
        du_ref[:, lanes] = narrow(step * dw + spread(rows[4:6], u.shape) * dy)
        all_started.append(narrow(started))
        all_ended.append(narrow(ended * step))
        reads = lane_sums(started * times_back(c_ref[...], state))[0:2]
        writes = lane_sums(ended * left)[0:2]
        sums = sums_ref[pair]
        written = sums[2:4] + writes
        slope = sums[0:2] + reads - rows[2:4] * written
        products = jnp.sum(wide(state) * wide(grad), axis=1, keepdims=True)
        height = products.shape[0] // 2
        across = jnp.concatenate(
            [
                jnp.sum(products[:height], axis=0, keepdims=True),
                jnp.sum(products[height:], axis=0, keepdims=True),
            ],
            axis=0,
        ) * jnp.exp(last)
        across = across + jnp.sum(rows[2:4] * writes, axis=1, keepdims=True)
        held = jnp.concatenate([slope, jnp.zeros((6, tokens), jnp.float32)], axis=0)
        place = lax.broadcasted_iota(jnp.int32, held.shape, 1)
        reach = 1
        while reach < tokens:
            held = held + jnp.where(place < tokens - reach, pltpu.roll(held, tokens - reach, 1), 0.0)
            reach = 2 * reach
        flow = held[0:2] + across
        steps_ref[pair] = jnp.concatenate([written + rows[6:8] * flow, flow, held[2:6]], axis=0)
    dc_ref[...] += matmul_low(jnp.concatenate(all_started, axis=1), state_ref[...])
    db_ref[...] += matmul_low(jnp.concatenate(all_ended, axis=1), grad_ref[...])


def attend_scores(rank_ref, k_ref, q_ref, own, factor):
    scores = times_back(k_ref[...], q_ref[...]) * factor
    keys, queries = scores.shape
    row = lax.broadcasted_iota(jnp.int32, (own, queries), 0)
    column = lax.broadcasted_iota(jnp.int32, (own, queries), 1) + pl.program_id(1) * queries
    near = jnp.where(row <= column, scores[:own], NEG_FILL)
    if keys == own:
        return near
    far_row = lax.broadcasted_iota(jnp.int32, (keys - own, queries), 0)
    far = jnp.where(far_row < rank_ref[0] * own, scores[own:], NEG_FILL)
    return jnp.concatenate([near, far], axis=0)


def attend_kernel(rank_ref, q_ref, k_ref, v_ref, out_ref, log_ref, flat_ref, *, own, factor):
    @pl.when((pl.program_id(0) == 0) & (pl.program_id(1) == 0))
    def _():
        flat_ref[...] = v_ref[...].T

    scores = attend_scores(rank_ref, k_ref, q_ref, own, factor)
    maxima = jnp.max(scores, axis=0, keepdims=True)
    weights = jnp.exp(scores - maxima)
    totals = jnp.sum(weights, axis=0, keepdims=True)
    probability = narrow(weights * (1.0 / totals))
    out_ref[...] = narrow(matmul_low(flat_ref[...], probability).T)
    log_ref[0] = jnp.broadcast_to(maxima + jnp.log(totals), log_ref.shape[1:])


def attend_back_kernel(
    rank_ref, q_ref, do_ref, log_ref, k_ref, v_ref, dq_ref, dk_ref, dv_ref, flat_ref, *, own, factor
):
    @pl.when((pl.program_id(0) == 0) & (pl.program_id(1) == 0))
    def _():
        flat_ref[...] = k_ref[...].T
        dk_ref[...] = jnp.zeros_like(dk_ref)
        dv_ref[...] = jnp.zeros_like(dv_ref)

    scores = attend_scores(rank_ref, k_ref, q_ref, own, factor)
    probability = jnp.exp(scores - log_ref[0][0:1])
    dv_ref[...] += matmul_low(narrow(probability), do_ref[...])
    grad_prob = times_back(v_ref[...], do_ref[...])
    centre = jnp.sum(probability * grad_prob, axis=0, keepdims=True)
    grad_score = narrow(probability * (grad_prob - centre))
    dk_ref[...] += matmul_low(grad_score, q_ref[...]) * factor
    dq_ref[...] = narrow((matmul_low(flat_ref[...], grad_score) * factor).T)


def call(name, kernel, grid, specs, args, outs, scratch=()):
    return pl.pallas_call(
        kernel,
        name=name,
        grid=grid,
        in_specs=specs,
        out_specs=[spec for _, spec in outs],
        out_shape=[out for out, _ in outs],
        scratch_shapes=list(scratch),
        cost_estimate=pl.CostEstimate(flops=0, bytes_accessed=0, transcendentals=0),
        compiler_params=pltpu.CompilerParams(vmem_limit_bytes=48 * 1024 * 1024),
    )(*args)


def like(shape, kind):
    return jax.ShapeDtypeStruct(shape, kind)


class Scan:
    def __init__(self, tokens, inner, state):
        self.tokens, self.inner, self.state = (tokens, inner, state)
        self.pairs = inner // 128
        self.shared = pl.BlockSpec((tokens, state), lambda p: (0, 0))
        self.small_like = like((self.pairs, 8, tokens), jnp.float32)
        self.square = pltpu.VMEM((tokens, tokens), jnp.float32)

    def specs(self, group):
        group = math.gcd(group, self.pairs)
        return (
            (self.pairs // group,),
            pl.BlockSpec((self.tokens, 128 * group), lambda p: (0, p)),
            pl.BlockSpec((group, 8, self.tokens), lambda p: (p, 0, 0)),
            pl.BlockSpec((128 * group, self.state), lambda p: (p, 0)),
        )

    def rows_like(self, kind):
        return like((self.tokens, self.inner), kind)

    def own_state(self, u, small, b, to_end):
        grid, tile, row, states = self.specs(6)
        return call(
            "own_state",
            partial(state_kernel, to_end=to_end),
            grid,
            [tile, row, self.shared],
            (u, small, b),
            [(like((self.inner, self.state), jnp.bfloat16), states)],
        )[0]

    def within(self, u, small, b, c):
        grid, tile, row, states = self.specs(6)
        return call(
            "scan",
            scan_kernel,
            grid,
            [tile, row, self.shared, self.shared],
            (u, small, b, c),
            [(self.rows_like(jnp.float32), tile)],
            [self.square],
        )[0]

    def carried(self, y, z, small, c, state):
        grid, tile, row, states = self.specs(6)
        return call(
            "carry",
            carry_kernel,
            grid,
            [tile, tile, row, self.shared, states],
            (y, z, small, c, state),
            [(self.rows_like(jnp.float32), tile), (self.rows_like(jnp.bfloat16), tile)],
        )

    def within_back(self, u, dy, small, b, c):
        shared = like((self.tokens, self.state), jnp.float32)
        grid, tile, row, states = self.specs(1)
        return call(
            "scan_back",
            scan_back_kernel,
            grid,
            [tile, tile, row, self.shared, self.shared],
            (u, dy, small, b, c),
            [(self.rows_like(jnp.float32), tile), (self.small_like, row)] + 2 * [(shared, self.shared)],
            [self.square, self.square],
        )

    def carried_back(self, u, dy, small, sums, dw, b, c, state, grad, db, dc):
        shared = like((self.tokens, self.state), jnp.float32)
        grid, tile, row, states = self.specs(6)
        return call(
            "carry_back",
            carry_back_kernel,
            grid,
            [tile, tile, row, row, tile] + 2 * [self.shared] + 2 * [states] + 2 * [self.shared],
            (u, dy, small, sums, dw, b, c, state, grad, db, dc),
            [(self.rows_like(jnp.bfloat16), tile), (self.small_like, row)] + 2 * [(shared, self.shared)],
        )


class Attend:
    def __init__(self, tokens, keys, heads):
        self.tokens, self.keys, self.heads = (tokens, keys, heads)
        size = min(256, tokens)
        self.grid = (heads, tokens // size)
        self.factor = 1.0 / math.sqrt(AHEAD_DIM)
        self.rank = pl.BlockSpec(memory_space=pltpu.SMEM)
        self.tile = pl.BlockSpec((size, AHEAD_DIM), lambda h, q: (q, h))
        self.log = pl.BlockSpec((1, 8, size), lambda h, q: (h, 0, q))
        self.whole = pl.BlockSpec((keys, AHEAD_DIM), lambda h, q: (0, 0))
        self.rows_like = like((tokens, heads * AHEAD_DIM), jnp.bfloat16)
        self.flat = pltpu.VMEM((AHEAD_DIM, keys), jnp.bfloat16)

    def forward(self, rank, q, k, v):
        return call(
            "attend",
            partial(attend_kernel, own=self.tokens, factor=self.factor),
            self.grid,
            [self.rank, self.tile, self.whole, self.whole],
            (rank, q, k, v),
            [(self.rows_like, self.tile), (like((self.heads, 8, self.tokens), jnp.float32), self.log)],
            [self.flat],
        )

    def back(self, rank, q, do, log, k, v):
        whole = like((self.keys, AHEAD_DIM), jnp.float32)
        return call(
            "attend_back",
            partial(attend_back_kernel, own=self.tokens, factor=self.factor),
            self.grid,
            [self.rank, self.tile, self.tile, self.log, self.whole, self.whole],
            (rank, q, do, log, k, v),
            [(self.rows_like, self.tile), (whole, self.whole), (whole, self.whole)],
            [self.flat],
        )


def call_at(name, kernel, scalars, grid, specs, args, outs):
    return pl.pallas_call(
        kernel,
        name=name,
        grid_spec=pltpu.PrefetchScalarGridSpec(
            num_scalar_prefetch=1,
            grid=grid,
            in_specs=specs,
            out_specs=[spec for _, spec in outs],
        ),
        out_shape=[out for out, _ in outs],
        cost_estimate=pl.CostEstimate(flops=0, bytes_accessed=0, transcendentals=0),
        compiler_params=pltpu.CompilerParams(vmem_limit_bytes=48 * 1024 * 1024),
    )(scalars, *args)


def mean_scale(values):
    return lax.rsqrt(jnp.mean(values * values, axis=-1, keepdims=True) + EPSILON)


def norm_kernel(x_ref, gain_ref, out_ref):
    x = wide(x_ref[...])
    out_ref[...] = narrow(x * mean_scale(x) * gain_ref[...])


def normed(x, gain):
    rows, width = x.shape
    size = min(128, rows)
    tile = pl.BlockSpec((size, width), lambda i: (i, 0))
    line = pl.BlockSpec((1, width), lambda i: (0, 0))
    return call(
        "norm_one", norm_kernel, (rows // size,), [tile, line], (x, gain), [(like(x.shape, x.dtype), tile)]
    )[0]


def middle_kernel(at_ref, x_ref, mine_ref, theirs_ref, gain_ref, middle_ref, out_ref, sum_ref):
    @pl.when(pl.program_id(0) == 0)
    def _():
        sum_ref[...] = jnp.zeros_like(sum_ref)

    mixed = wide(mine_ref[...]) + wide(theirs_ref[...])
    middle = wide(x_ref[...]) + mixed
    middle_ref[...] = middle
    out_ref[...] = narrow(middle * mean_scale(middle) * gain_ref[...])
    sum_ref[...] += jnp.sum(mixed * mixed, axis=0, keepdims=True)


def middle_norm(at, x, mine, theirs, gain):
    rows, width = mine.shape
    size = min(128, rows)
    steps = rows // size
    tile = pl.BlockSpec((size, width), lambda i, at: (i, 0))
    half = pl.BlockSpec((size, width), lambda i, at: (at[0] * steps + i, 0))
    line = pl.BlockSpec((1, width), lambda i, at: (0, 0))
    return call_at(
        "norm_two",
        middle_kernel,
        at,
        (steps,),
        [half, tile, tile, line],
        (x, mine, theirs, gain),
        [
            (like(mine.shape, jnp.float32), tile),
            (like(mine.shape, jnp.bfloat16), tile),
            (like((1, width), jnp.float32), line),
        ],
    )


def norm_back_kernel(at_ref, x_ref, base_ref, mine_ref, theirs_ref, gain_ref, *outs):
    sum_ref = outs[-1]

    @pl.when(pl.program_id(0) == 0)
    def _():
        sum_ref[...] = jnp.zeros_like(sum_ref)

    grad = wide(mine_ref[...]) + wide(theirs_ref[...])
    x = wide(x_ref[...])
    scale = mean_scale(x)
    weighted = grad * gain_ref[...]
    inner = jnp.mean(weighted * x, axis=-1, keepdims=True)
    total = wide(base_ref[...]) + (scale * weighted - x * (scale * scale * scale * inner))
    for out_ref in outs[:-1]:
        out_ref[...] = total.astype(out_ref.dtype)
    sum_ref[...] += jnp.sum(grad * x * scale, axis=0, keepdims=True)


def norm_grad(name, at, x, base, mine, theirs, gain, kinds):
    rows, width = mine.shape
    size = min(128, rows)
    steps = rows // size
    tile = pl.BlockSpec((size, width), lambda i, at: (i, 0))
    half = pl.BlockSpec((size, width), lambda i, at: (at[0] * steps + i, 0))
    line = pl.BlockSpec((1, width), lambda i, at: (0, 0))
    return call_at(
        name,
        norm_back_kernel,
        at,
        (steps,),
        [half if x.shape[0] > rows else tile, half if base.shape[0] > rows else tile, tile, tile, line],
        (x, base, mine, theirs, gain),
        [(like(mine.shape, kind), tile) for kind in kinds] + [(like((1, width), jnp.float32), line)],
    )


def expand_kernel(x_ref, gate_ref, up_ref, dact_ref, act_ref, grad_ref):
    gate = matmul_low(x_ref[...], gate_ref[...])
    up = matmul_low(x_ref[...], up_ref[...])
    dact = dact_ref[...]
    logistic = jax.nn.sigmoid(gate)
    silu = gate * logistic
    act_ref[...] = narrow(silu * up)
    grad_ref[0] = narrow(dact * up * (logistic * (1.0 + gate * (1.0 - logistic))))
    grad_ref[1] = narrow(dact * silu)


def expand(x, weight, dact):
    rows, depth = x.shape
    width = dact.shape[1]
    size = min(256, width)
    steps = width // size
    return call(
        "expand",
        expand_kernel,
        (steps,),
        [
            pl.BlockSpec((rows, depth), lambda j: (0, 0)),
            pl.BlockSpec((depth, size), lambda j: (0, j)),
            pl.BlockSpec((depth, size), lambda j: (0, steps + j)),
            pl.BlockSpec((rows, size), lambda j: (0, j)),
        ],
        (x, weight, weight, dact),
        [
            (like((rows, width), jnp.bfloat16), pl.BlockSpec((rows, size), lambda j: (0, j))),
            (like((2, rows, width), jnp.bfloat16), pl.BlockSpec((2, rows, size), lambda j: (0, 0, j))),
        ],
    )


def share_kernel(at_ref, *refs, count, back, added):
    total = jnp.zeros(refs[-1].shape, jnp.float32)
    for former, latter in zip(refs[:count], refs[count : 2 * count], strict=True):
        rows = former[...].reshape(former.shape[-2:])
        total = total + (times_back(rows, latter[...]) if back else matmul_low(rows, latter[...]))
    if added:
        total = total + wide(refs[2 * count][...])
    refs[-1][...] = narrow(total)


def half_share(name, at, terms, back, added=None):
    rows = terms[0][0].shape[-2] // 2
    width = terms[0][2].shape[0 if back else 1]
    size = min(512, width)
    specs = []
    for former, plane, _, _ in terms:
        if former.ndim == 3:
            specs.append(
                pl.BlockSpec((1, rows, former.shape[2]), lambda j, at, plane=plane: (plane, at[0], 0))
            )
        else:
            specs.append(pl.BlockSpec((rows, former.shape[1]), lambda j, at: (at[0], 0)))
    for former, _, latter, columns in terms:
        if back:
            specs.append(pl.BlockSpec((size, former.shape[-1]), lambda j, at, c=columns: (j, c)))
        else:
            specs.append(pl.BlockSpec((former.shape[-1], size), lambda j, at: (0, j)))
    args = [term[0] for term in terms] + [term[2] for term in terms]
    tile = pl.BlockSpec((rows, size), lambda j, at: (0, j))
    if added is not None:
        specs.append(tile)
        args.append(added)
    kernel = partial(share_kernel, count=len(terms), back=back, added=added is not None)
    return call_at(
        name, kernel, at, (width // size,), specs, args, [(like((rows, width), jnp.bfloat16), tile)]
    )[0]


def weight_kernel(at_ref, own_ref, *refs, shifts, count):
    out_ref = refs[-1]
    half = own_ref.shape[0] // 2
    pairs = refs[: 2 * shifts]
    seconds = refs[2 * shifts : -1]
    own = own_ref[...].T
    flat = [ref[...].T for ref in pairs]
    places = [pl.ds(pl.multiple_of(which * half, half), half) for which in (at_ref[0], 1 - at_ref[0])]
    at = 0
    for index in range(count):
        planes = seconds[index].shape[0] if seconds[index].ndim == 3 else 1
        for plane in range(planes):
            width = seconds[index].shape[-1]
            for start in range(0, width, 512):
                stop = min(width, start + 512)

                def rows(ref, place):
                    if planes > 1:
                        return ref[plane, place, start:stop]
                    return ref[place, start:stop]

                total = matmul_low(own, rows(seconds[index], slice(None)))
                for shift in range(shifts):
                    ref = seconds[count * (shift + 1) + index]
                    for which in range(2):
                        total = total + matmul_low(flat[2 * shift + which], rows(ref, places[which]))
                out_ref[:, at + start : at + stop] = narrow(total)
            at = at + width


def weight_part(name, at, own, others, seconds, arrived):
    shifts = len(others)
    tokens = own.shape[0]
    share = own.shape[1] // (shifts + 1)
    size = min(256, share)
    specs = [pl.BlockSpec((tokens, size), lambda m, at: (0, at[1] * (share // size) + m))]
    args = [own]
    for pair in others:
        for part in pair:
            specs.append(pl.BlockSpec((tokens // 2, size), lambda m, at: (0, m)))
            args.append(part)
    width = 0
    for group in [seconds] + list(arrived):
        for part in group:
            specs.append(pl.BlockSpec(part.shape, lambda m, at, nd=part.ndim: (0,) * nd))
            args.append(part)
    for part in seconds:
        width = width + part.shape[-1] * (part.shape[0] if part.ndim == 3 else 1)
    kernel = partial(weight_kernel, shifts=shifts, count=len(seconds))
    tile = pl.BlockSpec((size, width), lambda m, at: (m, 0))
    return call_at(
        name, kernel, at, (share // size,), specs, args, [(like((share, width), jnp.bfloat16), tile)]
    )[0]


def body(
    hidden,
    cotangent,
    norm1_gain,
    ssm_in,
    ssm_bc,
    ssm_dt,
    dt_bias,
    a_log,
    d_skip,
    ssm_out,
    attn_q,
    attn_kv,
    attn_out,
    norm2_gain,
    mlp_gate_up,
    mlp_down,
):
    ctx_rank = lax.axis_index("ctx")
    ctx_count = lax.axis_size("ctx")
    tensor_rank = lax.axis_index("tensor")
    core = tensor_rank % 2
    chip = tensor_rank // 2
    hidden_rows = hidden[0]
    grad_low = cotangent[0]
    tokens, model_width = hidden_rows.shape
    half = tokens // 2
    inner_local = ssm_in.shape[2]
    heads_local = ssm_dt.shape[1]
    head_width = inner_local // heads_local
    head_pairs = heads_local // 2
    state_width = ssm_bc.shape[2]
    bc_share = 2 * state_width // 4
    heads_query = attn_q.shape[1] // AHEAD_DIM
    ff_local = mlp_down.shape[0]
    here = jnp.stack([core, lax.axis_index("dp")]).astype(jnp.int32)
    there = jnp.stack([1 - core, lax.axis_index("dp")]).astype(jnp.int32)
    gain_one = norm1_gain[None]
    gain_two = norm2_gain[None]

    input_one = normed(hidden_rows, gain_one)
    u_matrix = ssm_in[:, 1]
    bc_matrix = ssm_bc.reshape(model_width, 2 * state_width)
    source_rows = matmul_low(input_one, u_matrix).astype(jnp.bfloat16)
    bc_rows = matmul_low(input_one, bc_matrix).astype(jnp.bfloat16)
    write_rows = bc_rows[:, :state_width]
    read_rows = bc_rows[:, state_width:]
    dt_pre = lax.dot_general(
        ssm_dt, input_one, (((0,), (1,)), ((), ())), preferred_element_type=jnp.float32
    ) + dt_bias[:, None]
    dt_rows = jax.nn.softplus(dt_pre)
    decay_rate = -jnp.exp(a_log)
    running = jnp.cumsum(dt_rows * decay_rate[:, None], axis=1)

    def by_head(value):
        return jnp.broadcast_to(value[:, None], (heads_local, tokens))

    small_rows = jnp.stack([running, dt_rows, by_head(d_skip), by_head(decay_rate)], axis=1)
    small_rows = small_rows.reshape(head_pairs, 2, 4, tokens).transpose(0, 2, 1, 3)
    small_rows = small_rows.reshape(head_pairs, 8, tokens)
    scan = Scan(tokens, inner_local, state_width)
    own_state = scan.own_state(source_rows, small_rows, write_rows, True)

    one_late = after(input_one, own_state)
    kv_pair = cut(attn_kv, chip, AHEAD_DIM, 2)
    key_value = matmul_low(one_late, kv_pair.reshape(model_width, 2 * AHEAD_DIM)).astype(jnp.bfloat16)
    kv_sent = cut(key_value, core, AHEAD_DIM, 1)
    kv_got = [kv_sent] + [moved(kv_sent, "ctx", shift) for shift in range(1, ctx_count)]
    cot_sent = send_columns(cut(after(grad_low, own_state), core, half, 0))
    one_sent = send_columns(cut(one_late, core, half, 0))
    z_matrix = after(ssm_in, own_state)[:, 0]
    queries = matmul_low(one_late, attn_q).astype(jnp.bfloat16)
    gate_ssm = matmul_low(one_late, z_matrix)
    attend = Attend(tokens, ctx_count * tokens, heads_query)
    rank = ctx_rank.astype(jnp.int32)[None]
    kept = {}

    def fill_within(sent):
        kept["within"] = scan.within(source_rows, after(small_rows, own_state), write_rows, read_rows)
        return (kept["within"], gate_ssm, queries)

    def fill_attend(sent):
        mine = jnp.concatenate(kv_got, axis=0)
        other = partner(mine, CORE)
        kept["key"] = jnp.where(core == 0, mine, other)
        kept["value"] = jnp.where(core == 0, other, mine)
        kept["attended"], kept["log"] = attend.forward(
            after(rank, sent), queries, kept["key"], kept["value"]
        )
        kept["attended_sent"] = send_rows(kept["attended"])
        return (kept["attended"],)

    def fill_act(sent):
        kept["act"] = times_back(after(grad_low, sent), mlp_down)
        return (kept["act"],)

    entering = chained(own_state, running[:, -1], True, [fill_within, fill_attend, fill_act])
    key_rows, value_rows, attended = (kept["key"], kept["value"], kept["attended"])
    ssm_values, gated_rows = scan.carried(kept["within"], gate_ssm, small_rows, read_rows, entering)
    outs_sent = [
        [gated, att] for gated, att in zip(send_rows(gated_rows), kept["attended_sent"], strict=True)
    ]

    terms = [(gated_rows, 0, ssm_out, 0), (attended, 0, attn_out, 0)]
    given = partner(half_share("mix_other", there, terms, False), CORE)
    mix_mine = half_share("mix_own", here, terms, False, given)
    mix_theirs = partner(mix_mine, CHIP)
    gu_matrix = after(mlp_gate_up, mix_mine).reshape(model_width, 2 * ff_local)
    cot_columns = both_halves([after(part, mix_mine) for part in cot_sent])
    one_columns = both_halves([after(part, mix_mine) for part in one_sent])
    mix_theirs = after(mix_theirs, gu_matrix)
    middle, two_mine, mix_squares = middle_norm(here, hidden_rows, mix_mine, mix_theirs, gain_two)

    input_two = gather_rows(two_mine, core)
    activated, grad_gu = expand(input_two, gu_matrix, kept["act"])
    act_sent = send_rows(activated)
    two_sent = send_columns(two_mine)
    gu_sent = send_rows(grad_gu)
    terms = [(grad_gu, 0, gu_matrix, 0), (grad_gu, 1, gu_matrix, 1)]
    given = partner(half_share("two_other", there, terms, True), CORE)
    two_back = half_share("two_own", here, terms, True, given)
    two_theirs = partner(two_back, CHIP)
    terms = [(after(activated, two_back), 0, mlp_down, 0)]
    given = partner(half_share("mlp_other", there, terms, False), CORE)
    mlp_mine = half_share("mlp_own", here, terms, False, given)
    down_part = weight_part(
        "grad_down", after(here, mlp_mine), grad_low, cot_columns, [activated], [[part] for part in act_sent]
    )
    grad_down = ctx_sum(down_part)
    two_theirs = after(two_theirs, down_part)
    grad_middle, mix_grad_mine, gain_two_sum = norm_grad(
        "norm_two_back", here, middle, grad_low, two_back, two_theirs, gain_two, (jnp.float32, jnp.bfloat16)
    )

    grad_mix = gather_rows(mix_grad_mine, core)
    mix_sent = send_columns(mix_grad_mine)
    grad_gated = times_back(grad_mix, ssm_out)
    grad_values = (grad_gated * jax.nn.silu(gate_ssm)).astype(jnp.bfloat16)
    own_grad = scan.own_state(grad_values, small_rows, read_rows, False)
    mlp_theirs = partner(after(mlp_mine, own_grad), CHIP)
    grad_gate_ssm = (grad_gated * ssm_values * silu_slope(gate_ssm)).astype(jnp.bfloat16)
    grad_attended = times_back(after(grad_mix, own_grad), attn_out).astype(jnp.bfloat16)
    gate_sent = send_rows(grad_gate_ssm)

    def fill_attend_back(sent):
        grad_query, grad_key, grad_value = attend.back(
            after(rank, own_grad), queries, grad_attended, kept["log"], key_rows, value_rows
        )
        kept["grad_query"] = grad_query
        kept["query_sent"] = send_rows(grad_query)
        own_part = jnp.where(core == 0, grad_key, grad_value)
        given = partner(jnp.where(core == 0, grad_value, grad_key).astype(jnp.bfloat16), CORE)
        paired = (own_part + given.astype(jnp.float32)).reshape(ctx_count, tokens, AHEAD_DIM)
        kept["kv"] = paired[0]
        kept["kv_sent"] = [
            moved(paired[shift].astype(jnp.bfloat16), "ctx", -shift) for shift in range(1, ctx_count)
        ]
        return (grad_query,)

    def fill_scan_back(sent):
        kept["scan"] = scan.within_back(
            source_rows, after(grad_values, sent), small_rows, write_rows, read_rows
        )
        return (kept["scan"][0],)

    def fill_weights(sent):
        kept["gate_up"] = weight_part(
            "grad_gate_up",
            after(here, sent),
            input_two,
            both_halves(two_sent),
            [grad_gu],
            [[part] for part in gu_sent],
        )
        kept["outs"] = weight_part(
            "grad_outs", after(here, sent), grad_mix, both_halves(mix_sent), [gated_rows, attended], outs_sent
        )
        return (kept["gate_up"], kept["outs"])

    leaving = chained(own_grad, running[:, -1], False, [fill_attend_back, fill_scan_back, fill_weights])
    grad_gate_up = ctx_sum(kept["gate_up"])
    grad_outs = ctx_sum(kept["outs"])
    grad_written, scan_sums, grad_b, grad_c = kept["scan"]
    grad_source, steps, grad_b, grad_c = scan.carried_back(
        source_rows, grad_values, small_rows, scan_sums, grad_written,
        write_rows, read_rows, entering, leaving, grad_b, grad_c,
    )
    source_sent = send_rows(grad_source)
    grad_bc = jnp.concatenate([grad_b, grad_c], axis=1)
    bc_sent = partner(cut(grad_bc, 1 - core, 2 * bc_share, 1).astype(jnp.bfloat16), CORE)
    bc_mine = cut(grad_bc, core, 2 * bc_share, 1) + bc_sent.astype(jnp.float32)
    bc_given = partner(cut(bc_mine, 1 - chip, bc_share, 1).astype(jnp.bfloat16), CHIP)
    grad_bc_low = (cut(bc_mine, chip, bc_share, 1) + bc_given.astype(jnp.float32)).astype(jnp.bfloat16)
    kv_sum = kept["kv"]
    for part in kept["kv_sent"]:
        kv_sum = kv_sum + part.astype(jnp.float32)
    grad_kv_low = kv_sum.astype(jnp.bfloat16)
    grad_query = kept["grad_query"]
    kv_columns = cut(attn_kv, chip, AHEAD_DIM, 2)
    kv_columns = lax.dynamic_index_in_dim(kv_columns, core, 1, keepdims=False)
    ins_first = weight_part(
        "grad_ins_first",
        here,
        input_one,
        one_columns,
        [grad_gate_ssm, grad_query],
        [[gate, query] for gate, query in zip(gate_sent, kept["query_sent"], strict=True)],
    )
    grad_ins_first = ctx_sum(ins_first)

    grad_dt_pre = steps[:, 0:2].reshape(heads_local, tokens) * jax.nn.sigmoid(dt_pre)
    flow_rows = steps[:, 2:4].reshape(heads_local, tokens)
    grad_dt_bias = jnp.sum(grad_dt_pre, axis=1)
    grad_a_log = decay_rate * jnp.sum(dt_rows * flow_rows, axis=1)
    grad_d_skip = jnp.sum(scan_sums[:, 4, : 2 * head_width].reshape(heads_local, head_width), axis=1)
    pad = -heads_local % AHEAD_DIM
    grad_dt_low = jnp.pad(grad_dt_pre.astype(jnp.bfloat16).T, ((0, 0), (0, pad)))
    grad_small = jnp.concatenate([grad_kv_low, grad_bc_low, grad_dt_low], axis=1)
    small_sent = send_rows(grad_small)
    weight_small = jnp.concatenate(
        [
            kv_columns,
            cut(bc_matrix, 2 * core + chip, bc_share, 1),
            jnp.pad(ssm_dt, ((0, 0), (0, pad))),
        ],
        axis=1,
    )
    terms = [
        (grad_gate_ssm, 0, z_matrix, 0),
        (grad_source, 0, u_matrix, 0),
        (grad_query, 0, attn_q, 0),
        (grad_small, 0, weight_small, 0),
    ]
    given = partner(half_share("one_other", there, terms, True), CORE)
    one_back = half_share("one_own", here, terms, True, given)
    one_theirs = partner(one_back, CHIP)
    ins_small = weight_part(
        "grad_ins_small", after(here, one_back), input_one, one_columns, [grad_small], [[p] for p in small_sent]
    )
    grad_ins_small = ctx_sum(ins_small)
    ins_source = weight_part(
        "grad_ins_source", after(here, ins_small), input_one, one_columns, [grad_source], [[p] for p in source_sent]
    )
    grad_ins_source = ctx_sum(ins_source)
    one_theirs = after(one_theirs, ins_source)
    hidden_mine, gain_one_sum = norm_grad(
        "norm_one_back", here, hidden_rows, grad_middle, one_back, one_theirs, gain_one, (jnp.bfloat16,)
    )
    grad_hidden = gather_rows(hidden_mine, core)

    mlp_total = mlp_mine.astype(jnp.float32) + mlp_theirs.astype(jnp.float32)
    block_out = middle + mlp_total
    output = gather_rows(block_out.astype(jnp.bfloat16), core)

    kv_part = grad_ins_small[:, :AHEAD_DIM]
    bc_part = grad_ins_small[:, AHEAD_DIM : AHEAD_DIM + bc_share]
    grad_ssm_dt = grad_ins_small[:, AHEAD_DIM + bc_share : AHEAD_DIM + bc_share + heads_local]
    share = kv_part.shape[0] // 4
    blocks = [cut(kv_part, tensor_rank, share, 0)]
    for stride in range(1, 4):
        blocks.append(partner(cut(kv_part, tensor_rank ^ stride, share, 0), stride))
    blocks = jnp.stack(blocks)
    bc_blocks = jnp.stack([bc_part] + [partner(bc_part, stride) for stride in range(1, 4)])

    def of_rank(pieces, rank):
        return lax.dynamic_index_in_dim(pieces, tensor_rank ^ rank, 0, keepdims=False)

    grad_attn_kv = jnp.stack(
        [
            jnp.concatenate([of_rank(blocks, kind), of_rank(blocks, 2 + kind)], axis=1)
            for kind in range(2)
        ],
        axis=1,
    )
    grad_ssm_bc = jnp.concatenate(
        [of_rank(bc_blocks, 2 * (place % 2) + place // 2) for place in range(4)], axis=1
    ).reshape(-1, 2, state_width)

    gains = jnp.concatenate([gain_one_sum, gain_two_sum], axis=0).T
    gains = gains + partner(gains, CORE)
    gains = scatter_sum(scatter_sum(gains, "dp"), "ctx")
    squares = jnp.stack([jnp.sum(mix_squares), jnp.sum(mlp_total * mlp_total), jnp.sum(block_out * block_out)])
    squares = squares + partner(squares, CORE)
    small = jnp.concatenate([grad_dt_bias, grad_a_log, grad_d_skip, squares])
    small = all_sum(all_sum(small, "dp"), "ctx")
    counted = tokens * model_width * lax.axis_size("dp") * ctx_count
    branch_rms = jnp.sqrt(small[3 * heads_local :] / counted)
    return (
        output[None],
        grad_hidden[None],
        gains[:, 0],
        jnp.stack([grad_ins_first[:, :inner_local], grad_ins_source], axis=1),
        grad_ssm_bc,
        grad_ssm_dt,
        small[:heads_local],
        small[heads_local : 2 * heads_local],
        small[2 * heads_local : 3 * heads_local],
        grad_outs[:, :inner_local].T,
        grad_ins_first[:, inner_local:],
        grad_attn_kv,
        grad_outs[:, inner_local:].T,
        gains[:, 1],
        grad_gate_up.reshape(-1, 2, ff_local),
        grad_down.T,
        branch_rms,
    )


def solution(mesh):
    return jax.shard_map(
        body,
        mesh=mesh,
        in_specs=(
            P("dp", "ctx", None),
            P("dp", "ctx", None),
            P(),
            P(None, None, "tensor"),
            P(),
            P(None, "tensor"),
            P("tensor"),
            P("tensor"),
            P("tensor"),
            P("tensor", None),
            P(None, "tensor"),
            P(),
            P("tensor", None),
            P(),
            P(None, None, "tensor"),
            P("tensor", None),
        ),
        out_specs=(
            P("dp", "ctx", None),
            P("dp", "ctx", None),
            P(("dp", "ctx")),
            P(("dp", "ctx"), None, "tensor"),
            P(("dp", "ctx"), None, None),
            P(("dp", "ctx"), "tensor"),
            P("tensor"),
            P("tensor"),
            P("tensor"),
            P("tensor", ("dp", "ctx")),
            P(("dp", "ctx"), "tensor"),
            P(("dp", "ctx", "tensor"), None, None),
            P("tensor", ("dp", "ctx")),
            P(("dp", "ctx")),
            P(("dp", "ctx"), None, "tensor"),
            P("tensor", ("dp", "ctx")),
            P(),
        ),
        check_vma=False,
    )
```

```python
from functools import partial
import math

import jax
import jax.numpy as jnp
from jax import lax
from jax.experimental import pallas as pl
from jax.experimental.pallas import tpu as pltpu
from jax.sharding import PartitionSpec as P

AHEAD_DIM = 128
SCAN_BLOCK = 256


EPSILON = 1e-05
NEG_FILL = -1e30
VMEM_GRANT = 28 * 1024 * 1024

CORE, CHIP = (1, 2)


def partner(value, stride):
    return lax.ppermute(value, "tensor", [(rank, rank ^ stride) for rank in range(4)])


def shifted(value, axis, shift):
    count = lax.axis_size(axis)
    return lax.ppermute(value, axis, [(i, (i + shift) % count) for i in range(count)])


def moved(value, axis, shift):
    count = lax.axis_size(axis)
    pairs = [(i, i + shift) for i in range(count) if 0 <= i + shift < count]
    return lax.ppermute(value, axis, pairs)


def after(value, *others):
    return lax.optimization_barrier((value,) + others)[0]


def cut(value, index, size, axis):
    return lax.dynamic_slice_in_dim(value, index * size, size, axis)


def paired_rows(mine, other, core):
    first = jnp.where(core == 0, mine, other)
    second = jnp.where(core == 0, other, mine)
    return jnp.concatenate([first, second], axis=0)


def gather_rows(mine, core):
    return paired_rows(mine, partner(mine, CORE), core)


def send_columns(rows):
    count, mine = (lax.axis_size("dp"), lax.axis_index("dp"))
    share = rows.shape[1] // count
    return [
        shifted(cut(rows, (mine + shift) % count, share, 1), "dp", shift) for shift in range(1, count)
    ]


def both_halves(arrived):
    return [(part, partner(part, CORE)) for part in arrived]


def send_rows(value):
    return [shifted(value, "dp", shift) for shift in range(1, lax.axis_size("dp"))]


def ctx_partner(value, stride):
    return lax.ppermute(value, "ctx", [(rank, rank ^ stride) for rank in range(4)])


def all_sum(value, axis):
    count, mine = (lax.axis_size(axis), lax.axis_index(axis))
    pieces = jnp.stack([value] + [shifted(value, axis, shift) for shift in range(1, count)])
    total = jnp.zeros_like(value)
    for rank in range(count):
        total = total + lax.dynamic_index_in_dim(pieces, (mine - rank) % count, 0, keepdims=False)
    return total


def chained(state, log_decay, forward, fillers):
    count = lax.axis_size("ctx")
    decay = jnp.exp(log_decay)[:, None, None]
    per_head = (decay.shape[0], state.shape[0] // decay.shape[0], state.shape[1])
    own = state.reshape(per_head)
    sent = state
    entering = None
    for step in range(1, count):
        pair = (step - 1, step) if forward else (count - step, count - step - 1)
        arrived = lax.ppermute(sent, "ctx", [pair])
        if step <= len(fillers):
            arrived = after(arrived, *fillers[step - 1](sent))
        entering = arrived if entering is None else entering + arrived
        if step < count - 1:
            total = own.astype(jnp.float32) + decay * arrived.reshape(per_head).astype(jnp.float32)
            sent = total.astype(jnp.bfloat16).reshape(state.shape)
    return entering


def matmul_low(former, latter):
    return jnp.dot(former, latter, preferred_element_type=jnp.float32)


def inner_rows(former, latter):
    return lax.dot_general(
        former, latter, (((0,), (0,)), ((), ())), preferred_element_type=jnp.float32
    )


def times_back(former, latter):
    return lax.dot_general(
        former, latter, (((1,), (1,)), ((), ())), preferred_element_type=jnp.float32
    )


def split_lanes(first, second, shape):
    lane = lax.broadcasted_iota(jnp.int32, shape, 1)
    return jnp.where(lane < shape[1] // 2, first, second)


def wide(values):
    return values.astype(jnp.float32)


def narrow(values):
    return values.astype(jnp.bfloat16)


def in_two(values):
    high = narrow(values)
    return (high, narrow(values - wide(high)))


def spread(rows, shape):
    rows = jnp.concatenate([rows, jnp.zeros((6, rows.shape[1]), jnp.float32)], axis=0)
    place = lax.broadcasted_iota(jnp.int32, (8, shape[1]), 0)
    lane = lax.broadcasted_iota(jnp.int32, (8, shape[1]), 1)
    chosen = narrow(jnp.where(place == lane // (shape[1] // 2), 1.0, 0.0))
    high, low = in_two(rows.T)
    return matmul_low(high, chosen) + matmul_low(low, chosen)


def lane_sums(values):
    place = lax.broadcasted_iota(jnp.int32, (8, values.shape[1]), 0)
    lane = lax.broadcasted_iota(jnp.int32, (8, values.shape[1]), 1)
    chosen = narrow(jnp.where(place == lane // (values.shape[1] // 2), 1.0, 0.0))
    high, low = in_two(values)
    return times_back(chosen, high) + times_back(chosen, low)


def lanes_of(ref):
    return [slice(at, at + 128) for at in range(0, ref.shape[1], 128)]


def state_kernel(u_ref, small_ref, b_ref, state_ref, *, to_end):
    for pair, lanes in enumerate(lanes_of(u_ref)):
        rows = small_ref[pair]
        if to_end:
            last = rows[0:2, rows.shape[1] - 1 :]
            weights = jnp.exp(last - rows[0:2]) * rows[2:4]
        else:
            weights = jnp.exp(rows[0:2])
        u = wide(u_ref[:, lanes])
        weighted = narrow(u * spread(weights, u.shape))
        state_ref[lanes, :] = narrow(inner_rows(weighted, b_ref[...]))


def scan_kernel(u_ref, small_ref, b_ref, c_ref, y_ref, cb_ref):
    size = SCAN_BLOCK
    count = u_ref.shape[0] // size
    block = [slice(i * size, (i + 1) * size) for i in range(count)]

    @pl.when(pl.program_id(0) == 0)
    def _():
        for i in range(count):
            for j in range(i + 1):
                cb_ref[block[i], block[j]] = times_back(c_ref[block[i], :], b_ref[block[j], :])

    lower = lax.broadcasted_iota(jnp.int32, (size, size), 0) >= lax.broadcasted_iota(
        jnp.int32, (size, size), 1
    )
    for pair, lanes in enumerate(lanes_of(u_ref)):
        rows = small_ref[pair]
        cols = rows.T
        for i in range(count):
            parts = []
            for h in range(2):
                total = jnp.zeros((size, 128), jnp.float32)
                for j in range(i + 1):
                    difference = cols[block[i], h : h + 1] - rows[h : h + 1, block[j]]
                    if i == j:
                        difference = jnp.where(lower, difference, NEG_FILL)
                    weights = cb_ref[block[i], block[j]] * rows[2 + h : 3 + h, block[j]]
                    mixing = narrow(jnp.exp(difference) * weights)
                    total = total + matmul_low(mixing, u_ref[block[j], lanes])
                parts.append(total)
            skip = split_lanes(cols[block[i], 4:5], cols[block[i], 5:6], parts[0].shape)
            values = split_lanes(*parts, parts[0].shape) + skip * wide(u_ref[block[i], lanes])
            y_ref[block[i], lanes] = values


def carry_kernel(y_ref, z_ref, small_ref, c_ref, state_ref, out_ref, gated_ref):
    for pair, lanes in enumerate(lanes_of(y_ref)):
        carried = times_back(c_ref[...], state_ref[lanes, :])
        decay = spread(jnp.exp(small_ref[pair][0:2]), carried.shape)
        values = y_ref[:, lanes] + carried * decay
        out_ref[:, lanes] = values
        gate = z_ref[:, lanes]
        gated_ref[:, lanes] = narrow(values * (gate * jax.nn.sigmoid(gate)))


def scan_back_kernel(u_ref, dy_ref, small_ref, b_ref, c_ref, dw_ref, sums_ref, db_ref, dc_ref, cb_ref, mix_ref):
    size = SCAN_BLOCK
    count = u_ref.shape[0] // size
    width = u_ref.shape[1]
    block = [slice(i * size, (i + 1) * size) for i in range(count)]

    @pl.when(pl.program_id(0) == 0)
    def _():
        mix_ref[...] = jnp.zeros_like(mix_ref)
        for i in range(count):
            for j in range(i, count):
                cb_ref[block[i], block[j]] = times_back(b_ref[block[i], :], c_ref[block[j], :])

    rows = small_ref[0]
    cols = rows.T
    upper = lax.broadcasted_iota(jnp.int32, (size, size), 0) <= lax.broadcasted_iota(
        jnp.int32, (size, size), 1
    )
    lane = lax.broadcasted_iota(jnp.int32, (size, width), 1)
    read_sums = [[jnp.zeros((1, size), jnp.float32) for _ in range(count)] for _ in range(2)]
    write_sums = [[], []]
    ones = jnp.ones((8, size), jnp.bfloat16)
    for i in range(count):
        parts = []
        for h in range(2):
            total = jnp.zeros((size, width), jnp.float32)
            write_sum = jnp.zeros((8, size), jnp.float32)
            step = cols[block[i], 2 + h : 3 + h]
            for j in range(i, count):
                difference = rows[h : h + 1, block[j]] - cols[block[i], h : h + 1]
                if i == j:
                    difference = jnp.where(upper, difference, NEG_FILL)
                decay = jnp.exp(difference)
                dy = dy_ref[block[j], :]
                dy_head = jnp.where((lane < width // 2) == (h == 0), dy, jnp.zeros_like(dy))
                product = decay * times_back(u_ref[block[i], :], dy_head)
                crossing = cb_ref[block[i], block[j]]
                total = total + matmul_low(narrow(decay * crossing), dy)
                weighted = product * step
                mix_ref[block[i], block[j]] += weighted
                high, low = in_two(product * crossing)
                write_sum = write_sum + times_back(ones, high) + times_back(ones, low)
                read_sums[h][j] = read_sums[h][j] + jnp.sum(weighted * crossing, axis=0, keepdims=True)
            parts.append(total)
            write_sums[h].append(write_sum)
        dw_ref[block[i], :] = split_lanes(*parts, parts[0].shape)
    writes = [jnp.concatenate(write_sums[h], axis=1)[0:1] for h in range(2)]
    skip = jnp.sum(wide(u_ref[...]) * wide(dy_ref[...]), axis=0, keepdims=True)
    skip = jnp.concatenate([skip, jnp.zeros((1, u_ref.shape[0] - width), jnp.float32)], axis=1)
    reads = [jnp.concatenate(read_sums[h], axis=1) for h in range(2)]
    sums_ref[0] = jnp.concatenate(reads + writes + [skip, jnp.zeros_like(skip)] + reads, axis=0)

    @pl.when(pl.program_id(0) == pl.num_programs(0) - 1)
    def _():
        for i in range(count):
            total = jnp.zeros((size, b_ref.shape[1]), jnp.float32)
            for j in range(i, count):
                total = total + matmul_low(narrow(mix_ref[block[i], block[j]]), c_ref[block[j], :])
            db_ref[block[i], :] = total
        for j in range(count):
            total = jnp.zeros((size, b_ref.shape[1]), jnp.float32)
            for i in range(j + 1):
                total = total + inner_rows(narrow(mix_ref[block[i], block[j]]), b_ref[block[i], :])
            dc_ref[block[j], :] = total


def carry_back_kernel(
    u_ref, dy_ref, small_ref, sums_ref, dw_ref, b_ref, c_ref, state_ref, grad_ref, db_in_ref, dc_in_ref,
    du_ref, steps_ref, db_ref, dc_ref,
):
    tokens = u_ref.shape[0]

    @pl.when(pl.program_id(0) == 0)
    def _():
        db_ref[...] = db_in_ref[...]
        dc_ref[...] = dc_in_ref[...]

    all_started, all_ended = ([], [])
    for pair, lanes in enumerate(lanes_of(u_ref)):
        rows = small_ref[pair]
        last = rows[0:2, tokens - 1 :]
        u = wide(u_ref[:, lanes])
        dy = wide(dy_ref[:, lanes])
        state = state_ref[lanes, :]
        grad = grad_ref[lanes, :]
        started = spread(jnp.exp(rows[0:2]), u.shape) * dy
        tail = spread(jnp.exp(last - rows[0:2]), u.shape)
        ended = tail * u
        step = spread(rows[2:4], u.shape)
        left = times_back(b_ref[...], grad)
        dw = dw_ref[:, lanes] + tail * left
        du_ref[:, lanes] = narrow(step * dw + spread(rows[4:6], u.shape) * dy)
        all_started.append(narrow(started))
        all_ended.append(narrow(ended * step))
        reads = lane_sums(started * times_back(c_ref[...], state))[0:2]
        writes = lane_sums(ended * left)[0:2]
        sums = sums_ref[pair]
        written = sums[2:4] + writes
        slope = sums[0:2] + reads - rows[2:4] * written
        products = jnp.sum(wide(state) * wide(grad), axis=1, keepdims=True)
        height = products.shape[0] // 2
        across = jnp.concatenate(
            [
                jnp.sum(products[:height], axis=0, keepdims=True),
                jnp.sum(products[height:], axis=0, keepdims=True),
            ],
            axis=0,
        ) * jnp.exp(last)
        across = across + jnp.sum(rows[2:4] * writes, axis=1, keepdims=True)
        held = jnp.concatenate([slope, jnp.zeros((6, tokens), jnp.float32)], axis=0)
        place = lax.broadcasted_iota(jnp.int32, held.shape, 1)
        reach = 1
        while reach < tokens:
            held = held + jnp.where(place < tokens - reach, pltpu.roll(held, tokens - reach, 1), 0.0)
            reach = 2 * reach
        flow = held[0:2] + across
        steps_ref[pair] = jnp.concatenate([written + rows[6:8] * flow, flow, held[2:6]], axis=0)
    dc_ref[...] += matmul_low(jnp.concatenate(all_started, axis=1), state_ref[...])
    db_ref[...] += matmul_low(jnp.concatenate(all_ended, axis=1), grad_ref[...])


def attend_scores(rank_ref, k_ref, q_ref, own, factor):
    scores = times_back(k_ref[...], q_ref[...]) * factor
    keys, queries = scores.shape
    row = lax.broadcasted_iota(jnp.int32, (own, queries), 0)
    column = lax.broadcasted_iota(jnp.int32, (own, queries), 1) + pl.program_id(1) * queries
    near = jnp.where(row <= column, scores[:own], NEG_FILL)
    if keys == own:
        return near
    far_row = lax.broadcasted_iota(jnp.int32, (keys - own, queries), 0)
    far = jnp.where(far_row < rank_ref[0] * own, scores[own:], NEG_FILL)
    return jnp.concatenate([near, far], axis=0)


def attend_kernel(rank_ref, q_ref, k_ref, v_ref, out_ref, log_ref, flat_ref, *, own, factor):
    @pl.when((pl.program_id(0) == 0) & (pl.program_id(1) == 0))
    def _():
        flat_ref[...] = v_ref[...].T

    scores = attend_scores(rank_ref, k_ref, q_ref, own, factor)
    maxima = jnp.max(scores, axis=0, keepdims=True)
    weights = jnp.exp(scores - maxima)
    totals = jnp.sum(weights, axis=0, keepdims=True)
    probability = narrow(weights * (1.0 / totals))
    out_ref[...] = narrow(matmul_low(flat_ref[...], probability).T)
    log_ref[0] = jnp.broadcast_to(maxima + jnp.log(totals), log_ref.shape[1:])


def attend_back_kernel(
    rank_ref, q_ref, do_ref, log_ref, k_ref, v_ref, dq_ref, dk_ref, dv_ref, flat_ref, *, own, factor
):
    @pl.when((pl.program_id(0) == 0) & (pl.program_id(1) == 0))
    def _():
        flat_ref[...] = k_ref[...].T
        dk_ref[...] = jnp.zeros_like(dk_ref)
        dv_ref[...] = jnp.zeros_like(dv_ref)

    scores = attend_scores(rank_ref, k_ref, q_ref, own, factor)
    probability = jnp.exp(scores - log_ref[0][0:1])
    dv_ref[...] += matmul_low(narrow(probability), do_ref[...])
    grad_prob = times_back(v_ref[...], do_ref[...])
    centre = jnp.sum(probability * grad_prob, axis=0, keepdims=True)
    grad_score = narrow(probability * (grad_prob - centre))
    dk_ref[...] += matmul_low(grad_score, q_ref[...]) * factor
    dq_ref[...] = narrow((matmul_low(flat_ref[...], grad_score) * factor).T)


def call(name, kernel, grid, specs, args, outs, scratch=()):
    return pl.pallas_call(
        kernel,
        name=name,
        grid=grid,
        in_specs=specs,
        out_specs=[spec for _, spec in outs],
        out_shape=[out for out, _ in outs],
        scratch_shapes=list(scratch),
        cost_estimate=pl.CostEstimate(flops=1, bytes_accessed=1, transcendentals=0),
        compiler_params=pltpu.CompilerParams(vmem_limit_bytes=VMEM_GRANT),
    )(*args)


def like(shape, kind):
    return jax.ShapeDtypeStruct(shape, kind)


class Scan:
    def __init__(self, tokens, inner, state):
        self.tokens, self.inner, self.state = (tokens, inner, state)
        self.pairs = inner // 128
        self.shared = pl.BlockSpec((tokens, state), lambda p: (0, 0))
        self.small_like = like((self.pairs, 8, tokens), jnp.float32)
        self.square = pltpu.VMEM((tokens, tokens), jnp.float32)

    def specs(self, group):
        group = math.gcd(group, self.pairs)
        return (
            (self.pairs // group,),
            pl.BlockSpec((self.tokens, 128 * group), lambda p: (0, p)),
            pl.BlockSpec((group, 8, self.tokens), lambda p: (p, 0, 0)),
            pl.BlockSpec((128 * group, self.state), lambda p: (p, 0)),
        )

    def rows_like(self, kind):
        return like((self.tokens, self.inner), kind)

    def own_state(self, u, small, b, to_end):
        grid, tile, row, states = self.specs(6)
        return call(
            "own_state",
            partial(state_kernel, to_end=to_end),
            grid,
            [tile, row, self.shared],
            (u, small, b),
            [(like((self.inner, self.state), jnp.bfloat16), states)],
        )[0]

    def within(self, u, small, b, c):
        grid, tile, row, states = self.specs(6)
        return call(
            "scan",
            scan_kernel,
            grid,
            [tile, row, self.shared, self.shared],
            (u, small, b, c),
            [(self.rows_like(jnp.float32), tile)],
            [self.square],
        )[0]

    def carried(self, y, z, small, c, state):
        grid, tile, row, states = self.specs(6)
        return call(
            "carry",
            carry_kernel,
            grid,
            [tile, tile, row, self.shared, states],
            (y, z, small, c, state),
            [(self.rows_like(jnp.float32), tile), (self.rows_like(jnp.bfloat16), tile)],
        )

    def within_back(self, u, dy, small, b, c):
        shared = like((self.tokens, self.state), jnp.float32)
        grid, tile, row, states = self.specs(1)
        return call(
            "scan_back",
            scan_back_kernel,
            grid,
            [tile, tile, row, self.shared, self.shared],
            (u, dy, small, b, c),
            [(self.rows_like(jnp.float32), tile), (self.small_like, row)] + 2 * [(shared, self.shared)],
            [self.square, self.square],
        )

    def carried_back(self, u, dy, small, sums, dw, b, c, state, grad, db, dc):
        shared = like((self.tokens, self.state), jnp.float32)
        grid, tile, row, states = self.specs(6)
        return call(
            "carry_back",
            carry_back_kernel,
            grid,
            [tile, tile, row, row, tile] + 2 * [self.shared] + 2 * [states] + 2 * [self.shared],
            (u, dy, small, sums, dw, b, c, state, grad, db, dc),
            [(self.rows_like(jnp.bfloat16), tile), (self.small_like, row)] + 2 * [(shared, self.shared)],
        )


class Attend:
    def __init__(self, tokens, keys, heads):
        self.tokens, self.keys, self.heads = (tokens, keys, heads)
        size = min(256, tokens)
        self.grid = (heads, tokens // size)
        self.factor = 1.0 / math.sqrt(AHEAD_DIM)
        self.rank = pl.BlockSpec(memory_space=pltpu.SMEM)
        self.tile = pl.BlockSpec((size, AHEAD_DIM), lambda h, q: (q, h))
        self.log = pl.BlockSpec((1, 8, size), lambda h, q: (h, 0, q))
        self.whole = pl.BlockSpec((keys, AHEAD_DIM), lambda h, q: (0, 0))
        self.rows_like = like((tokens, heads * AHEAD_DIM), jnp.bfloat16)
        self.flat = pltpu.VMEM((AHEAD_DIM, keys), jnp.bfloat16)

    def forward(self, rank, q, k, v):
        return call(
            "attend",
            partial(attend_kernel, own=self.tokens, factor=self.factor),
            self.grid,
            [self.rank, self.tile, self.whole, self.whole],
            (rank, q, k, v),
            [(self.rows_like, self.tile), (like((self.heads, 8, self.tokens), jnp.float32), self.log)],
            [self.flat],
        )

    def back(self, rank, q, do, log, k, v):
        whole = like((self.keys, AHEAD_DIM), jnp.float32)
        return call(
            "attend_back",
            partial(attend_back_kernel, own=self.tokens, factor=self.factor),
            self.grid,
            [self.rank, self.tile, self.tile, self.log, self.whole, self.whole],
            (rank, q, do, log, k, v),
            [(self.rows_like, self.tile), (whole, self.whole), (whole, self.whole)],
            [self.flat],
        )


def call_at(name, kernel, scalars, grid, specs, args, outs):
    return pl.pallas_call(
        kernel,
        name=name,
        grid_spec=pltpu.PrefetchScalarGridSpec(
            num_scalar_prefetch=1,
            grid=grid,
            in_specs=specs,
            out_specs=[spec for _, spec in outs],
        ),
        out_shape=[out for out, _ in outs],
        cost_estimate=pl.CostEstimate(flops=1, bytes_accessed=1, transcendentals=0),
        compiler_params=pltpu.CompilerParams(vmem_limit_bytes=VMEM_GRANT),
    )(scalars, *args)


def mean_scale(values):
    return lax.rsqrt(jnp.mean(values * values, axis=-1, keepdims=True) + EPSILON)


def norm_kernel(x_ref, gain_ref, out_ref):
    x = wide(x_ref[...])
    out_ref[...] = narrow(x * mean_scale(x) * gain_ref[...])


def normed(x, gain):
    rows, width = x.shape
    size = min(128, rows)
    tile = pl.BlockSpec((size, width), lambda i: (i, 0))
    line = pl.BlockSpec((1, width), lambda i: (0, 0))
    return call(
        "norm_one", norm_kernel, (rows // size,), [tile, line], (x, gain), [(like(x.shape, x.dtype), tile)]
    )[0]


def middle_kernel(at_ref, x_ref, mine_ref, theirs_ref, gain_ref, middle_ref, out_ref, sum_ref):
    @pl.when(pl.program_id(0) == 0)
    def _():
        sum_ref[...] = jnp.zeros_like(sum_ref)

    mixed = wide(mine_ref[...]) + wide(theirs_ref[...])
    middle = wide(x_ref[...]) + mixed
    middle_ref[...] = middle
    out_ref[...] = narrow(middle * mean_scale(middle) * gain_ref[...])
    sum_ref[...] += jnp.sum(mixed * mixed, axis=0, keepdims=True)


def middle_norm(at, x, mine, theirs, gain):
    rows, width = mine.shape
    size = min(128, rows)
    steps = rows // size
    tile = pl.BlockSpec((size, width), lambda i, at: (i, 0))
    half = pl.BlockSpec((size, width), lambda i, at: (at[0] * steps + i, 0))
    line = pl.BlockSpec((1, width), lambda i, at: (0, 0))
    return call_at(
        "norm_two",
        middle_kernel,
        at,
        (steps,),
        [half, tile, tile, line],
        (x, mine, theirs, gain),
        [
            (like(mine.shape, jnp.float32), tile),
            (like(mine.shape, jnp.bfloat16), tile),
            (like((1, width), jnp.float32), line),
        ],
    )


def norm_back_kernel(at_ref, x_ref, base_ref, mine_ref, theirs_ref, gain_ref, *outs):
    sum_ref = outs[-1]

    @pl.when(pl.program_id(0) == 0)
    def _():
        sum_ref[...] = jnp.zeros_like(sum_ref)

    grad = wide(mine_ref[...]) + wide(theirs_ref[...])
    x = wide(x_ref[...])
    scale = mean_scale(x)
    weighted = grad * gain_ref[...]
    inner = jnp.mean(weighted * x, axis=-1, keepdims=True)
    total = wide(base_ref[...]) + (scale * weighted - x * (scale * scale * scale * inner))
    for out_ref in outs[:-1]:
        out_ref[...] = total.astype(out_ref.dtype)
    sum_ref[...] += jnp.sum(grad * x * scale, axis=0, keepdims=True)


def norm_grad(name, at, x, base, mine, theirs, gain, kinds):
    rows, width = mine.shape
    size = min(128, rows)
    steps = rows // size
    tile = pl.BlockSpec((size, width), lambda i, at: (i, 0))
    half = pl.BlockSpec((size, width), lambda i, at: (at[0] * steps + i, 0))
    line = pl.BlockSpec((1, width), lambda i, at: (0, 0))
    return call_at(
        name,
        norm_back_kernel,
        at,
        (steps,),
        [half if x.shape[0] > rows else tile, half if base.shape[0] > rows else tile, tile, tile, line],
        (x, base, mine, theirs, gain),
        [(like(mine.shape, kind), tile) for kind in kinds] + [(like((1, width), jnp.float32), line)],
    )


def half_places(at_ref, rows):
    half = rows // 2
    return [pl.ds(pl.multiple_of(which * half, half), half) for which in (at_ref[0], 1 - at_ref[0])]


def project_kernel(x_ref, weight_ref, out_ref):
    out_ref[...] = matmul_low(x_ref[...], weight_ref[...]).astype(out_ref.dtype)


def project(name, x, weight, start, width, kind):
    rows, depth = x.shape
    size = math.gcd(256, width)
    return call(
        name,
        project_kernel,
        (width // size,),
        [
            pl.BlockSpec((rows, depth), lambda j: (0, 0)),
            pl.BlockSpec((depth, size), lambda j: (0, start // size + j)),
        ],
        (x, weight),
        [(like((rows, width), kind), pl.BlockSpec((rows, size), lambda j: (0, j)))],
    )[0]


def expand_kernel(at_ref, mine_ref, other_ref, gate_ref, up_ref, dact_ref, act_ref, dgate_ref, dup_ref):
    for place, x_ref in zip(half_places(at_ref, dact_ref.shape[0]), (mine_ref, other_ref), strict=True):
        gate = matmul_low(x_ref[...], gate_ref[...])
        up = matmul_low(x_ref[...], up_ref[...])
        dact = dact_ref[place, :]
        logistic = jax.nn.sigmoid(gate)
        silu = gate * logistic
        act_ref[place, :] = narrow(silu * up)
        dgate_ref[place, :] = narrow(dact * up * (logistic * (1.0 + gate * (1.0 - logistic))))
        dup_ref[place, :] = narrow(dact * silu)


def expand(at, mine, other, weight, dact):
    half, depth = mine.shape
    rows, width = dact.shape
    size = min(256, width)
    steps = width // size
    tile = pl.BlockSpec((rows, size), lambda j, at: (0, j))
    return call_at(
        "expand",
        expand_kernel,
        at,
        (steps,),
        [
            pl.BlockSpec((half, depth), lambda j, at: (0, 0)),
            pl.BlockSpec((half, depth), lambda j, at: (0, 0)),
            pl.BlockSpec((depth, size), lambda j, at: (0, j)),
            pl.BlockSpec((depth, size), lambda j, at: (0, steps + j)),
            tile,
        ],
        (mine, other, weight, weight, dact),
        [(like((rows, width), jnp.bfloat16), tile)] * 3,
    )


def gated_back_kernel(
    at_ref, mine_ref, other_ref, weight_ref, gate_ref, y_ref, dy_ref, dgate_ref
):
    for place, x_ref in zip(half_places(at_ref, gate_ref.shape[0]), (mine_ref, other_ref), strict=True):
        dgated = times_back(x_ref[...], weight_ref[...])
        gate = gate_ref[place, :]
        logistic = jax.nn.sigmoid(gate)
        dy_ref[place, :] = narrow(dgated * (gate * logistic))
        dgate_ref[place, :] = narrow(
            dgated * y_ref[place, :] * (logistic * (1.0 + gate * (1.0 - logistic)))
        )


def gated_back(at, mine, other, weight, gate, y):
    half, depth = mine.shape
    rows, width = gate.shape
    size = min(256, width)
    tile = pl.BlockSpec((rows, size), lambda j, at: (0, j))
    whole = pl.BlockSpec((half, depth), lambda j, at: (0, 0))
    return call_at(
        "gated_back",
        gated_back_kernel,
        at,
        (width // size,),
        [whole, whole, pl.BlockSpec((size, depth), lambda j, at: (j, 0)), tile, tile],
        (mine, other, weight, gate, y),
        [(like((rows, width), jnp.bfloat16), tile)] * 2,
    )


def rows_back_kernel(at_ref, mine_ref, other_ref, weight_ref, out_ref):
    for place, x_ref in zip(half_places(at_ref, out_ref.shape[0]), (mine_ref, other_ref), strict=True):
        out_ref[place, :] = narrow(times_back(x_ref[...], weight_ref[...]))


def rows_back(at, mine, other, weight):
    half, depth = mine.shape
    width = weight.shape[0]
    size = min(256, width)
    whole = pl.BlockSpec((half, depth), lambda j, at: (0, 0))
    return call_at(
        "attended_back",
        rows_back_kernel,
        at,
        (width // size,),
        [whole, whole, pl.BlockSpec((size, depth), lambda j, at: (j, 0))],
        (mine, other, weight),
        [(like((2 * half, width), jnp.bfloat16), pl.BlockSpec((2 * half, size), lambda j, at: (0, j)))],
    )[0]


def share_kernel(at_ref, *refs, count, back, added):
    total = jnp.zeros(refs[-1].shape, jnp.float32)
    for former, latter in zip(refs[:count], refs[count : 2 * count], strict=True):
        product = times_back if back else matmul_low
        total = total + product(former[...], latter[...])
    if added:
        total = total + wide(refs[2 * count][...])
    refs[-1][...] = narrow(total)


def half_share(name, at, terms, back, added=None):
    rows = terms[0][0].shape[0] // 2
    width = terms[0][1].shape[0 if back else 1]
    size = min(1024, width)
    specs = [pl.BlockSpec((rows, former.shape[1]), lambda j, at: (at[0], 0)) for former, _, _ in terms]
    for former, latter, columns in terms:
        if back:
            specs.append(pl.BlockSpec((size, former.shape[1]), lambda j, at, c=columns: (j, c)))
        else:
            specs.append(pl.BlockSpec((former.shape[1], size), lambda j, at: (0, j)))
    args = [term[0] for term in terms] + [term[1] for term in terms]
    tile = pl.BlockSpec((rows, size), lambda j, at: (0, j))
    if added is not None:
        specs.append(tile)
        args.append(added)
    kernel = partial(share_kernel, count=len(terms), back=back, added=added is not None)
    return call_at(
        name, kernel, at, (width // size,), specs, args, [(like((rows, width), jnp.bfloat16), tile)]
    )[0]


def weight_kernel(at_ref, *refs, ranks, count, added):
    out_ref = refs[-1]
    firsts = [ref[...].T for ref in refs[: 2 * ranks]]
    seconds = refs[2 * ranks : 2 * ranks + ranks * count]
    places = half_places(at_ref, seconds[0].shape[0])
    at = 0
    for index in range(count):
        width = seconds[index].shape[1]
        for start in range(0, width, 512):
            stop = min(width, start + 512)
            total = None
            for rank in range(ranks):
                ref = seconds[count * rank + index]
                for which in range(2):
                    part = matmul_low(firsts[2 * rank + which], ref[places[which], start:stop])
                    total = part if total is None else total + part
            if added:
                total = total + wide(refs[-2][:, at + start : at + stop])
            out_ref[:, at + start : at + stop] = narrow(total)
        at = at + width


class WeightGrad:
    def __init__(self, name, own, others, seconds, arrived, core, ctx_rank):
        self.name = name
        whole = own[0].shape[1] if isinstance(own, tuple) else own.shape[1]
        self.ranks = len(others) + 1
        self.size = whole // self.ranks // 4
        self.own, self.others = (own, others)
        self.groups = [list(seconds)] + [list(group) for group in arrived]
        self.width = sum(part.shape[1] for part in seconds)
        dp_rank = lax.axis_index("dp")
        near = ctx_rank ^ 1
        self.given = jnp.stack([core, dp_rank, near ^ 2, near]).astype(jnp.int32)
        self.held = jnp.stack([core, dp_rank, ctx_rank ^ 2, ctx_rank]).astype(jnp.int32)

    def part(self, suffix, at, added=None, whole=False):
        size = self.size
        half = self.groups[0][0].shape[0] // 2
        steps = 4 if whole else 2
        own = list(self.own) if isinstance(self.own, tuple) else [self.own]
        others = [array for pair in self.others for array in pair]
        if size % 128 and whole:
            steps, size = (1, 4 * size)
            own = [cut(array, at[1], size, 1) for array in own]
        elif size % 128:
            steps, size = (1, 2 * size)
            own = [self.columns(array, 4 * at[1] + at[2], 4 * at[1] + at[3]) for array in own]
            others = [self.columns(array, at[2], at[3]) for array in others]

        def first_spec(row, from_dp):
            def place(m, at):
                if steps == 1:
                    return (row(at), m)
                return (row(at), (m if whole else at[2 + m]) + (4 * at[1] if from_dp else 0))

            return pl.BlockSpec((half, size), place)

        if len(own) == 2:
            specs = 2 * [first_spec(lambda at: 0, True)]
        else:
            specs = [first_spec(lambda at: at[0], True), first_spec(lambda at: 1 - at[0], True)]
            own = 2 * own
        specs += [first_spec(lambda at: 0, False) for _ in others]
        args = own + others
        for group in self.groups:
            for array in group:
                specs.append(pl.BlockSpec(array.shape, lambda m, at: (0, 0)))
                args.append(array)
        tile = pl.BlockSpec((size, self.width), lambda m, at: (m, 0))
        if added is not None:
            specs.append(tile)
            args.append(added)
        kernel = partial(
            weight_kernel, ranks=self.ranks, count=len(self.groups[0]), added=added is not None
        )
        out = like((steps * size, self.width), jnp.bfloat16)
        return call_at(self.name + suffix, kernel, at, (steps,), specs, args, [(out, tile)])[0]

    def columns(self, array, *blocks):
        return jnp.concatenate([cut(array, block, self.size, 1) for block in blocks], axis=1)

    def whole(self, *awaited):
        self.made = self.part("_all", after(self.given, *awaited), whole=True)
        self.total = lax.psum_scatter(self.made, "ctx", scatter_dimension=0, tiled=True)
        return self.made

    def start(self, *awaited):
        self.sent = self.part("_given", after(self.given, *awaited))
        self.near = ctx_partner(self.sent, 1)
        return self.sent

    def turn(self, *awaited):
        self.kept = self.part("_held", after(self.held, *awaited), self.near)
        self.far = ctx_partner(self.kept[: self.size], 2)
        return self.kept

    def end(self):
        return wide(self.kept[self.size :]) + wide(self.far)


def body(
    hidden,
    cotangent,
    norm1_gain,
    ssm_in,
    ssm_bc,
    ssm_dt,
    dt_bias,
    a_log,
    d_skip,
    ssm_out,
    attn_q,
    attn_kv,
    attn_out,
    norm2_gain,
    mlp_gate_up,
    mlp_down,
):
    ctx_rank = lax.axis_index("ctx")
    ctx_count = lax.axis_size("ctx")
    tensor_rank = lax.axis_index("tensor")
    core = tensor_rank % 2
    chip = tensor_rank // 2
    hidden_rows = hidden[0]
    grad_low = cotangent[0]
    tokens, model_width = hidden_rows.shape
    half = tokens // 2
    inner_local = ssm_in.shape[2]
    heads_local = ssm_dt.shape[1]
    head_width = inner_local // heads_local
    head_pairs = heads_local // 2
    state_width = ssm_bc.shape[2]
    bc_share = 2 * state_width // 4
    heads_query = attn_q.shape[1] // AHEAD_DIM
    ff_local = mlp_down.shape[0]
    here = core.astype(jnp.int32)[None]
    there = 1 - here
    gain_one = norm1_gain[None]
    gain_two = norm2_gain[None]

    input_one = normed(hidden_rows, gain_one)
    in_matrix = ssm_in.reshape(model_width, 2 * inner_local)
    bc_matrix = ssm_bc.reshape(model_width, 2 * state_width)
    source_rows = project("project_u", input_one, in_matrix, inner_local, inner_local, jnp.bfloat16)
    bc_rows = matmul_low(input_one, bc_matrix).astype(jnp.bfloat16)
    write_rows = bc_rows[:, :state_width]
    read_rows = bc_rows[:, state_width:]
    dt_pre = lax.dot_general(
        ssm_dt, input_one, (((0,), (1,)), ((), ())), preferred_element_type=jnp.float32
    ) + dt_bias[:, None]
    dt_rows = jax.nn.softplus(dt_pre)
    decay_rate = -jnp.exp(a_log)
    running = jnp.cumsum(dt_rows * decay_rate[:, None], axis=1)

    def by_head(value):
        return jnp.broadcast_to(value[:, None], (heads_local, tokens))

    small_rows = jnp.stack([running, dt_rows, by_head(d_skip), by_head(decay_rate)], axis=1)
    small_rows = small_rows.reshape(head_pairs, 2, 4, tokens).transpose(0, 2, 1, 3)
    small_rows = small_rows.reshape(head_pairs, 8, tokens)
    scan = Scan(tokens, inner_local, state_width)
    own_state = scan.own_state(source_rows, small_rows, write_rows, True)

    one_late = after(input_one, own_state)
    kv_pair = cut(attn_kv, chip, AHEAD_DIM, 2)
    key_value = matmul_low(one_late, kv_pair.reshape(model_width, 2 * AHEAD_DIM)).astype(jnp.bfloat16)
    kv_sent = cut(key_value, core, AHEAD_DIM, 1)
    kv_got = [kv_sent] + [moved(kv_sent, "ctx", shift) for shift in range(1, ctx_count)]
    cot_sent = send_columns(cut(after(grad_low, own_state), core, half, 0))
    one_sent = send_columns(cut(one_late, core, half, 0))
    queries = matmul_low(one_late, attn_q).astype(jnp.bfloat16)
    gate_ssm = project("project_z", one_late, in_matrix, 0, inner_local, jnp.float32)
    attend = Attend(tokens, ctx_count * tokens, heads_query)
    rank = ctx_rank.astype(jnp.int32)[None]
    kept = {}

    def fill_within(sent):
        kept["within"] = scan.within(source_rows, after(small_rows, own_state), write_rows, read_rows)
        return (kept["within"], gate_ssm, queries, cot_sent)

    def fill_attend(sent):
        mine = jnp.concatenate(kv_got, axis=0)
        other = partner(mine, CORE)
        kept["key"] = jnp.where(core == 0, mine, other)
        kept["value"] = jnp.where(core == 0, other, mine)
        kept["attended"], kept["log"] = attend.forward(
            after(rank, sent), queries, kept["key"], kept["value"]
        )
        kept["attended_sent"] = send_rows(kept["attended"])
        return (kept["attended"], one_sent)

    def fill_act(sent):
        kept["act"] = times_back(after(grad_low, sent), mlp_down)
        return (kept["act"],)

    entering = chained(own_state, running[:, -1], True, [fill_within, fill_attend, fill_act])
    key_rows, value_rows, attended = (kept["key"], kept["value"], kept["attended"])
    ssm_values, gated_rows = scan.carried(kept["within"], gate_ssm, small_rows, read_rows, entering)
    outs_sent = [
        [gated, att] for gated, att in zip(send_rows(gated_rows), kept["attended_sent"], strict=True)
    ]

    terms = [(gated_rows, ssm_out, 0), (attended, attn_out, 0)]
    given = partner(half_share("mix_other", there, terms, False), CORE)
    mix_mine = half_share("mix_own", here, terms, False, given)
    mix_theirs = partner(mix_mine, CHIP)
    gu_matrix = after(mlp_gate_up, mix_mine).reshape(model_width, 2 * ff_local)
    cot_columns = both_halves([after(part, mix_mine) for part in cot_sent])
    one_columns = both_halves([after(part, mix_mine) for part in one_sent])
    kv_columns = lax.dynamic_index_in_dim(after(kv_pair, mix_mine), core, 1, keepdims=False)
    pad = -heads_local % AHEAD_DIM
    weight_small = jnp.concatenate(
        [
            kv_columns,
            cut(bc_matrix, 2 * core + chip, bc_share, 1),
            jnp.pad(ssm_dt, ((0, 0), (0, pad))),
        ],
        axis=1,
    )
    mix_theirs = after(mix_theirs, gu_matrix, cot_columns, one_columns, weight_small, outs_sent)
    middle, two_mine, mix_squares = middle_norm(here, hidden_rows, mix_mine, mix_theirs, gain_two)

    two_other = partner(two_mine, CORE)
    activated, grad_gate, grad_up = expand(here, two_mine, two_other, gu_matrix, kept["act"])
    act_sent = send_rows(activated)
    two_sent = send_columns(two_mine)
    gate_sent = send_rows(grad_gate)
    up_sent = send_rows(grad_up)
    terms = [(grad_gate, gu_matrix, 0), (grad_up, gu_matrix, 1)]
    given = partner(half_share("two_other", there, terms, True), CORE)
    two_back = half_share("two_own", here, terms, True, given)
    two_theirs = partner(two_back, CHIP)
    down = WeightGrad(
        "grad_down", grad_low, cot_columns, [activated], [[part] for part in act_sent], core, ctx_rank
    )
    two_theirs = after(two_theirs, act_sent, two_sent)
    grad_middle, mix_grad_mine, gain_two_sum = norm_grad(
        "norm_two_back", here, middle, grad_low, two_back, two_theirs, gain_two, (jnp.float32, jnp.bfloat16)
    )

    mix_grad_other = partner(mix_grad_mine, CORE)
    mix_sent = send_columns(mix_grad_mine)
    down.whole(mix_grad_mine)
    grad_values, grad_gate_ssm = gated_back(
        after(here, down.made), mix_grad_mine, mix_grad_other, ssm_out, gate_ssm, ssm_values
    )
    own_grad = scan.own_state(grad_values, small_rows, read_rows, False)
    z_sent = send_rows(grad_gate_ssm)
    two_pair = (two_mine, two_other)
    two_columns = both_halves([after(part, mix_grad_mine) for part in two_sent])
    gate = WeightGrad(
        "grad_gate", two_pair, two_columns, [grad_gate], [[part] for part in gate_sent], core, ctx_rank
    )
    up = WeightGrad(
        "grad_up", two_pair, two_columns, [grad_up], [[part] for part in up_sent], core, ctx_rank
    )
    outs = WeightGrad(
        "grad_outs",
        (mix_grad_mine, mix_grad_other),
        both_halves(mix_sent),
        [gated_rows, attended],
        outs_sent,
        core,
        ctx_rank,
    )

    def fill_attend_back(sent):
        grad_attended = rows_back(after(here, sent), mix_grad_mine, mix_grad_other, attn_out)
        kept["grads"] = attend.back(rank, queries, grad_attended, kept["log"], key_rows, value_rows)
        kept["query_sent"] = send_rows(kept["grads"][0])
        return (kept["grads"][0], gate_sent, two_columns)

    def fill_scan_back(sent):
        gate.whole(sent)
        kept["scan"] = scan.within_back(
            source_rows, after(grad_values, gate.made), small_rows, write_rows, read_rows
        )
        return (kept["scan"][0], up_sent)

    def fill_weights(sent):
        up.whole(sent)
        return (up.made,)

    leaving = chained(own_grad, running[:, -1], False, [fill_attend_back, fill_scan_back, fill_weights])
    leaving = after(leaving, down.total)
    grad_query, grad_key, grad_value = kept["grads"]
    own_part = jnp.where(core == 0, grad_key, grad_value)
    given = partner(after(jnp.where(core == 0, grad_value, grad_key).astype(jnp.bfloat16), leaving), CORE)
    grad_written, scan_sums, grad_b, grad_c = kept["scan"]
    grad_source, steps, grad_b, grad_c = scan.carried_back(
        source_rows, grad_values, small_rows, scan_sums, grad_written,
        write_rows, read_rows, entering, leaving, grad_b, grad_c,
    )
    source_sent = send_rows(grad_source)
    paired = (own_part + given.astype(jnp.float32)).reshape(ctx_count, tokens, AHEAD_DIM)
    kv_sent_back = [
        moved(paired[shift].astype(jnp.bfloat16), "ctx", -shift) for shift in range(1, ctx_count)
    ]
    grad_bc = jnp.concatenate([grad_b, grad_c], axis=1)
    bc_sent = partner(cut(grad_bc, 1 - core, 2 * bc_share, 1).astype(jnp.bfloat16), CORE)
    bc_mine = cut(grad_bc, core, 2 * bc_share, 1) + bc_sent.astype(jnp.float32)
    bc_given = partner(cut(bc_mine, 1 - chip, bc_share, 1).astype(jnp.bfloat16), CHIP)
    grad_bc_low = (cut(bc_mine, chip, bc_share, 1) + bc_given.astype(jnp.float32)).astype(jnp.bfloat16)
    kv_sum = paired[0]
    for part in kv_sent_back:
        kv_sum = kv_sum + part.astype(jnp.float32)
    grad_kv_low = kv_sum.astype(jnp.bfloat16)
    first = WeightGrad(
        "grad_first",
        input_one,
        one_columns,
        [grad_gate_ssm, grad_query],
        [[gate, query] for gate, query in zip(z_sent, kept["query_sent"], strict=True)],
        core,
        ctx_rank,
    )
    outs.whole(grad_source)
    first.whole(outs.made)

    grad_dt_pre = steps[:, 0:2].reshape(heads_local, tokens) * jax.nn.sigmoid(dt_pre)
    flow_rows = steps[:, 2:4].reshape(heads_local, tokens)
    grad_dt_bias = jnp.sum(grad_dt_pre, axis=1)
    grad_a_log = decay_rate * jnp.sum(dt_rows * flow_rows, axis=1)
    grad_d_skip = jnp.sum(scan_sums[:, 4, : 2 * head_width].reshape(heads_local, head_width), axis=1)
    grad_dt_low = jnp.pad(grad_dt_pre.astype(jnp.bfloat16).T, ((0, 0), (0, pad)))
    grad_small = jnp.concatenate([grad_kv_low, grad_bc_low, grad_dt_low], axis=1)
    small_sent = send_rows(grad_small)
    terms = [
        (grad_gate_ssm, in_matrix, 0),
        (grad_source, in_matrix, 1),
        (grad_query, attn_q, 0),
        (grad_small, weight_small, 0),
    ]
    given = partner(half_share("one_other", after(there, first.made), terms, True), CORE)
    one_back = half_share("one_own", after(here, source_sent), terms, True, given)
    one_theirs = partner(one_back, CHIP)
    source = WeightGrad(
        "grad_source", input_one, one_columns, [grad_source], [[part] for part in source_sent], core, ctx_rank
    )
    little = WeightGrad(
        "grad_little", input_one, one_columns, [grad_small], [[part] for part in small_sent], core, ctx_rank
    )
    little.start(one_back)
    source.start(little.sent)
    terms = [(activated, mlp_down, 0)]
    given = partner(half_share("mlp_other", after(there, source.sent), terms, False), CORE)
    mlp_mine = half_share("mlp_own", here, terms, False, given)
    mlp_theirs = partner(mlp_mine, CHIP)
    one_theirs = after(one_theirs, mlp_mine, gate.total)
    hidden_mine, gain_one_sum = norm_grad(
        "norm_one_back", here, hidden_rows, grad_middle, one_back, one_theirs, gain_one, (jnp.bfloat16,)
    )
    grad_hidden = gather_rows(hidden_mine, core)
    little.turn(hidden_mine)
    source.turn(little.kept)
    mlp_total = mlp_mine.astype(jnp.float32) + after(mlp_theirs, source.kept).astype(jnp.float32)
    block_out = middle + mlp_total
    output = gather_rows(block_out.astype(jnp.bfloat16), core)

    grad_little = little.end()
    held = narrow(grad_little[:, : AHEAD_DIM + bc_share])
    pieces = jnp.stack([held] + [partner(held, stride) for stride in range(1, 4)])

    def of_rank(rank):
        return lax.dynamic_index_in_dim(pieces, tensor_rank ^ rank, 0, keepdims=False).astype(jnp.float32)

    by_rank = [of_rank(rank) for rank in range(4)]
    kv_rows = held.shape[0] // 4
    kv_parts = [cut(part[:, :AHEAD_DIM], tensor_rank, kv_rows, 0) for part in by_rank]
    grad_attn_kv = jnp.stack(
        [jnp.concatenate([kv_parts[kind], kv_parts[2 + kind]], axis=1) for kind in range(2)], axis=1
    )
    grad_ssm_bc = jnp.concatenate(
        [by_rank[2 * (place % 2) + place // 2][:, AHEAD_DIM:] for place in range(4)], axis=1
    ).reshape(-1, 2, state_width)
    grad_ssm_dt = grad_little[:, AHEAD_DIM + bc_share : AHEAD_DIM + bc_share + heads_local]

    squares = jnp.stack([jnp.sum(mix_squares), jnp.sum(mlp_total * mlp_total), jnp.sum(block_out * block_out)])
    halves = jnp.concatenate([gain_one_sum[0], gain_two_sum[0], squares])
    halves = halves + partner(halves, CORE)
    sums = jnp.concatenate([halves, grad_dt_bias, grad_a_log, grad_d_skip])
    sums = jnp.pad(sums, (0, -sums.shape[0] % 1024)).reshape(-1, 128)
    sums = all_sum(all_sum(sums, "dp"), "ctx").reshape(-1)
    place = lax.axis_index("dp") * ctx_count + ctx_rank
    share = model_width // (lax.axis_size("dp") * ctx_count)
    small = sums[2 * model_width :]
    counted = tokens * model_width * lax.axis_size("dp") * ctx_count
    grad_down = wide(down.total)
    grad_gate_up = jnp.stack([wide(gate.total), wide(after(up.total, grad_down))], axis=1)
    grad_outs = wide(after(outs.total, grad_gate_up))
    grad_first = wide(after(first.total, grad_outs))
    branch_rms = jnp.sqrt(small[:3] / counted)
    return (
        output[None],
        grad_hidden[None],
        cut(sums[:model_width], place, share, 0),
        jnp.stack([grad_first[:, :inner_local], source.end()], axis=1),
        grad_ssm_bc,
        grad_ssm_dt,
        small[3 : 3 + heads_local],
        small[3 + heads_local : 3 + 2 * heads_local],
        small[3 + 2 * heads_local : 3 + 3 * heads_local],
        grad_outs[:, :inner_local].T,
        grad_first[:, inner_local:],
        grad_attn_kv,
        grad_outs[:, inner_local:].T,
        cut(sums[model_width : 2 * model_width], place, share, 0),
        grad_gate_up,
        grad_down.T,
        branch_rms,
    )


def solution(mesh):
    return jax.shard_map(
        body,
        mesh=mesh,
        in_specs=(
            P("dp", "ctx", None),
            P("dp", "ctx", None),
            P(),
            P(None, None, "tensor"),
            P(),
            P(None, "tensor"),
            P("tensor"),
            P("tensor"),
            P("tensor"),
            P("tensor", None),
            P(None, "tensor"),
            P(),
            P("tensor", None),
            P(),
            P(None, None, "tensor"),
            P("tensor", None),
        ),
        out_specs=(
            P("dp", "ctx", None),
            P("dp", "ctx", None),
            P(("dp", "ctx")),
            P(("dp", "ctx"), None, "tensor"),
            P(("dp", "ctx"), None, None),
            P(("dp", "ctx"), "tensor"),
            P("tensor"),
            P("tensor"),
            P("tensor"),
            P("tensor", ("dp", "ctx")),
            P(("dp", "ctx"), "tensor"),
            P(("dp", "ctx", "tensor"), None, None),
            P("tensor", ("dp", "ctx")),
            P(("dp", "ctx")),
            P(("dp", "ctx"), None, "tensor"),
            P("tensor", ("dp", "ctx")),
            P(),
        ),
        check_vma=False,
    )
```

```python
from functools import partial
import math

import jax
import jax.numpy as jnp
from jax import lax
from jax.experimental import pallas as pl
from jax.experimental.pallas import tpu as pltpu
from jax.sharding import PartitionSpec as P

AHEAD_DIM = 128
SCAN_BLOCK = 256


EPSILON = 1e-05
NEG_FILL = -1e30
VMEM_GRANT = 28 * 1024 * 1024
WIDE_GRANT = 60 * 1024 * 1024

CORE, CHIP = (1, 2)


def partner(value, stride):
    return lax.ppermute(value, "tensor", [(rank, rank ^ stride) for rank in range(4)])


def shifted(value, axis, shift):
    count = lax.axis_size(axis)
    return lax.ppermute(value, axis, [(i, (i + shift) % count) for i in range(count)])


def moved(value, axis, shift):
    count = lax.axis_size(axis)
    pairs = [(i, i + shift) for i in range(count) if 0 <= i + shift < count]
    return lax.ppermute(value, axis, pairs)


def after(value, *others):
    return lax.optimization_barrier((value,) + others)[0]


def cut(value, index, size, axis):
    return lax.dynamic_slice_in_dim(value, index * size, size, axis)


def paired_rows(mine, other, core):
    first = jnp.where(core == 0, mine, other)
    second = jnp.where(core == 0, other, mine)
    return jnp.concatenate([first, second], axis=0)


def gather_rows(mine, core):
    return paired_rows(mine, partner(mine, CORE), core)


def send_columns(rows):
    count, mine = (lax.axis_size("dp"), lax.axis_index("dp"))
    share = rows.shape[1] // count
    return [
        shifted(cut(rows, (mine + shift) % count, share, 1), "dp", shift) for shift in range(1, count)
    ]


def both_halves(arrived):
    return [(part, partner(part, CORE)) for part in arrived]


def send_rows(value):
    return [shifted(value, "dp", shift) for shift in range(1, lax.axis_size("dp"))]


def all_sum(value, axis):
    count, mine = (lax.axis_size(axis), lax.axis_index(axis))
    pieces = jnp.stack([value] + [shifted(value, axis, shift) for shift in range(1, count)])
    total = jnp.zeros_like(value)
    for rank in range(count):
        total = total + lax.dynamic_index_in_dim(pieces, (mine - rank) % count, 0, keepdims=False)
    return total


def chained(state, log_decay, forward, fillers):
    count = lax.axis_size("ctx")
    decay = jnp.exp(log_decay)[:, None, None]
    per_head = (decay.shape[0], state.shape[0] // decay.shape[0], state.shape[1])
    own = state.reshape(per_head)
    sent = state
    entering = None
    for step in range(1, count):
        pair = (step - 1, step) if forward else (count - step, count - step - 1)
        arrived = lax.ppermute(sent, "ctx", [pair])
        if step <= len(fillers):
            arrived = after(arrived, *fillers[step - 1](sent))
        entering = arrived if entering is None else entering + arrived
        if step < count - 1:
            total = own.astype(jnp.float32) + decay * arrived.reshape(per_head).astype(jnp.float32)
            sent = total.astype(jnp.bfloat16).reshape(state.shape)
    return entering


def matmul_low(former, latter):
    return jnp.dot(former, latter, preferred_element_type=jnp.float32)


def inner_rows(former, latter):
    return lax.dot_general(
        former, latter, (((0,), (0,)), ((), ())), preferred_element_type=jnp.float32
    )


def times_back(former, latter):
    return lax.dot_general(
        former, latter, (((1,), (1,)), ((), ())), preferred_element_type=jnp.float32
    )


def split_lanes(first, second, shape):
    lane = lax.broadcasted_iota(jnp.int32, shape, 1)
    return jnp.where(lane < shape[1] // 2, first, second)


def wide(values):
    return values.astype(jnp.float32)


def narrow(values):
    return values.astype(jnp.bfloat16)


def in_two(values):
    high = narrow(values)
    return (high, narrow(values - wide(high)))


def spread(rows, shape):
    rows = jnp.concatenate([rows, jnp.zeros((6, rows.shape[1]), jnp.float32)], axis=0)
    place = lax.broadcasted_iota(jnp.int32, (8, shape[1]), 0)
    lane = lax.broadcasted_iota(jnp.int32, (8, shape[1]), 1)
    chosen = narrow(jnp.where(place == lane // (shape[1] // 2), 1.0, 0.0))
    high, low = in_two(rows.T)
    return matmul_low(high, chosen) + matmul_low(low, chosen)


def lane_sums(values):
    place = lax.broadcasted_iota(jnp.int32, (8, values.shape[1]), 0)
    lane = lax.broadcasted_iota(jnp.int32, (8, values.shape[1]), 1)
    chosen = narrow(jnp.where(place == lane // (values.shape[1] // 2), 1.0, 0.0))
    high, low = in_two(values)
    return times_back(chosen, high) + times_back(chosen, low)


def lanes_of(ref):
    return [slice(at, at + 128) for at in range(0, ref.shape[1], 128)]


def state_kernel(u_ref, small_ref, b_ref, state_ref, *, to_end):
    for pair, lanes in enumerate(lanes_of(u_ref)):
        rows = small_ref[pair]
        if to_end:
            last = rows[0:2, rows.shape[1] - 1 :]
            weights = jnp.exp(last - rows[0:2]) * rows[2:4]
        else:
            weights = jnp.exp(rows[0:2])
        u = wide(u_ref[:, lanes])
        weighted = narrow(u * spread(weights, u.shape))
        state_ref[lanes, :] = narrow(inner_rows(weighted, b_ref[...]))


def scan_kernel(u_ref, small_ref, b_ref, c_ref, y_ref, cb_ref):
    size = SCAN_BLOCK
    count = u_ref.shape[0] // size
    block = [slice(i * size, (i + 1) * size) for i in range(count)]

    @pl.when(pl.program_id(0) == 0)
    def _():
        for i in range(count):
            for j in range(i + 1):
                cb_ref[block[i], block[j]] = times_back(c_ref[block[i], :], b_ref[block[j], :])

    lower = lax.broadcasted_iota(jnp.int32, (size, size), 0) >= lax.broadcasted_iota(
        jnp.int32, (size, size), 1
    )
    for pair, lanes in enumerate(lanes_of(u_ref)):
        rows = small_ref[pair]
        cols = rows.T
        for i in range(count):
            parts = []
            for h in range(2):
                total = jnp.zeros((size, 128), jnp.float32)
                for j in range(i + 1):
                    difference = cols[block[i], h : h + 1] - rows[h : h + 1, block[j]]
                    if i == j:
                        difference = jnp.where(lower, difference, NEG_FILL)
                    weights = cb_ref[block[i], block[j]] * rows[2 + h : 3 + h, block[j]]
                    mixing = narrow(jnp.exp(difference) * weights)
                    total = total + matmul_low(mixing, u_ref[block[j], lanes])
                parts.append(total)
            skip = split_lanes(cols[block[i], 4:5], cols[block[i], 5:6], parts[0].shape)
            values = split_lanes(*parts, parts[0].shape) + skip * wide(u_ref[block[i], lanes])
            y_ref[block[i], lanes] = values


def carry_kernel(y_ref, z_ref, small_ref, c_ref, state_ref, out_ref, gated_ref):
    for pair, lanes in enumerate(lanes_of(y_ref)):
        carried = times_back(c_ref[...], state_ref[lanes, :])
        decay = spread(jnp.exp(small_ref[pair][0:2]), carried.shape)
        values = y_ref[:, lanes] + carried * decay
        out_ref[:, lanes] = values
        gate = z_ref[:, lanes]
        gated_ref[:, lanes] = narrow(values * (gate * jax.nn.sigmoid(gate)))


def scan_back_kernel(u_ref, dy_ref, small_ref, b_ref, c_ref, dw_ref, sums_ref, db_ref, dc_ref, cb_ref, mix_ref):
    size = SCAN_BLOCK
    count = u_ref.shape[0] // size
    width = u_ref.shape[1]
    block = [slice(i * size, (i + 1) * size) for i in range(count)]

    @pl.when(pl.program_id(0) == 0)
    def _():
        mix_ref[...] = jnp.zeros_like(mix_ref)
        for i in range(count):
            for j in range(i, count):
                cb_ref[block[i], block[j]] = times_back(b_ref[block[i], :], c_ref[block[j], :])

    rows = small_ref[0]
    cols = rows.T
    upper = lax.broadcasted_iota(jnp.int32, (size, size), 0) <= lax.broadcasted_iota(
        jnp.int32, (size, size), 1
    )
    lane = lax.broadcasted_iota(jnp.int32, (size, width), 1)
    read_sums = [[jnp.zeros((1, size), jnp.float32) for _ in range(count)] for _ in range(2)]
    write_sums = [[], []]
    ones = jnp.ones((8, size), jnp.bfloat16)
    for i in range(count):
        parts = []
        for h in range(2):
            total = jnp.zeros((size, width), jnp.float32)
            write_sum = jnp.zeros((8, size), jnp.float32)
            step = cols[block[i], 2 + h : 3 + h]
            for j in range(i, count):
                difference = rows[h : h + 1, block[j]] - cols[block[i], h : h + 1]
                if i == j:
                    difference = jnp.where(upper, difference, NEG_FILL)
                decay = jnp.exp(difference)
                dy = dy_ref[block[j], :]
                dy_head = jnp.where((lane < width // 2) == (h == 0), dy, jnp.zeros_like(dy))
                product = decay * times_back(u_ref[block[i], :], dy_head)
                crossing = cb_ref[block[i], block[j]]
                total = total + matmul_low(narrow(decay * crossing), dy)
                weighted = product * step
                mix_ref[block[i], block[j]] += weighted
                high, low = in_two(product * crossing)
                write_sum = write_sum + times_back(ones, high) + times_back(ones, low)
                read_sums[h][j] = read_sums[h][j] + jnp.sum(weighted * crossing, axis=0, keepdims=True)
            parts.append(total)
            write_sums[h].append(write_sum)
        dw_ref[block[i], :] = split_lanes(*parts, parts[0].shape)
    writes = [jnp.concatenate(write_sums[h], axis=1)[0:1] for h in range(2)]
    skip = jnp.sum(wide(u_ref[...]) * wide(dy_ref[...]), axis=0, keepdims=True)
    skip = jnp.concatenate([skip, jnp.zeros((1, u_ref.shape[0] - width), jnp.float32)], axis=1)
    reads = [jnp.concatenate(read_sums[h], axis=1) for h in range(2)]
    sums_ref[0] = jnp.concatenate(reads + writes + [skip, jnp.zeros_like(skip)] + reads, axis=0)

    @pl.when(pl.program_id(0) == pl.num_programs(0) - 1)
    def _():
        for i in range(count):
            total = jnp.zeros((size, b_ref.shape[1]), jnp.float32)
            for j in range(i, count):
                total = total + matmul_low(narrow(mix_ref[block[i], block[j]]), c_ref[block[j], :])
            db_ref[block[i], :] = total
        for j in range(count):
            total = jnp.zeros((size, b_ref.shape[1]), jnp.float32)
            for i in range(j + 1):
                total = total + inner_rows(narrow(mix_ref[block[i], block[j]]), b_ref[block[i], :])
            dc_ref[block[j], :] = total


def carry_back_kernel(
    u_ref, dy_ref, small_ref, sums_ref, dw_ref, b_ref, c_ref, state_ref, grad_ref, db_in_ref, dc_in_ref,
    du_ref, steps_ref, db_ref, dc_ref,
):
    tokens = u_ref.shape[0]

    @pl.when(pl.program_id(0) == 0)
    def _():
        db_ref[...] = db_in_ref[...]
        dc_ref[...] = dc_in_ref[...]

    all_started, all_ended = ([], [])
    for pair, lanes in enumerate(lanes_of(u_ref)):
        rows = small_ref[pair]
        last = rows[0:2, tokens - 1 :]
        u = wide(u_ref[:, lanes])
        dy = wide(dy_ref[:, lanes])
        state = state_ref[lanes, :]
        grad = grad_ref[lanes, :]
        started = spread(jnp.exp(rows[0:2]), u.shape) * dy
        tail = spread(jnp.exp(last - rows[0:2]), u.shape)
        ended = tail * u
        step = spread(rows[2:4], u.shape)
        left = times_back(b_ref[...], grad)
        dw = dw_ref[:, lanes] + tail * left
        du_ref[:, lanes] = narrow(step * dw + spread(rows[4:6], u.shape) * dy)
        all_started.append(narrow(started))
        all_ended.append(narrow(ended * step))
        reads = lane_sums(started * times_back(c_ref[...], state))[0:2]
        writes = lane_sums(ended * left)[0:2]
        sums = sums_ref[pair]
        written = sums[2:4] + writes
        slope = sums[0:2] + reads - rows[2:4] * written
        products = jnp.sum(wide(state) * wide(grad), axis=1, keepdims=True)
        height = products.shape[0] // 2
        across = jnp.concatenate(
            [
                jnp.sum(products[:height], axis=0, keepdims=True),
                jnp.sum(products[height:], axis=0, keepdims=True),
            ],
            axis=0,
        ) * jnp.exp(last)
        across = across + jnp.sum(rows[2:4] * writes, axis=1, keepdims=True)
        held = jnp.concatenate([slope, jnp.zeros((6, tokens), jnp.float32)], axis=0)
        place = lax.broadcasted_iota(jnp.int32, held.shape, 1)
        reach = 1
        while reach < tokens:
            held = held + jnp.where(place < tokens - reach, pltpu.roll(held, tokens - reach, 1), 0.0)
            reach = 2 * reach
        flow = held[0:2] + across
        steps_ref[pair] = jnp.concatenate([written + rows[6:8] * flow, flow, held[2:6]], axis=0)
    dc_ref[...] += matmul_low(jnp.concatenate(all_started, axis=1), state_ref[...])
    db_ref[...] += matmul_low(jnp.concatenate(all_ended, axis=1), grad_ref[...])


def attend_scores(rank_ref, k_ref, q_ref, own, factor):
    scores = times_back(k_ref[...], q_ref[...]) * factor
    keys, queries = scores.shape
    row = lax.broadcasted_iota(jnp.int32, (own, queries), 0)
    column = lax.broadcasted_iota(jnp.int32, (own, queries), 1) + pl.program_id(1) * queries
    near = jnp.where(row <= column, scores[:own], NEG_FILL)
    if keys == own:
        return near
    far_row = lax.broadcasted_iota(jnp.int32, (keys - own, queries), 0)
    far = jnp.where(far_row < rank_ref[0] * own, scores[own:], NEG_FILL)
    return jnp.concatenate([near, far], axis=0)


def attend_kernel(rank_ref, q_ref, k_ref, v_ref, out_ref, log_ref, flat_ref, *, own, factor):
    @pl.when((pl.program_id(0) == 0) & (pl.program_id(1) == 0))
    def _():
        flat_ref[...] = v_ref[...].T

    scores = attend_scores(rank_ref, k_ref, q_ref, own, factor)
    maxima = jnp.max(scores, axis=0, keepdims=True)
    weights = jnp.exp(scores - maxima)
    totals = jnp.sum(weights, axis=0, keepdims=True)
    probability = narrow(weights * (1.0 / totals))
    out_ref[...] = narrow(matmul_low(flat_ref[...], probability).T)
    log_ref[0] = jnp.broadcast_to(maxima + jnp.log(totals), log_ref.shape[1:])


def attend_back_kernel(
    rank_ref, q_ref, do_ref, log_ref, k_ref, v_ref, dq_ref, dk_ref, dv_ref, flat_ref, *, own, factor
):
    @pl.when((pl.program_id(0) == 0) & (pl.program_id(1) == 0))
    def _():
        flat_ref[...] = k_ref[...].T
        dk_ref[...] = jnp.zeros_like(dk_ref)
        dv_ref[...] = jnp.zeros_like(dv_ref)

    scores = attend_scores(rank_ref, k_ref, q_ref, own, factor)
    probability = jnp.exp(scores - log_ref[0][0:1])
    dv_ref[...] += matmul_low(narrow(probability), do_ref[...])
    grad_prob = times_back(v_ref[...], do_ref[...])
    centre = jnp.sum(probability * grad_prob, axis=0, keepdims=True)
    grad_score = narrow(probability * (grad_prob - centre))
    dk_ref[...] += matmul_low(grad_score, q_ref[...]) * factor
    dq_ref[...] = narrow((matmul_low(flat_ref[...], grad_score) * factor).T)


def call(name, kernel, grid, specs, args, outs, scratch=(), grant=VMEM_GRANT):
    return pl.pallas_call(
        kernel,
        name=name,
        grid=grid,
        in_specs=specs,
        out_specs=[spec for _, spec in outs],
        out_shape=[out for out, _ in outs],
        scratch_shapes=list(scratch),
        cost_estimate=pl.CostEstimate(flops=1, bytes_accessed=1, transcendentals=0),
        compiler_params=pltpu.CompilerParams(vmem_limit_bytes=grant),
    )(*args)


def like(shape, kind):
    return jax.ShapeDtypeStruct(shape, kind)


class Scan:
    def __init__(self, tokens, inner, state):
        self.tokens, self.inner, self.state = (tokens, inner, state)
        self.pairs = inner // 128
        self.shared = pl.BlockSpec((tokens, state), lambda p: (0, 0))
        self.small_like = like((self.pairs, 8, tokens), jnp.float32)
        self.square = pltpu.VMEM((tokens, tokens), jnp.float32)

    def specs(self, group):
        group = math.gcd(group, self.pairs)
        return (
            (self.pairs // group,),
            pl.BlockSpec((self.tokens, 128 * group), lambda p: (0, p)),
            pl.BlockSpec((group, 8, self.tokens), lambda p: (p, 0, 0)),
            pl.BlockSpec((128 * group, self.state), lambda p: (p, 0)),
        )

    def rows_like(self, kind):
        return like((self.tokens, self.inner), kind)

    def own_state(self, u, small, b, to_end):
        grid, tile, row, states = self.specs(6)
        return call(
            "own_state",
            partial(state_kernel, to_end=to_end),
            grid,
            [tile, row, self.shared],
            (u, small, b),
            [(like((self.inner, self.state), jnp.bfloat16), states)],
        )[0]

    def within(self, u, small, b, c):
        grid, tile, row, states = self.specs(6)
        return call(
            "scan",
            scan_kernel,
            grid,
            [tile, row, self.shared, self.shared],
            (u, small, b, c),
            [(self.rows_like(jnp.float32), tile)],
            [self.square],
        )[0]

    def carried(self, y, z, small, c, state):
        grid, tile, row, states = self.specs(6)
        return call(
            "carry",
            carry_kernel,
            grid,
            [tile, tile, row, self.shared, states],
            (y, z, small, c, state),
            [(self.rows_like(jnp.float32), tile), (self.rows_like(jnp.bfloat16), tile)],
        )

    def within_back(self, u, dy, small, b, c):
        shared = like((self.tokens, self.state), jnp.float32)
        grid, tile, row, states = self.specs(1)
        return call(
            "scan_back",
            scan_back_kernel,
            grid,
            [tile, tile, row, self.shared, self.shared],
            (u, dy, small, b, c),
            [(self.rows_like(jnp.float32), tile), (self.small_like, row)] + 2 * [(shared, self.shared)],
            [self.square, self.square],
        )

    def carried_back(self, u, dy, small, sums, dw, b, c, state, grad, db, dc):
        shared = like((self.tokens, self.state), jnp.float32)
        grid, tile, row, states = self.specs(6)
        return call(
            "carry_back",
            carry_back_kernel,
            grid,
            [tile, tile, row, row, tile] + 2 * [self.shared] + 2 * [states] + 2 * [self.shared],
            (u, dy, small, sums, dw, b, c, state, grad, db, dc),
            [(self.rows_like(jnp.bfloat16), tile), (self.small_like, row)] + 2 * [(shared, self.shared)],
            grant=WIDE_GRANT,
        )


class Attend:
    def __init__(self, tokens, keys, heads):
        self.tokens, self.keys, self.heads = (tokens, keys, heads)
        size = min(256, tokens)
        self.grid = (heads, tokens // size)
        self.factor = 1.0 / math.sqrt(AHEAD_DIM)
        self.rank = pl.BlockSpec(memory_space=pltpu.SMEM)
        self.tile = pl.BlockSpec((size, AHEAD_DIM), lambda h, q: (q, h))
        self.log = pl.BlockSpec((1, 8, size), lambda h, q: (h, 0, q))
        self.whole = pl.BlockSpec((keys, AHEAD_DIM), lambda h, q: (0, 0))
        self.rows_like = like((tokens, heads * AHEAD_DIM), jnp.bfloat16)
        self.flat = pltpu.VMEM((AHEAD_DIM, keys), jnp.bfloat16)

    def forward(self, rank, q, k, v):
        return call(
            "attend",
            partial(attend_kernel, own=self.tokens, factor=self.factor),
            self.grid,
            [self.rank, self.tile, self.whole, self.whole],
            (rank, q, k, v),
            [(self.rows_like, self.tile), (like((self.heads, 8, self.tokens), jnp.float32), self.log)],
            [self.flat],
        )

    def back(self, rank, q, do, log, k, v):
        whole = like((self.keys, AHEAD_DIM), jnp.float32)
        return call(
            "attend_back",
            partial(attend_back_kernel, own=self.tokens, factor=self.factor),
            self.grid,
            [self.rank, self.tile, self.tile, self.log, self.whole, self.whole],
            (rank, q, do, log, k, v),
            [(self.rows_like, self.tile), (whole, self.whole), (whole, self.whole)],
            [self.flat],
        )


def call_at(name, kernel, scalars, grid, specs, args, outs, grant=VMEM_GRANT):
    return pl.pallas_call(
        kernel,
        name=name,
        grid_spec=pltpu.PrefetchScalarGridSpec(
            num_scalar_prefetch=1,
            grid=grid,
            in_specs=specs,
            out_specs=[spec for _, spec in outs],
        ),
        out_shape=[out for out, _ in outs],
        cost_estimate=pl.CostEstimate(flops=1, bytes_accessed=1, transcendentals=0),
        compiler_params=pltpu.CompilerParams(vmem_limit_bytes=grant),
    )(scalars, *args)


def mean_scale(values):
    return lax.rsqrt(jnp.mean(values * values, axis=-1, keepdims=True) + EPSILON)


def norm_kernel(x_ref, gain_ref, out_ref):
    x = wide(x_ref[...])
    out_ref[...] = narrow(x * mean_scale(x) * gain_ref[...])


def normed(x, gain):
    rows, width = x.shape
    size = min(128, rows)
    tile = pl.BlockSpec((size, width), lambda i: (i, 0))
    line = pl.BlockSpec((1, width), lambda i: (0, 0))
    return call(
        "norm_one", norm_kernel, (rows // size,), [tile, line], (x, gain), [(like(x.shape, x.dtype), tile)]
    )[0]


def middle_kernel(at_ref, x_ref, mine_ref, theirs_ref, gain_ref, middle_ref, out_ref, sum_ref):
    @pl.when(pl.program_id(0) == 0)
    def _():
        sum_ref[...] = jnp.zeros_like(sum_ref)

    mixed = wide(mine_ref[...]) + wide(theirs_ref[...])
    middle = wide(x_ref[...]) + mixed
    middle_ref[...] = middle
    out_ref[...] = narrow(middle * mean_scale(middle) * gain_ref[...])
    sum_ref[...] += jnp.sum(mixed * mixed, axis=0, keepdims=True)


def middle_norm(at, x, mine, theirs, gain):
    rows, width = mine.shape
    size = min(128, rows)
    steps = rows // size
    tile = pl.BlockSpec((size, width), lambda i, at: (i, 0))
    half = pl.BlockSpec((size, width), lambda i, at: (at[0] * steps + i, 0))
    line = pl.BlockSpec((1, width), lambda i, at: (0, 0))
    return call_at(
        "norm_two",
        middle_kernel,
        at,
        (steps,),
        [half, tile, tile, line],
        (x, mine, theirs, gain),
        [
            (like(mine.shape, jnp.float32), tile),
            (like(mine.shape, jnp.bfloat16), tile),
            (like((1, width), jnp.float32), line),
        ],
    )


def norm_back_kernel(at_ref, x_ref, base_ref, mine_ref, theirs_ref, gain_ref, *outs):
    sum_ref = outs[-1]

    @pl.when(pl.program_id(0) == 0)
    def _():
        sum_ref[...] = jnp.zeros_like(sum_ref)

    grad = wide(mine_ref[...]) + wide(theirs_ref[...])
    x = wide(x_ref[...])
    scale = mean_scale(x)
    weighted = grad * gain_ref[...]
    inner = jnp.mean(weighted * x, axis=-1, keepdims=True)
    total = wide(base_ref[...]) + (scale * weighted - x * (scale * scale * scale * inner))
    for out_ref in outs[:-1]:
        out_ref[...] = total.astype(out_ref.dtype)
    sum_ref[...] += jnp.sum(grad * x * scale, axis=0, keepdims=True)


def norm_grad(name, at, x, base, mine, theirs, gain, kinds):
    rows, width = mine.shape
    size = min(128, rows)
    steps = rows // size
    tile = pl.BlockSpec((size, width), lambda i, at: (i, 0))
    half = pl.BlockSpec((size, width), lambda i, at: (at[0] * steps + i, 0))
    line = pl.BlockSpec((1, width), lambda i, at: (0, 0))
    return call_at(
        name,
        norm_back_kernel,
        at,
        (steps,),
        [half if x.shape[0] > rows else tile, half if base.shape[0] > rows else tile, tile, tile, line],
        (x, base, mine, theirs, gain),
        [(like(mine.shape, kind), tile) for kind in kinds] + [(like((1, width), jnp.float32), line)],
    )


def half_places(at_ref, rows):
    half = rows // 2
    return [pl.ds(pl.multiple_of(which * half, half), half) for which in (at_ref[0], 1 - at_ref[0])]


def project_kernel(x_ref, weight_ref, out_ref):
    out_ref[...] = matmul_low(x_ref[...], weight_ref[...]).astype(out_ref.dtype)


def project(name, x, weight, start, width, kind):
    rows, depth = x.shape
    size = math.gcd(256, width)
    return call(
        name,
        project_kernel,
        (width // size,),
        [
            pl.BlockSpec((rows, depth), lambda j: (0, 0)),
            pl.BlockSpec((depth, size), lambda j: (0, start // size + j)),
        ],
        (x, weight),
        [(like((rows, width), kind), pl.BlockSpec((rows, size), lambda j: (0, j)))],
        grant=VMEM_GRANT,
    )[0]


def expand_kernel(at_ref, mine_ref, other_ref, gate_ref, up_ref, dact_ref, act_ref, dgate_ref, dup_ref):
    for place, x_ref in zip(half_places(at_ref, dact_ref.shape[0]), (mine_ref, other_ref), strict=True):
        gate = matmul_low(x_ref[...], gate_ref[...])
        up = matmul_low(x_ref[...], up_ref[...])
        dact = dact_ref[place, :]
        logistic = jax.nn.sigmoid(gate)
        silu = gate * logistic
        act_ref[place, :] = narrow(silu * up)
        dgate_ref[place, :] = narrow(dact * up * (logistic * (1.0 + gate * (1.0 - logistic))))
        dup_ref[place, :] = narrow(dact * silu)


def expand(at, mine, other, weight, dact):
    half, depth = mine.shape
    rows, width = dact.shape
    size = min(256, width)
    steps = width // size
    tile = pl.BlockSpec((rows, size), lambda j, at: (0, j))
    return call_at(
        "expand",
        expand_kernel,
        at,
        (steps,),
        [
            pl.BlockSpec((half, depth), lambda j, at: (0, 0)),
            pl.BlockSpec((half, depth), lambda j, at: (0, 0)),
            pl.BlockSpec((depth, size), lambda j, at: (0, j)),
            pl.BlockSpec((depth, size), lambda j, at: (0, steps + j)),
            tile,
        ],
        (mine, other, weight, weight, dact),
        [(like((rows, width), jnp.bfloat16), tile)] * 3,
        VMEM_GRANT,
    )


def gated_back_kernel(
    at_ref, mine_ref, other_ref, weight_ref, gate_ref, y_ref, dy_ref, dgate_ref
):
    for place, x_ref in zip(half_places(at_ref, gate_ref.shape[0]), (mine_ref, other_ref), strict=True):
        dgated = times_back(x_ref[...], weight_ref[...])
        gate = gate_ref[place, :]
        logistic = jax.nn.sigmoid(gate)
        dy_ref[place, :] = narrow(dgated * (gate * logistic))
        dgate_ref[place, :] = narrow(
            dgated * y_ref[place, :] * (logistic * (1.0 + gate * (1.0 - logistic)))
        )


def gated_back(at, mine, other, weight, gate, y):
    half, depth = mine.shape
    rows, width = gate.shape
    size = min(256, width)
    tile = pl.BlockSpec((rows, size), lambda j, at: (0, j))
    whole = pl.BlockSpec((half, depth), lambda j, at: (0, 0))
    return call_at(
        "gated_back",
        gated_back_kernel,
        at,
        (width // size,),
        [whole, whole, pl.BlockSpec((size, depth), lambda j, at: (j, 0)), tile, tile],
        (mine, other, weight, gate, y),
        [(like((rows, width), jnp.bfloat16), tile)] * 2,
        VMEM_GRANT,
    )


def rows_back_kernel(at_ref, mine_ref, other_ref, weight_ref, out_ref):
    for place, x_ref in zip(half_places(at_ref, out_ref.shape[0]), (mine_ref, other_ref), strict=True):
        out_ref[place, :] = narrow(times_back(x_ref[...], weight_ref[...]))


def rows_back(at, mine, other, weight):
    half, depth = mine.shape
    width = weight.shape[0]
    size = min(256, width)
    whole = pl.BlockSpec((half, depth), lambda j, at: (0, 0))
    return call_at(
        "attended_back",
        rows_back_kernel,
        at,
        (width // size,),
        [whole, whole, pl.BlockSpec((size, depth), lambda j, at: (j, 0))],
        (mine, other, weight),
        [(like((2 * half, width), jnp.bfloat16), pl.BlockSpec((2 * half, size), lambda j, at: (0, j)))],
    )[0]


def share_kernel(at_ref, *refs, count, back, added):
    total = jnp.zeros(refs[-1].shape, jnp.float32)
    for former, latter in zip(refs[:count], refs[count : 2 * count], strict=True):
        product = times_back if back else matmul_low
        total = total + product(former[...], latter[...])
    if added:
        total = total + wide(refs[2 * count][...])
    refs[-1][...] = narrow(total)


def half_share(name, at, terms, back, added=None):
    rows = terms[0][0].shape[0] // 2
    width = terms[0][1].shape[0 if back else 1]
    size = min(1024, width)
    specs = [pl.BlockSpec((rows, former.shape[1]), lambda j, at: (at[0], 0)) for former, _, _ in terms]
    for former, latter, columns in terms:
        if back:
            specs.append(pl.BlockSpec((size, former.shape[1]), lambda j, at, c=columns: (j, c)))
        else:
            specs.append(pl.BlockSpec((former.shape[1], size), lambda j, at: (0, j)))
    args = [term[0] for term in terms] + [term[1] for term in terms]
    tile = pl.BlockSpec((rows, size), lambda j, at: (0, j))
    if added is not None:
        specs.append(tile)
        args.append(added)
    kernel = partial(share_kernel, count=len(terms), back=back, added=added is not None)
    outs = [(like((rows, width), jnp.bfloat16), tile)]
    return call_at(name, kernel, at, (width // size,), specs, args, outs, VMEM_GRANT)[0]


def weight_kernel(at_ref, *refs, ranks, counts):
    out_ref = refs[-1]
    refs = list(refs[:-1])
    firsts = [[refs.pop(0)[...].T for _ in range(2 * ranks)] for _ in counts]
    at = 0
    for first, count in zip(firsts, counts, strict=True):
        seconds = [refs.pop(0) for _ in range(ranks * count)]
        places = half_places(at_ref, seconds[0].shape[0])
        for index in range(count):
            width = seconds[index].shape[1]
            for start in range(0, width, 512):
                stop = min(width, start + 512)
                total = None
                for rank in range(ranks):
                    ref = seconds[count * rank + index]
                    for which in range(2):
                        part = matmul_low(first[2 * rank + which], ref[places[which], start:stop])
                        total = part if total is None else total + part
                out_ref[:, at + start : at + stop] = narrow(total)
            at = at + width


def weight_grad(name, core, sets, *awaited):
    ranks = lax.axis_size("dp")
    dp_rank = lax.axis_index("dp")
    at = after(jnp.stack([core, dp_rank]).astype(jnp.int32), *awaited)
    specs, args, pieces, counts = ([], [], [], [])
    width = 0
    for own, others, seconds, arrived in sets:
        own = list(own) if isinstance(own, tuple) else [own]
        others = [array for pair in others for array in pair]
        groups = [list(seconds)] + [list(group) for group in arrived]
        half = seconds[0].shape[0] // 2
        share = own[0].shape[1] // ranks
        size = min(256, share)
        steps = share // size

        def spec(row, from_dp, half=half, size=size, steps=steps):
            return pl.BlockSpec(
                (half, size), lambda m, at: (row(at), m + (steps * at[1] if from_dp else 0))
            )

        if len(own) == 2:
            specs += 2 * [spec(lambda at: 0, True)]
        else:
            specs += [spec(lambda at: at[0], True), spec(lambda at: 1 - at[0], True)]
            own = 2 * own
        specs += [spec(lambda at: 0, False) for _ in others]
        args += own + others
        for group in groups:
            pieces += group
        counts.append(len(seconds))
        width = width + sum(part.shape[1] for part in seconds)
    for array in pieces:
        specs.append(pl.BlockSpec(array.shape, lambda m, at: (0, 0)))
        args.append(array)
    kernel = partial(weight_kernel, ranks=ranks, counts=tuple(counts))
    out = like((share, width), jnp.bfloat16)
    tile = pl.BlockSpec((size, width), lambda m, at: (m, 0))
    made = call_at(name, kernel, at, (steps,), specs, args, [(out, tile)])[0]
    return (made, lax.psum_scatter(made, "ctx", scatter_dimension=0, tiled=True))


def listed(*arrived):
    return [list(group) for group in zip(*arrived, strict=True)]


def body(
    hidden,
    cotangent,
    norm1_gain,
    ssm_in,
    ssm_bc,
    ssm_dt,
    dt_bias,
    a_log,
    d_skip,
    ssm_out,
    attn_q,
    attn_kv,
    attn_out,
    norm2_gain,
    mlp_gate_up,
    mlp_down,
):
    ctx_rank = lax.axis_index("ctx")
    ctx_count = lax.axis_size("ctx")
    tensor_rank = lax.axis_index("tensor")
    core = tensor_rank % 2
    chip = tensor_rank // 2
    hidden_rows = hidden[0]
    grad_low = cotangent[0]
    tokens, model_width = hidden_rows.shape
    half = tokens // 2
    inner_local = ssm_in.shape[2]
    heads_local = ssm_dt.shape[1]
    head_width = inner_local // heads_local
    head_pairs = heads_local // 2
    state_width = ssm_bc.shape[2]
    bc_share = 2 * state_width // 4
    heads_query = attn_q.shape[1] // AHEAD_DIM
    ff_local = mlp_down.shape[0]
    here = core.astype(jnp.int32)[None]
    there = 1 - here
    gain_one = norm1_gain[None]
    gain_two = norm2_gain[None]

    input_one = normed(hidden_rows, gain_one)
    in_matrix = ssm_in.reshape(model_width, 2 * inner_local)
    bc_matrix = ssm_bc.reshape(model_width, 2 * state_width)
    source_rows = project("project_u", input_one, in_matrix, inner_local, inner_local, jnp.bfloat16)
    bc_rows = matmul_low(input_one, bc_matrix).astype(jnp.bfloat16)
    write_rows = bc_rows[:, :state_width]
    read_rows = bc_rows[:, state_width:]
    dt_pre = lax.dot_general(
        ssm_dt, input_one, (((0,), (1,)), ((), ())), preferred_element_type=jnp.float32
    ) + dt_bias[:, None]
    dt_rows = jax.nn.softplus(dt_pre)
    decay_rate = -jnp.exp(a_log)
    running = jnp.cumsum(dt_rows * decay_rate[:, None], axis=1)

    def by_head(value):
        return jnp.broadcast_to(value[:, None], (heads_local, tokens))

    small_rows = jnp.stack([running, dt_rows, by_head(d_skip), by_head(decay_rate)], axis=1)
    small_rows = small_rows.reshape(head_pairs, 2, 4, tokens).transpose(0, 2, 1, 3)
    small_rows = small_rows.reshape(head_pairs, 8, tokens)
    scan = Scan(tokens, inner_local, state_width)
    own_state = scan.own_state(source_rows, small_rows, write_rows, True)

    one_late = after(input_one, own_state)
    kv_pair = cut(attn_kv, chip, AHEAD_DIM, 2)
    key_value = matmul_low(one_late, kv_pair.reshape(model_width, 2 * AHEAD_DIM)).astype(jnp.bfloat16)
    kv_sent = cut(key_value, core, AHEAD_DIM, 1)
    kv_got = [kv_sent] + [moved(kv_sent, "ctx", shift) for shift in range(1, ctx_count)]
    cot_sent = send_columns(cut(after(grad_low, own_state), core, half, 0))
    one_sent = send_columns(cut(one_late, core, half, 0))
    queries = matmul_low(one_late, attn_q).astype(jnp.bfloat16)
    gate_ssm = project("project_z", one_late, in_matrix, 0, inner_local, jnp.float32)
    attend = Attend(tokens, ctx_count * tokens, heads_query)
    rank = ctx_rank.astype(jnp.int32)[None]
    kept = {}

    def fill_within(sent):
        kept["within"] = scan.within(source_rows, after(small_rows, own_state), write_rows, read_rows)
        return (kept["within"], gate_ssm, queries, cot_sent)

    def fill_attend(sent):
        mine = jnp.concatenate(kv_got, axis=0)
        other = partner(mine, CORE)
        kept["key"] = jnp.where(core == 0, mine, other)
        kept["value"] = jnp.where(core == 0, other, mine)
        kept["attended"], kept["log"] = attend.forward(
            after(rank, sent), queries, kept["key"], kept["value"]
        )
        kept["attended_sent"] = send_rows(kept["attended"])
        return (kept["attended"], one_sent)

    def fill_act(sent):
        kept["act"] = times_back(after(grad_low, sent), mlp_down)
        return (kept["act"],)

    entering = chained(own_state, running[:, -1], True, [fill_within, fill_attend, fill_act])
    key_rows, value_rows, attended = (kept["key"], kept["value"], kept["attended"])
    ssm_values, gated_rows = scan.carried(kept["within"], gate_ssm, small_rows, read_rows, entering)
    outs_sent = [
        [gated, att] for gated, att in zip(send_rows(gated_rows), kept["attended_sent"], strict=True)
    ]

    terms = [(gated_rows, ssm_out, 0), (attended, attn_out, 0)]
    given = partner(half_share("mix_other", there, terms, False), CORE)
    mix_mine = half_share("mix_own", here, terms, False, given)
    mix_theirs = partner(mix_mine, CHIP)
    gu_matrix = after(mlp_gate_up, mix_mine).reshape(model_width, 2 * ff_local)
    cot_columns = both_halves([after(part, mix_mine) for part in cot_sent])
    one_columns = both_halves([after(part, mix_mine) for part in one_sent])
    kv_columns = lax.dynamic_index_in_dim(after(kv_pair, mix_mine), core, 1, keepdims=False)
    pad = -heads_local % AHEAD_DIM
    weight_small = jnp.concatenate(
        [
            kv_columns,
            cut(bc_matrix, 2 * core + chip, bc_share, 1),
            jnp.pad(ssm_dt, ((0, 0), (0, pad))),
        ],
        axis=1,
    )
    mix_theirs = after(mix_theirs, gu_matrix, cot_columns, one_columns, weight_small, outs_sent)
    middle, two_mine, mix_squares = middle_norm(here, hidden_rows, mix_mine, mix_theirs, gain_two)

    two_other = partner(two_mine, CORE)
    activated, grad_gate, grad_up = expand(here, two_mine, two_other, gu_matrix, kept["act"])
    act_sent = send_rows(activated)
    two_sent = send_columns(two_mine)
    gate_sent = send_rows(grad_gate)
    up_sent = send_rows(grad_up)
    terms = [(grad_gate, gu_matrix, 0), (grad_up, gu_matrix, 1)]
    given = partner(half_share("two_other", there, terms, True), CORE)
    two_back = half_share("two_own", here, terms, True, given)
    two_theirs = partner(two_back, CHIP)
    down_made, down_sum = weight_grad(
        "grad_down", core, [(grad_low, cot_columns, [activated], listed(act_sent))], two_back
    )
    two_theirs = after(two_theirs, down_made, two_sent, gate_sent)
    grad_middle, mix_grad_mine, gain_two_sum = norm_grad(
        "norm_two_back", here, middle, grad_low, two_back, two_theirs, gain_two, (jnp.float32, jnp.bfloat16)
    )

    mix_grad_other = partner(mix_grad_mine, CORE)
    mix_sent = send_columns(mix_grad_mine)
    grad_values, grad_gate_ssm = gated_back(
        here, mix_grad_mine, mix_grad_other, ssm_out, gate_ssm, ssm_values
    )
    own_grad = scan.own_state(grad_values, small_rows, read_rows, False)
    z_sent = send_rows(grad_gate_ssm)
    two_columns = both_halves([after(part, mix_grad_mine) for part in two_sent])
    mlp_terms = [(activated, mlp_down, 0)]

    def fill_attend_back(sent):
        kept["mlp_given"] = partner(half_share("mlp_other", after(there, sent), mlp_terms, False), CORE)
        kept["gate_up"] = weight_grad(
            "grad_gate_up",
            core,
            [((two_mine, two_other), two_columns, [grad_gate, grad_up], listed(gate_sent, up_sent))],
            sent,
        )
        grad_attended = rows_back(after(here, kept["gate_up"][0]), mix_grad_mine, mix_grad_other, attn_out)
        kept["grads"] = attend.back(rank, queries, grad_attended, kept["log"], key_rows, value_rows)
        grad_query, grad_key, grad_value = kept["grads"]
        kept["query_sent"] = send_rows(grad_query)
        kept["kv_given"] = jnp.where(core == 0, grad_value, grad_key).astype(jnp.bfloat16)
        return (grad_query, kept["kv_given"], kept["mlp_given"])

    def fill_scan_back(sent):
        given = partner(after(kept["kv_given"], sent), CORE)
        kept["scan"] = scan.within_back(
            source_rows, after(grad_values, sent), small_rows, write_rows, read_rows
        )
        _, grad_key, grad_value = kept["grads"]
        own_part = jnp.where(core == 0, grad_key, grad_value)
        paired = (own_part + given.astype(jnp.float32)).reshape(ctx_count, tokens, AHEAD_DIM)
        kept["kv"] = [paired[0]] + [paired[shift].astype(jnp.bfloat16) for shift in range(1, ctx_count)]
        return (kept["scan"][0], kept["kv"], mix_sent, z_sent, kept["query_sent"])

    def fill_weights(sent):
        kept["kv_back"] = [
            moved(after(part, sent), "ctx", -shift) for shift, part in enumerate(kept["kv"]) if shift
        ]
        kept["mlp_mine"] = half_share("mlp_own", after(here, sent), mlp_terms, False, kept["mlp_given"])
        mix_columns = both_halves([after(part, sent) for part in mix_sent])
        kept["mixer"] = weight_grad(
            "grad_mixer",
            core,
            [
                ((mix_grad_mine, mix_grad_other), mix_columns, [gated_rows, attended], outs_sent),
                (
                    input_one,
                    one_columns,
                    [grad_gate_ssm, kept["grads"][0]],
                    listed(z_sent, kept["query_sent"]),
                ),
            ],
            kept["mlp_mine"],
        )
        return (kept["mixer"][0],)

    leaving = chained(own_grad, running[:, -1], False, [fill_attend_back, fill_scan_back, fill_weights])
    grad_query = kept["grads"][0]
    grad_written, scan_sums, grad_b, grad_c = kept["scan"]
    grad_source, steps, grad_b, grad_c = scan.carried_back(
        source_rows, grad_values, small_rows, scan_sums, grad_written,
        write_rows, read_rows, entering, leaving, grad_b, grad_c,
    )
    source_sent = send_rows(grad_source)
    grad_bc = jnp.concatenate([grad_b, grad_c], axis=1)
    bc_sent = partner(cut(grad_bc, 1 - core, 2 * bc_share, 1).astype(jnp.bfloat16), CORE)
    bc_mine = cut(grad_bc, core, 2 * bc_share, 1) + bc_sent.astype(jnp.float32)
    bc_given = partner(cut(bc_mine, 1 - chip, bc_share, 1).astype(jnp.bfloat16), CHIP)
    grad_bc_low = (cut(bc_mine, chip, bc_share, 1) + bc_given.astype(jnp.float32)).astype(jnp.bfloat16)
    kv_sum = kept["kv"][0]
    for part in kept["kv_back"]:
        kv_sum = kv_sum + part.astype(jnp.float32)
    grad_kv_low = kv_sum.astype(jnp.bfloat16)
    grad_dt_pre = steps[:, 0:2].reshape(heads_local, tokens) * jax.nn.sigmoid(dt_pre)
    flow_rows = steps[:, 2:4].reshape(heads_local, tokens)
    grad_dt_bias = jnp.sum(grad_dt_pre, axis=1)
    grad_a_log = decay_rate * jnp.sum(dt_rows * flow_rows, axis=1)
    grad_d_skip = jnp.sum(scan_sums[:, 4, : 2 * head_width].reshape(heads_local, head_width), axis=1)
    grad_dt_low = jnp.pad(grad_dt_pre.astype(jnp.bfloat16).T, ((0, 0), (0, pad)))
    grad_small = jnp.concatenate([grad_kv_low, grad_bc_low, grad_dt_low], axis=1)
    small_sent = send_rows(grad_small)
    terms = [
        (grad_gate_ssm, in_matrix, 0),
        (grad_source, in_matrix, 1),
        (grad_query, attn_q, 0),
        (grad_small, weight_small, 0),
    ]
    mlp_theirs = partner(after(kept["mlp_mine"], grad_bc_low), CHIP)
    given = partner(half_share("one_other", after(there, source_sent, down_sum, kept["gate_up"][1]), terms, True), CORE)
    one_back = half_share("one_own", after(here, mlp_theirs), terms, True, given)
    one_theirs = partner(one_back, CHIP)
    last_made, last_sum = weight_grad(
        "grad_last",
        core,
        [(input_one, one_columns, [grad_source, grad_small], listed(source_sent, small_sent))],
        one_back,
    )
    one_theirs = after(one_theirs, last_made, kept["mixer"][1])
    hidden_mine, gain_one_sum = norm_grad(
        "norm_one_back", here, hidden_rows, grad_middle, one_back, one_theirs, gain_one, (jnp.bfloat16,)
    )
    grad_hidden = gather_rows(hidden_mine, core)
    mlp_total = wide(kept["mlp_mine"]) + wide(after(mlp_theirs, hidden_mine))
    block_out = middle + mlp_total
    output = gather_rows(block_out.astype(jnp.bfloat16), core)
    squares = jnp.stack([jnp.sum(mix_squares), jnp.sum(mlp_total * mlp_total), jnp.sum(block_out * block_out)])
    halves = jnp.concatenate([gain_one_sum[0], gain_two_sum[0], squares])
    halves = halves + partner(halves, CORE)
    sums = jnp.concatenate([halves, grad_dt_bias, grad_a_log, grad_d_skip])
    sums = jnp.pad(sums, (0, -sums.shape[0] % 1024)).reshape(-1, 128)
    sums = all_sum(all_sum(sums, "dp"), "ctx").reshape(-1)

    grad_last = wide(after(last_sum, kept["mixer"][1], sums))
    grad_little = grad_last[:, inner_local:]
    held = narrow(grad_little[:, : AHEAD_DIM + bc_share])
    pieces = jnp.stack([held] + [partner(held, stride) for stride in range(1, 4)])

    def of_rank(rank):
        return lax.dynamic_index_in_dim(pieces, tensor_rank ^ rank, 0, keepdims=False).astype(jnp.float32)

    by_rank = [of_rank(rank) for rank in range(4)]
    kv_rows = held.shape[0] // 4
    kv_parts = [cut(part[:, :AHEAD_DIM], tensor_rank, kv_rows, 0) for part in by_rank]
    grad_attn_kv = jnp.stack(
        [jnp.concatenate([kv_parts[kind], kv_parts[2 + kind]], axis=1) for kind in range(2)], axis=1
    )
    grad_ssm_bc = jnp.concatenate(
        [by_rank[2 * (place % 2) + place // 2][:, AHEAD_DIM:] for place in range(4)], axis=1
    ).reshape(-1, 2, state_width)
    grad_ssm_dt = grad_little[:, AHEAD_DIM + bc_share : AHEAD_DIM + bc_share + heads_local]

    place = lax.axis_index("dp") * ctx_count + ctx_rank
    share = model_width // (lax.axis_size("dp") * ctx_count)
    small = sums[2 * model_width :]
    counted = tokens * model_width * lax.axis_size("dp") * ctx_count
    grad_down = wide(down_sum)
    grad_gate_up = wide(after(kept["gate_up"][1], grad_down)).reshape(-1, 2, ff_local)
    grad_mixer = wide(after(kept["mixer"][1], grad_gate_up))
    outs_width = inner_local + heads_query * AHEAD_DIM
    grad_outs = grad_mixer[:, :outs_width]
    grad_first = grad_mixer[:, outs_width:]
    branch_rms = jnp.sqrt(small[:3] / counted)
    return (
        output[None],
        grad_hidden[None],
        cut(sums[:model_width], place, share, 0),
        jnp.stack([grad_first[:, :inner_local], grad_last[:, :inner_local]], axis=1),
        grad_ssm_bc,
        grad_ssm_dt,
        small[3 : 3 + heads_local],
        small[3 + heads_local : 3 + 2 * heads_local],
        small[3 + 2 * heads_local : 3 + 3 * heads_local],
        grad_outs[:, :inner_local].T,
        grad_first[:, inner_local:],
        grad_attn_kv,
        grad_outs[:, inner_local:].T,
        cut(sums[model_width : 2 * model_width], place, share, 0),
        grad_gate_up,
        grad_down.T,
        branch_rms,
    )


def solution(mesh):
    return jax.shard_map(
        body,
        mesh=mesh,
        in_specs=(
            P("dp", "ctx", None),
            P("dp", "ctx", None),
            P(),
            P(None, None, "tensor"),
            P(),
            P(None, "tensor"),
            P("tensor"),
            P("tensor"),
            P("tensor"),
            P("tensor", None),
            P(None, "tensor"),
            P(),
            P("tensor", None),
            P(),
            P(None, None, "tensor"),
            P("tensor", None),
        ),
        out_specs=(
            P("dp", "ctx", None),
            P("dp", "ctx", None),
            P(("dp", "ctx")),
            P(("dp", "ctx"), None, "tensor"),
            P(("dp", "ctx"), None, None),
            P(("dp", "ctx"), "tensor"),
            P("tensor"),
            P("tensor"),
            P("tensor"),
            P("tensor", ("dp", "ctx")),
            P(("dp", "ctx"), "tensor"),
            P(("dp", "ctx", "tensor"), None, None),
            P("tensor", ("dp", "ctx")),
            P(("dp", "ctx")),
            P(("dp", "ctx"), None, "tensor"),
            P("tensor", ("dp", "ctx")),
            P(),
        ),
        check_vma=False,
    )
```

```python
from functools import partial
import math

import jax
import jax.numpy as jnp
from jax import lax
from jax.experimental import pallas as pl
from jax.experimental.pallas import tpu as pltpu
from jax.sharding import PartitionSpec as P

AHEAD_DIM = 128
SCAN_BLOCK = 256


EPSILON = 1e-05
NEG_FILL = -1e30
VMEM_GRANT = 24 * 1024 * 1024
WIDE_GRANT = 60 * 1024 * 1024

CORE, CHIP = (1, 2)


def partner(value, stride):
    return lax.ppermute(value, "tensor", [(rank, rank ^ stride) for rank in range(4)])


def shifted(value, axis, shift):
    count = lax.axis_size(axis)
    return lax.ppermute(value, axis, [(i, (i + shift) % count) for i in range(count)])


def moved(value, axis, shift):
    count = lax.axis_size(axis)
    pairs = [(i, i + shift) for i in range(count) if 0 <= i + shift < count]
    return lax.ppermute(value, axis, pairs)


def after(value, *others):
    return lax.optimization_barrier((value,) + others)[0]


def cut(value, index, size, axis):
    return lax.dynamic_slice_in_dim(value, index * size, size, axis)


def gather_rows(name, at, mine):
    rows, width = mine.shape
    half = pl.BlockSpec((rows, width), lambda i, at: (0, 0))
    whole = pl.BlockSpec((2 * rows, width), lambda i, at: (0, 0))
    args = (mine, partner(mine, CORE))
    outs = [(like((2 * rows, width), mine.dtype), whole)]
    size = 4 * rows * width * mine.dtype.itemsize
    return call_at(name, gather_kernel, at, (1,), [half, half], args, outs, moved_bytes=size)[0]


def send_columns(rows):
    count, mine = (lax.axis_size("dp"), lax.axis_index("dp"))
    share = rows.shape[1] // count
    return [
        shifted(cut(rows, (mine + shift) % count, share, 1), "dp", shift) for shift in range(1, count)
    ]


def both_halves(arrived):
    return [(part, partner(part, CORE)) for part in arrived]


def send_rows(value):
    return [shifted(value, "dp", shift) for shift in range(1, lax.axis_size("dp"))]


def all_sum(value, axis):
    count, mine = (lax.axis_size(axis), lax.axis_index(axis))
    pieces = jnp.stack([value] + [shifted(value, axis, shift) for shift in range(1, count)])
    total = jnp.zeros_like(value)
    for rank in range(count):
        total = total + lax.dynamic_index_in_dim(pieces, (mine - rank) % count, 0, keepdims=False)
    return total


def scatter_sum(value, axis):
    count, mine = (lax.axis_size(axis), lax.axis_index(axis))
    share = value.shape[0] // count
    total = cut(value, mine, share, 0)
    for shift in range(1, count):
        total = total + shifted(cut(value, (mine + shift) % count, share, 0), axis, shift)
    return total


def chained(state, log_decay, forward, fillers):
    count = lax.axis_size("ctx")
    decay = jnp.exp(log_decay)[:, None, None]
    per_head = (decay.shape[0], state.shape[0] // decay.shape[0], state.shape[1])
    own = state.reshape(per_head)
    sent = state
    entering = None
    for step in range(1, count):
        pair = (step - 1, step) if forward else (count - step, count - step - 1)
        arrived = lax.ppermute(sent, "ctx", [pair])
        if step <= len(fillers):
            arrived = after(arrived, *fillers[step - 1](sent))
        entering = arrived if entering is None else entering + arrived
        if step < count - 1:
            total = own.astype(jnp.float32) + decay * arrived.reshape(per_head).astype(jnp.float32)
            sent = total.astype(jnp.bfloat16).reshape(state.shape)
    return entering


def matmul_low(former, latter):
    return jnp.dot(former, latter, preferred_element_type=jnp.float32)


def inner_rows(former, latter):
    return lax.dot_general(
        former, latter, (((0,), (0,)), ((), ())), preferred_element_type=jnp.float32
    )


def times_back(former, latter):
    return lax.dot_general(
        former, latter, (((1,), (1,)), ((), ())), preferred_element_type=jnp.float32
    )


def split_lanes(first, second, shape):
    lane = lax.broadcasted_iota(jnp.int32, shape, 1)
    return jnp.where(lane < shape[1] // 2, first, second)


def wide(values):
    return values.astype(jnp.float32)


def narrow(values):
    return values.astype(jnp.bfloat16)


def in_two(values):
    high = narrow(values)
    return (high, narrow(values - wide(high)))


def spread(rows, shape):
    rows = jnp.concatenate([rows, jnp.zeros((6, rows.shape[1]), jnp.float32)], axis=0)
    place = lax.broadcasted_iota(jnp.int32, (8, shape[1]), 0)
    lane = lax.broadcasted_iota(jnp.int32, (8, shape[1]), 1)
    chosen = narrow(jnp.where(place == lane // (shape[1] // 2), 1.0, 0.0))
    high, low = in_two(rows.T)
    return matmul_low(high, chosen) + matmul_low(low, chosen)


def lane_sums(values):
    place = lax.broadcasted_iota(jnp.int32, (8, values.shape[1]), 0)
    lane = lax.broadcasted_iota(jnp.int32, (8, values.shape[1]), 1)
    chosen = narrow(jnp.where(place == lane // (values.shape[1] // 2), 1.0, 0.0))
    high, low = in_two(values)
    return times_back(chosen, high) + times_back(chosen, low)


def lanes_of(ref):
    return [slice(at, at + 128) for at in range(0, ref.shape[1], 128)]


def state_kernel(u_ref, small_ref, b_ref, state_ref, *, to_end):
    for pair, lanes in enumerate(lanes_of(u_ref)):
        rows = small_ref[pair]
        if to_end:
            last = rows[0:2, rows.shape[1] - 1 :]
            weights = jnp.exp(last - rows[0:2]) * rows[2:4]
        else:
            weights = jnp.exp(rows[0:2])
        u = wide(u_ref[:, lanes])
        weighted = narrow(u * spread(weights, u.shape))
        state_ref[lanes, :] = narrow(inner_rows(weighted, b_ref[...]))


def scan_kernel(u_ref, small_ref, b_ref, c_ref, y_ref, cb_ref):
    size = SCAN_BLOCK
    count = u_ref.shape[0] // size
    block = [slice(i * size, (i + 1) * size) for i in range(count)]

    @pl.when(pl.program_id(0) == 0)
    def _():
        for i in range(count):
            for j in range(i + 1):
                cb_ref[block[i], block[j]] = times_back(c_ref[block[i], :], b_ref[block[j], :])

    lower = lax.broadcasted_iota(jnp.int32, (size, size), 0) >= lax.broadcasted_iota(
        jnp.int32, (size, size), 1
    )
    for pair, lanes in enumerate(lanes_of(u_ref)):
        rows = small_ref[pair]
        cols = rows.T
        for i in range(count):
            parts = []
            for h in range(2):
                total = jnp.zeros((size, 128), jnp.float32)
                for j in range(i + 1):
                    difference = cols[block[i], h : h + 1] - rows[h : h + 1, block[j]]
                    if i == j:
                        difference = jnp.where(lower, difference, NEG_FILL)
                    weights = cb_ref[block[i], block[j]] * rows[2 + h : 3 + h, block[j]]
                    mixing = narrow(jnp.exp(difference) * weights)
                    total = total + matmul_low(mixing, u_ref[block[j], lanes])
                parts.append(total)
            skip = split_lanes(cols[block[i], 4:5], cols[block[i], 5:6], parts[0].shape)
            values = split_lanes(*parts, parts[0].shape) + skip * wide(u_ref[block[i], lanes])
            y_ref[block[i], lanes] = values


def carry_kernel(y_ref, z_ref, small_ref, c_ref, state_ref, out_ref, gated_ref):
    for pair, lanes in enumerate(lanes_of(y_ref)):
        carried = times_back(c_ref[...], state_ref[lanes, :])
        decay = spread(jnp.exp(small_ref[pair][0:2]), carried.shape)
        values = y_ref[:, lanes] + carried * decay
        out_ref[:, lanes] = values
        gate = z_ref[:, lanes]
        gated_ref[:, lanes] = narrow(values * (gate * jax.nn.sigmoid(gate)))


def scan_back_kernel(u_ref, dy_ref, small_ref, b_ref, c_ref, dw_ref, sums_ref, db_ref, dc_ref, cb_ref, mix_ref):
    size = SCAN_BLOCK
    count = u_ref.shape[0] // size
    width = u_ref.shape[1]
    block = [slice(i * size, (i + 1) * size) for i in range(count)]

    @pl.when(pl.program_id(0) == 0)
    def _():
        mix_ref[...] = jnp.zeros_like(mix_ref)
        for i in range(count):
            for j in range(i, count):
                cb_ref[block[i], block[j]] = times_back(b_ref[block[i], :], c_ref[block[j], :])

    rows = small_ref[0]
    cols = rows.T
    upper = lax.broadcasted_iota(jnp.int32, (size, size), 0) <= lax.broadcasted_iota(
        jnp.int32, (size, size), 1
    )
    lane = lax.broadcasted_iota(jnp.int32, (size, width), 1)
    read_sums = [[jnp.zeros((1, size), jnp.float32) for _ in range(count)] for _ in range(2)]
    write_sums = [[], []]
    ones = jnp.ones((8, size), jnp.bfloat16)
    for i in range(count):
        parts = []
        for h in range(2):
            total = jnp.zeros((size, width), jnp.float32)
            write_sum = jnp.zeros((8, size), jnp.float32)
            step = cols[block[i], 2 + h : 3 + h]
            for j in range(i, count):
                difference = rows[h : h + 1, block[j]] - cols[block[i], h : h + 1]
                if i == j:
                    difference = jnp.where(upper, difference, NEG_FILL)
                decay = jnp.exp(difference)
                dy = dy_ref[block[j], :]
                dy_head = jnp.where((lane < width // 2) == (h == 0), dy, jnp.zeros_like(dy))
                product = decay * times_back(u_ref[block[i], :], dy_head)
                crossing = cb_ref[block[i], block[j]]
                total = total + matmul_low(narrow(decay * crossing), dy)
                weighted = product * step
                mix_ref[block[i], block[j]] += weighted
                high, low = in_two(product * crossing)
                write_sum = write_sum + times_back(ones, high) + times_back(ones, low)
                read_sums[h][j] = read_sums[h][j] + jnp.sum(weighted * crossing, axis=0, keepdims=True)
            parts.append(total)
            write_sums[h].append(write_sum)
        dw_ref[block[i], :] = split_lanes(*parts, parts[0].shape)
    writes = [jnp.concatenate(write_sums[h], axis=1)[0:1] for h in range(2)]
    skip = jnp.sum(wide(u_ref[...]) * wide(dy_ref[...]), axis=0, keepdims=True)
    skip = jnp.concatenate([skip, jnp.zeros((1, u_ref.shape[0] - width), jnp.float32)], axis=1)
    reads = [jnp.concatenate(read_sums[h], axis=1) for h in range(2)]
    sums_ref[0] = jnp.concatenate(reads + writes + [skip, jnp.zeros_like(skip)] + reads, axis=0)

    @pl.when(pl.program_id(0) == pl.num_programs(0) - 1)
    def _():
        for i in range(count):
            total = jnp.zeros((size, b_ref.shape[1]), jnp.float32)
            for j in range(i, count):
                total = total + matmul_low(narrow(mix_ref[block[i], block[j]]), c_ref[block[j], :])
            db_ref[block[i], :] = total
        for j in range(count):
            total = jnp.zeros((size, b_ref.shape[1]), jnp.float32)
            for i in range(j + 1):
                total = total + inner_rows(narrow(mix_ref[block[i], block[j]]), b_ref[block[i], :])
            dc_ref[block[j], :] = total


def carry_back_kernel(
    u_ref, dy_ref, small_ref, sums_ref, dw_ref, b_ref, c_ref, state_ref, grad_ref, db_in_ref, dc_in_ref,
    du_ref, steps_ref, db_ref, dc_ref,
):
    tokens = u_ref.shape[0]

    @pl.when(pl.program_id(0) == 0)
    def _():
        db_ref[...] = db_in_ref[...]
        dc_ref[...] = dc_in_ref[...]

    all_started, all_ended = ([], [])
    for pair, lanes in enumerate(lanes_of(u_ref)):
        rows = small_ref[pair]
        last = rows[0:2, tokens - 1 :]
        u = wide(u_ref[:, lanes])
        dy = wide(dy_ref[:, lanes])
        state = state_ref[lanes, :]
        grad = grad_ref[lanes, :]
        started = spread(jnp.exp(rows[0:2]), u.shape) * dy
        tail = spread(jnp.exp(last - rows[0:2]), u.shape)
        ended = tail * u
        step = spread(rows[2:4], u.shape)
        left = times_back(b_ref[...], grad)
        dw = dw_ref[:, lanes] + tail * left
        du_ref[:, lanes] = narrow(step * dw + spread(rows[4:6], u.shape) * dy)
        all_started.append(narrow(started))
        all_ended.append(narrow(ended * step))
        reads = lane_sums(started * times_back(c_ref[...], state))[0:2]
        writes = lane_sums(ended * left)[0:2]
        sums = sums_ref[pair]
        written = sums[2:4] + writes
        slope = sums[0:2] + reads - rows[2:4] * written
        products = jnp.sum(wide(state) * wide(grad), axis=1, keepdims=True)
        height = products.shape[0] // 2
        across = jnp.concatenate(
            [
                jnp.sum(products[:height], axis=0, keepdims=True),
                jnp.sum(products[height:], axis=0, keepdims=True),
            ],
            axis=0,
        ) * jnp.exp(last)
        across = across + jnp.sum(rows[2:4] * writes, axis=1, keepdims=True)
        held = jnp.concatenate([slope, jnp.zeros((6, tokens), jnp.float32)], axis=0)
        place = lax.broadcasted_iota(jnp.int32, held.shape, 1)
        reach = 1
        while reach < tokens:
            held = held + jnp.where(place < tokens - reach, pltpu.roll(held, tokens - reach, 1), 0.0)
            reach = 2 * reach
        flow = held[0:2] + across
        steps_ref[pair] = jnp.concatenate([written + rows[6:8] * flow, flow, held[2:6]], axis=0)
    dc_ref[...] += matmul_low(jnp.concatenate(all_started, axis=1), state_ref[...])
    db_ref[...] += matmul_low(jnp.concatenate(all_ended, axis=1), grad_ref[...])


def attend_scores(rank_ref, k_ref, q_ref, own, factor):
    scores = times_back(k_ref[...], q_ref[...]) * factor
    keys, queries = scores.shape
    row = lax.broadcasted_iota(jnp.int32, (own, queries), 0)
    column = lax.broadcasted_iota(jnp.int32, (own, queries), 1) + pl.program_id(1) * queries
    near = jnp.where(row <= column, scores[:own], NEG_FILL)
    if keys == own:
        return near
    far_row = lax.broadcasted_iota(jnp.int32, (keys - own, queries), 0)
    far = jnp.where(far_row < rank_ref[0] * own, scores[own:], NEG_FILL)
    return jnp.concatenate([near, far], axis=0)


def attend_kernel(rank_ref, q_ref, k_ref, v_ref, out_ref, log_ref, flat_ref, *, own, factor):
    @pl.when((pl.program_id(0) == 0) & (pl.program_id(1) == 0))
    def _():
        flat_ref[...] = v_ref[...].T

    scores = attend_scores(rank_ref, k_ref, q_ref, own, factor)
    maxima = jnp.max(scores, axis=0, keepdims=True)
    weights = jnp.exp(scores - maxima)
    totals = jnp.sum(weights, axis=0, keepdims=True)
    probability = narrow(weights * (1.0 / totals))
    out_ref[...] = narrow(matmul_low(flat_ref[...], probability).T)
    log_ref[0] = jnp.broadcast_to(maxima + jnp.log(totals), log_ref.shape[1:])


def attend_back_kernel(
    rank_ref, q_ref, do_ref, log_ref, k_ref, v_ref, dq_ref, dk_ref, dv_ref, flat_ref, *, own, factor
):
    @pl.when((pl.program_id(0) == 0) & (pl.program_id(1) == 0))
    def _():
        flat_ref[...] = k_ref[...].T
        dk_ref[...] = jnp.zeros_like(dk_ref)
        dv_ref[...] = jnp.zeros_like(dv_ref)

    scores = attend_scores(rank_ref, k_ref, q_ref, own, factor)
    probability = jnp.exp(scores - log_ref[0][0:1])
    dv_ref[...] += matmul_low(narrow(probability), do_ref[...])
    grad_prob = times_back(v_ref[...], do_ref[...])
    centre = jnp.sum(probability * grad_prob, axis=0, keepdims=True)
    grad_score = narrow(probability * (grad_prob - centre))
    dk_ref[...] += matmul_low(grad_score, q_ref[...]) * factor
    dq_ref[...] = narrow((matmul_low(flat_ref[...], grad_score) * factor).T)


def call(name, kernel, grid, specs, args, outs, scratch=(), grant=VMEM_GRANT):
    return pl.pallas_call(
        kernel,
        name=name,
        grid=grid,
        in_specs=specs,
        out_specs=[spec for _, spec in outs],
        out_shape=[out for out, _ in outs],
        scratch_shapes=list(scratch),
        cost_estimate=pl.CostEstimate(flops=1, bytes_accessed=1, transcendentals=0),
        compiler_params=pltpu.CompilerParams(vmem_limit_bytes=grant),
    )(*args)


def like(shape, kind):
    return jax.ShapeDtypeStruct(shape, kind)


class Scan:
    def __init__(self, tokens, inner, state):
        self.tokens, self.inner, self.state = (tokens, inner, state)
        self.pairs = inner // 128
        self.shared = pl.BlockSpec((tokens, state), lambda p: (0, 0))
        self.small_like = like((self.pairs, 8, tokens), jnp.float32)
        self.square = pltpu.VMEM((tokens, tokens), jnp.float32)

    def specs(self, group):
        group = math.gcd(group, self.pairs)
        return (
            (self.pairs // group,),
            pl.BlockSpec((self.tokens, 128 * group), lambda p: (0, p)),
            pl.BlockSpec((group, 8, self.tokens), lambda p: (p, 0, 0)),
            pl.BlockSpec((128 * group, self.state), lambda p: (p, 0)),
        )

    def rows_like(self, kind):
        return like((self.tokens, self.inner), kind)

    def own_state(self, u, small, b, to_end):
        grid, tile, row, states = self.specs(6)
        return call(
            "own_state",
            partial(state_kernel, to_end=to_end),
            grid,
            [tile, row, self.shared],
            (u, small, b),
            [(like((self.inner, self.state), jnp.bfloat16), states)],
        )[0]

    def within(self, u, small, b, c):
        grid, tile, row, states = self.specs(6)
        return call(
            "scan",
            scan_kernel,
            grid,
            [tile, row, self.shared, self.shared],
            (u, small, b, c),
            [(self.rows_like(jnp.float32), tile)],
            [self.square],
        )[0]

    def carried(self, y, z, small, c, state):
        grid, tile, row, states = self.specs(6)
        return call(
            "carry",
            carry_kernel,
            grid,
            [tile, tile, row, self.shared, states],
            (y, z, small, c, state),
            [(self.rows_like(jnp.float32), tile), (self.rows_like(jnp.bfloat16), tile)],
        )

    def within_back(self, u, dy, small, b, c):
        shared = like((self.tokens, self.state), jnp.float32)
        grid, tile, row, states = self.specs(1)
        return call(
            "scan_back",
            scan_back_kernel,
            grid,
            [tile, tile, row, self.shared, self.shared],
            (u, dy, small, b, c),
            [(self.rows_like(jnp.float32), tile), (self.small_like, row)] + 2 * [(shared, self.shared)],
            [self.square, self.square],
        )

    def carried_back(self, u, dy, small, sums, dw, b, c, state, grad, db, dc):
        shared = like((self.tokens, self.state), jnp.float32)
        grid, tile, row, states = self.specs(6)
        return call(
            "carry_back",
            carry_back_kernel,
            grid,
            [tile, tile, row, row, tile] + 2 * [self.shared] + 2 * [states] + 2 * [self.shared],
            (u, dy, small, sums, dw, b, c, state, grad, db, dc),
            [(self.rows_like(jnp.bfloat16), tile), (self.small_like, row)] + 2 * [(shared, self.shared)],
            grant=WIDE_GRANT,
        )


class Attend:
    def __init__(self, tokens, keys, heads):
        self.tokens, self.keys, self.heads = (tokens, keys, heads)
        size = min(256, tokens)
        self.grid = (heads, tokens // size)
        self.factor = 1.0 / math.sqrt(AHEAD_DIM)
        self.rank = pl.BlockSpec(memory_space=pltpu.SMEM)
        self.tile = pl.BlockSpec((size, AHEAD_DIM), lambda h, q: (q, h))
        self.log = pl.BlockSpec((1, 8, size), lambda h, q: (h, 0, q))
        self.whole = pl.BlockSpec((keys, AHEAD_DIM), lambda h, q: (0, 0))
        self.rows_like = like((tokens, heads * AHEAD_DIM), jnp.bfloat16)
        self.flat = pltpu.VMEM((AHEAD_DIM, keys), jnp.bfloat16)

    def forward(self, rank, q, k, v):
        return call(
            "attend",
            partial(attend_kernel, own=self.tokens, factor=self.factor),
            self.grid,
            [self.rank, self.tile, self.whole, self.whole],
            (rank, q, k, v),
            [(self.rows_like, self.tile), (like((self.heads, 8, self.tokens), jnp.float32), self.log)],
            [self.flat],
        )

    def back(self, rank, q, do, log, k, v):
        whole = like((self.keys, AHEAD_DIM), jnp.float32)
        return call(
            "attend_back",
            partial(attend_back_kernel, own=self.tokens, factor=self.factor),
            self.grid,
            [self.rank, self.tile, self.tile, self.log, self.whole, self.whole],
            (rank, q, do, log, k, v),
            [(self.rows_like, self.tile), (whole, self.whole), (whole, self.whole)],
            [self.flat],
        )


def call_at(name, kernel, scalars, grid, specs, args, outs, grant=VMEM_GRANT, moved_bytes=1):
    return pl.pallas_call(
        kernel,
        name=name,
        grid_spec=pltpu.PrefetchScalarGridSpec(
            num_scalar_prefetch=1,
            grid=grid,
            in_specs=specs,
            out_specs=[spec for _, spec in outs],
        ),
        out_shape=[out for out, _ in outs],
        cost_estimate=pl.CostEstimate(flops=1, bytes_accessed=moved_bytes, transcendentals=0),
        compiler_params=pltpu.CompilerParams(vmem_limit_bytes=grant),
    )(scalars, *args)


def mean_scale(values):
    return lax.rsqrt(jnp.mean(values * values, axis=-1, keepdims=True) + EPSILON)


def norm_kernel(x_ref, gain_ref, out_ref):
    x = wide(x_ref[...])
    out_ref[...] = narrow(x * mean_scale(x) * gain_ref[...])


def normed(x, gain):
    rows, width = x.shape
    size = min(128, rows)
    tile = pl.BlockSpec((size, width), lambda i: (i, 0))
    line = pl.BlockSpec((1, width), lambda i: (0, 0))
    return call(
        "norm_one", norm_kernel, (rows // size,), [tile, line], (x, gain), [(like(x.shape, x.dtype), tile)]
    )[0]


def middle_kernel(at_ref, x_ref, mine_ref, theirs_ref, gain_ref, middle_ref, out_ref, sum_ref):
    @pl.when(pl.program_id(0) == 0)
    def _():
        sum_ref[...] = jnp.zeros_like(sum_ref)

    mixed = wide(mine_ref[...]) + wide(theirs_ref[...])
    middle = wide(x_ref[...]) + mixed
    middle_ref[...] = middle
    out_ref[...] = narrow(middle * mean_scale(middle) * gain_ref[...])
    sum_ref[...] += jnp.sum(mixed * mixed, axis=0, keepdims=True)


def middle_norm(at, x, mine, theirs, gain):
    rows, width = mine.shape
    size = min(128, rows)
    steps = rows // size
    tile = pl.BlockSpec((size, width), lambda i, at: (i, 0))
    half = pl.BlockSpec((size, width), lambda i, at: (at[0] * steps + i, 0))
    line = pl.BlockSpec((1, width), lambda i, at: (0, 0))
    return call_at(
        "norm_two",
        middle_kernel,
        at,
        (steps,),
        [half, tile, tile, line],
        (x, mine, theirs, gain),
        [
            (like(mine.shape, jnp.float32), tile),
            (like(mine.shape, jnp.bfloat16), tile),
            (like((1, width), jnp.float32), line),
        ],
    )


def norm_back_kernel(at_ref, x_ref, base_ref, mine_ref, theirs_ref, gain_ref, *outs):
    sum_ref = outs[-1]

    @pl.when(pl.program_id(0) == 0)
    def _():
        sum_ref[...] = jnp.zeros_like(sum_ref)

    grad = wide(mine_ref[...]) + wide(theirs_ref[...])
    x = wide(x_ref[...])
    scale = mean_scale(x)
    weighted = grad * gain_ref[...]
    inner = jnp.mean(weighted * x, axis=-1, keepdims=True)
    total = wide(base_ref[...]) + (scale * weighted - x * (scale * scale * scale * inner))
    for out_ref in outs[:-1]:
        out_ref[...] = total.astype(out_ref.dtype)
    sum_ref[...] += jnp.sum(grad * x * scale, axis=0, keepdims=True)


def norm_grad(name, at, x, base, mine, theirs, gain, kinds):
    rows, width = mine.shape
    size = min(128, rows)
    steps = rows // size
    tile = pl.BlockSpec((size, width), lambda i, at: (i, 0))
    half = pl.BlockSpec((size, width), lambda i, at: (at[0] * steps + i, 0))
    line = pl.BlockSpec((1, width), lambda i, at: (0, 0))
    return call_at(
        name,
        norm_back_kernel,
        at,
        (steps,),
        [half if x.shape[0] > rows else tile, half if base.shape[0] > rows else tile, tile, tile, line],
        (x, base, mine, theirs, gain),
        [(like(mine.shape, kind), tile) for kind in kinds] + [(like((1, width), jnp.float32), line)],
    )


def half_places(at_ref, rows):
    half = rows // 2
    return [pl.ds(pl.multiple_of(which * half, half), half) for which in (at_ref[0], 1 - at_ref[0])]


def project_kernel(x_ref, weight_ref, out_ref):
    out_ref[...] = matmul_low(x_ref[...], weight_ref[...]).astype(out_ref.dtype)


def project(name, x, weight, start, width, kind):
    rows, depth = x.shape
    size = math.gcd(256, width)
    return call(
        name,
        project_kernel,
        (width // size,),
        [
            pl.BlockSpec((rows, depth), lambda j: (0, 0)),
            pl.BlockSpec((depth, size), lambda j: (0, start // size + j)),
        ],
        (x, weight),
        [(like((rows, width), kind), pl.BlockSpec((rows, size), lambda j: (0, j)))],
        grant=VMEM_GRANT,
    )[0]


def expand_kernel(at_ref, mine_ref, other_ref, gate_ref, up_ref, dact_ref, act_ref, dgate_ref, dup_ref):
    for place, x_ref in zip(half_places(at_ref, dact_ref.shape[0]), (mine_ref, other_ref), strict=True):
        gate = matmul_low(x_ref[...], gate_ref[...])
        up = matmul_low(x_ref[...], up_ref[...])
        dact = dact_ref[place, :]
        logistic = jax.nn.sigmoid(gate)
        silu = gate * logistic
        act_ref[place, :] = narrow(silu * up)
        dgate_ref[place, :] = narrow(dact * up * (logistic * (1.0 + gate * (1.0 - logistic))))
        dup_ref[place, :] = narrow(dact * silu)


def expand(at, mine, other, weight, dact):
    half, depth = mine.shape
    rows, width = dact.shape
    size = min(256, width)
    steps = width // size
    tile = pl.BlockSpec((rows, size), lambda j, at: (0, j))
    return call_at(
        "expand",
        expand_kernel,
        at,
        (steps,),
        [
            pl.BlockSpec((half, depth), lambda j, at: (0, 0)),
            pl.BlockSpec((half, depth), lambda j, at: (0, 0)),
            pl.BlockSpec((depth, size), lambda j, at: (0, j)),
            pl.BlockSpec((depth, size), lambda j, at: (0, steps + j)),
            tile,
        ],
        (mine, other, weight, weight, dact),
        [(like((rows, width), jnp.bfloat16), tile)] * 3,
        VMEM_GRANT,
    )


def gather_kernel(at_ref, mine_ref, other_ref, out_ref):
    for place, half_ref in zip(half_places(at_ref, out_ref.shape[0]), (mine_ref, other_ref), strict=True):
        out_ref[place, :] = half_ref[...]


def gated_back_kernel(
    at_ref, mine_ref, other_ref, weight_ref, gate_ref, y_ref, dy_ref, dgate_ref
):
    for place, x_ref in zip(half_places(at_ref, gate_ref.shape[0]), (mine_ref, other_ref), strict=True):
        dgated = times_back(x_ref[...], weight_ref[...])
        gate = gate_ref[place, :]
        logistic = jax.nn.sigmoid(gate)
        dy_ref[place, :] = narrow(dgated * (gate * logistic))
        dgate_ref[place, :] = narrow(
            dgated * y_ref[place, :] * (logistic * (1.0 + gate * (1.0 - logistic)))
        )


def gated_back(at, mine, other, weight, gate, y):
    half, depth = mine.shape
    rows, width = gate.shape
    size = min(256, width)
    tile = pl.BlockSpec((rows, size), lambda j, at: (0, j))
    whole = pl.BlockSpec((half, depth), lambda j, at: (0, 0))
    return call_at(
        "gated_back",
        gated_back_kernel,
        at,
        (width // size,),
        [whole, whole, pl.BlockSpec((size, depth), lambda j, at: (j, 0)), tile, tile],
        (mine, other, weight, gate, y),
        [(like((rows, width), jnp.bfloat16), tile)] * 2,
        VMEM_GRANT,
    )


def rows_back_kernel(at_ref, mine_ref, other_ref, weight_ref, out_ref):
    for place, x_ref in zip(half_places(at_ref, out_ref.shape[0]), (mine_ref, other_ref), strict=True):
        out_ref[place, :] = narrow(times_back(x_ref[...], weight_ref[...]))


def rows_back(at, mine, other, weight):
    half, depth = mine.shape
    width = weight.shape[0]
    size = min(256, width)
    whole = pl.BlockSpec((half, depth), lambda j, at: (0, 0))
    return call_at(
        "attended_back",
        rows_back_kernel,
        at,
        (width // size,),
        [whole, whole, pl.BlockSpec((size, depth), lambda j, at: (j, 0))],
        (mine, other, weight),
        [(like((2 * half, width), jnp.bfloat16), pl.BlockSpec((2 * half, size), lambda j, at: (0, j)))],
    )[0]


def share_kernel(at_ref, *refs, count, back, added):
    total = jnp.zeros(refs[-1].shape, jnp.float32)
    for former, latter in zip(refs[:count], refs[count : 2 * count], strict=True):
        product = times_back if back else matmul_low
        total = total + product(former[...], latter[...])
    if added:
        total = total + wide(refs[2 * count][...])
    refs[-1][...] = narrow(total)


def half_share(name, at, terms, back, added=None):
    rows = terms[0][0].shape[0] // 2
    width = terms[0][1].shape[0 if back else 1]
    size = min(1024, width)
    specs = [pl.BlockSpec((rows, former.shape[1]), lambda j, at: (at[0], 0)) for former, _, _ in terms]
    for former, latter, columns in terms:
        if back:
            specs.append(pl.BlockSpec((size, former.shape[1]), lambda j, at, c=columns: (j, c)))
        else:
            specs.append(pl.BlockSpec((former.shape[1], size), lambda j, at: (0, j)))
    args = [term[0] for term in terms] + [term[1] for term in terms]
    tile = pl.BlockSpec((rows, size), lambda j, at: (0, j))
    if added is not None:
        specs.append(tile)
        args.append(added)
    kernel = partial(share_kernel, count=len(terms), back=back, added=added is not None)
    outs = [(like((rows, width), jnp.bfloat16), tile)]
    return call_at(name, kernel, at, (width // size,), specs, args, outs, VMEM_GRANT)[0]


def weight_kernel(at_ref, *refs, ranks, counts):
    out_ref = refs[-1]
    refs = list(refs[:-1])
    firsts = [[refs.pop(0)[...].T for _ in range(2 * ranks)] for _ in counts]
    at = 0
    for first, count in zip(firsts, counts, strict=True):
        seconds = [refs.pop(0) for _ in range(ranks * count)]
        places = half_places(at_ref, seconds[0].shape[0])
        for index in range(count):
            width = seconds[index].shape[1]
            for start in range(0, width, 512):
                stop = min(width, start + 512)
                total = None
                for rank in range(ranks):
                    ref = seconds[count * rank + index]
                    for which in range(2):
                        part = matmul_low(first[2 * rank + which], ref[places[which], start:stop])
                        total = part if total is None else total + part
                out_ref[:, at + start : at + stop] = narrow(total)
            at = at + width


def weight_grad(name, core, sets, *awaited):
    ranks = lax.axis_size("dp")
    dp_rank = lax.axis_index("dp")
    at = after(jnp.stack([core, dp_rank]).astype(jnp.int32), *awaited)
    specs, args, pieces, counts = ([], [], [], [])
    width = 0
    for own, others, seconds, arrived in sets:
        own = list(own) if isinstance(own, tuple) else [own]
        others = [array for pair in others for array in pair]
        groups = [list(seconds)] + [list(group) for group in arrived]
        half = seconds[0].shape[0] // 2
        share = own[0].shape[1] // ranks
        size = min(256, share)
        steps = share // size

        def spec(row, from_dp, half=half, size=size, steps=steps):
            return pl.BlockSpec(
                (half, size), lambda m, at: (row(at), m + (steps * at[1] if from_dp else 0))
            )

        if len(own) == 2:
            specs += 2 * [spec(lambda at: 0, True)]
        else:
            specs += [spec(lambda at: at[0], True), spec(lambda at: 1 - at[0], True)]
            own = 2 * own
        specs += [spec(lambda at: 0, False) for _ in others]
        args += own + others
        for group in groups:
            pieces += group
        counts.append(len(seconds))
        width = width + sum(part.shape[1] for part in seconds)
    for array in pieces:
        specs.append(pl.BlockSpec(array.shape, lambda m, at: (0, 0)))
        args.append(array)
    kernel = partial(weight_kernel, ranks=ranks, counts=tuple(counts))
    out = like((share, width), jnp.bfloat16)
    tile = pl.BlockSpec((size, width), lambda m, at: (m, 0))
    made = call_at(name, kernel, at, (steps,), specs, args, [(out, tile)])[0]
    return (made, lax.psum_scatter(made, "ctx", scatter_dimension=0, tiled=True))


def listed(*arrived):
    return [list(group) for group in zip(*arrived, strict=True)]


def body(
    hidden,
    cotangent,
    norm1_gain,
    ssm_in,
    ssm_bc,
    ssm_dt,
    dt_bias,
    a_log,
    d_skip,
    ssm_out,
    attn_q,
    attn_kv,
    attn_out,
    norm2_gain,
    mlp_gate_up,
    mlp_down,
):
    ctx_rank = lax.axis_index("ctx")
    ctx_count = lax.axis_size("ctx")
    tensor_rank = lax.axis_index("tensor")
    core = tensor_rank % 2
    chip = tensor_rank // 2
    hidden_rows = hidden[0]
    grad_low = cotangent[0]
    tokens, model_width = hidden_rows.shape
    half = tokens // 2
    inner_local = ssm_in.shape[2]
    heads_local = ssm_dt.shape[1]
    head_width = inner_local // heads_local
    head_pairs = heads_local // 2
    state_width = ssm_bc.shape[2]
    bc_share = 2 * state_width // 4
    heads_query = attn_q.shape[1] // AHEAD_DIM
    ff_local = mlp_down.shape[0]
    here = core.astype(jnp.int32)[None]
    there = 1 - here
    gain_one = norm1_gain[None]
    gain_two = norm2_gain[None]

    input_one = normed(hidden_rows, gain_one)
    in_matrix = ssm_in.reshape(model_width, 2 * inner_local)
    bc_matrix = ssm_bc.reshape(model_width, 2 * state_width)
    source_rows = project("project_u", input_one, in_matrix, inner_local, inner_local, jnp.bfloat16)
    bc_rows = matmul_low(input_one, bc_matrix).astype(jnp.bfloat16)
    write_rows = bc_rows[:, :state_width]
    read_rows = bc_rows[:, state_width:]
    dt_pre = lax.dot_general(
        ssm_dt, input_one, (((0,), (1,)), ((), ())), preferred_element_type=jnp.float32
    ) + dt_bias[:, None]
    dt_rows = jax.nn.softplus(dt_pre)
    decay_rate = -jnp.exp(a_log)
    running = jnp.cumsum(dt_rows * decay_rate[:, None], axis=1)

    def by_head(value):
        return jnp.broadcast_to(value[:, None], (heads_local, tokens))

    small_rows = jnp.stack([running, dt_rows, by_head(d_skip), by_head(decay_rate)], axis=1)
    small_rows = small_rows.reshape(head_pairs, 2, 4, tokens).transpose(0, 2, 1, 3)
    small_rows = small_rows.reshape(head_pairs, 8, tokens)
    scan = Scan(tokens, inner_local, state_width)
    own_state = scan.own_state(source_rows, small_rows, write_rows, True)

    one_late = after(input_one, own_state)
    kv_pair = cut(attn_kv, chip, AHEAD_DIM, 2)
    key_value = matmul_low(one_late, kv_pair.reshape(model_width, 2 * AHEAD_DIM)).astype(jnp.bfloat16)
    kv_sent = cut(key_value, core, AHEAD_DIM, 1)
    kv_got = [kv_sent] + [moved(kv_sent, "ctx", shift) for shift in range(1, ctx_count)]
    cot_sent = send_columns(cut(after(grad_low, own_state), core, half, 0))
    one_sent = send_columns(cut(one_late, core, half, 0))
    queries = matmul_low(one_late, attn_q).astype(jnp.bfloat16)
    gate_ssm = project("project_z", one_late, in_matrix, 0, inner_local, jnp.float32)
    attend = Attend(tokens, ctx_count * tokens, heads_query)
    rank = ctx_rank.astype(jnp.int32)[None]
    kept = {}

    def fill_within(sent):
        kept["within"] = scan.within(source_rows, after(small_rows, own_state), write_rows, read_rows)
        return (kept["within"], gate_ssm, queries, cot_sent)

    def fill_attend(sent):
        mine = jnp.concatenate(kv_got, axis=0)
        other = partner(mine, CORE)
        kept["key"] = jnp.where(core == 0, mine, other)
        kept["value"] = jnp.where(core == 0, other, mine)
        kept["attended"], kept["log"] = attend.forward(
            after(rank, sent), queries, kept["key"], kept["value"]
        )
        kept["attended_sent"] = send_rows(kept["attended"])
        return (kept["attended"], one_sent)

    def fill_act(sent):
        kept["act"] = times_back(after(grad_low, sent), mlp_down)
        return (kept["act"],)

    entering = chained(own_state, running[:, -1], True, [fill_within, fill_attend, fill_act])
    key_rows, value_rows, attended = (kept["key"], kept["value"], kept["attended"])
    ssm_values, gated_rows = scan.carried(kept["within"], gate_ssm, small_rows, read_rows, entering)
    outs_sent = [
        [gated, att] for gated, att in zip(send_rows(gated_rows), kept["attended_sent"], strict=True)
    ]

    terms = [(gated_rows, ssm_out, 0), (attended, attn_out, 0)]
    given = partner(half_share("mix_other", there, terms, False), CORE)
    mix_mine = half_share("mix_own", here, terms, False, given)
    mix_theirs = partner(mix_mine, CHIP)
    gu_matrix = after(mlp_gate_up, mix_mine).reshape(model_width, 2 * ff_local)
    cot_columns = both_halves([after(part, mix_mine) for part in cot_sent])
    one_columns = both_halves([after(part, mix_mine) for part in one_sent])
    kv_columns = lax.dynamic_index_in_dim(after(kv_pair, mix_mine), core, 1, keepdims=False)
    pad = -heads_local % AHEAD_DIM
    weight_small = jnp.concatenate(
        [
            kv_columns,
            cut(bc_matrix, 2 * core + chip, bc_share, 1),
            jnp.pad(ssm_dt, ((0, 0), (0, pad))),
        ],
        axis=1,
    )
    mix_theirs = after(mix_theirs, gu_matrix, cot_columns, one_columns, weight_small, outs_sent)
    middle, two_mine, mix_squares = middle_norm(here, hidden_rows, mix_mine, mix_theirs, gain_two)

    two_other = partner(two_mine, CORE)
    activated, grad_gate, grad_up = expand(here, two_mine, two_other, gu_matrix, kept["act"])
    act_sent = send_rows(activated)
    two_sent = send_columns(two_mine)
    gate_sent = send_rows(grad_gate)
    up_sent = send_rows(grad_up)
    terms = [(grad_gate, gu_matrix, 0), (grad_up, gu_matrix, 1)]
    given = partner(half_share("two_other", there, terms, True), CORE)
    two_back = half_share("two_own", here, terms, True, given)
    two_theirs = partner(two_back, CHIP)
    down_made, down_sum = weight_grad(
        "grad_down", core, [(grad_low, cot_columns, [activated], listed(act_sent))], two_back
    )
    two_theirs = after(two_theirs, down_made)
    grad_middle, mix_grad_mine, gain_two_sum = norm_grad(
        "norm_two_back", here, middle, grad_low, two_back, two_theirs, gain_two, (jnp.float32, jnp.bfloat16)
    )

    mix_grad_other = partner(mix_grad_mine, CORE)
    mix_sent = send_columns(mix_grad_mine)
    two_pair = (two_mine, two_other)
    two_columns = both_halves([after(part, two_theirs) for part in two_sent])
    gate_made, gate_sum = weight_grad(
        "grad_gate", core, [(two_pair, two_columns, [grad_gate], listed(gate_sent))], mix_grad_mine
    )
    grad_values, grad_gate_ssm = gated_back(
        after(here, gate_made), mix_grad_mine, mix_grad_other, ssm_out, gate_ssm, ssm_values
    )
    own_grad = scan.own_state(grad_values, small_rows, read_rows, False)
    z_sent = send_rows(grad_gate_ssm)
    mlp_terms = [(activated, mlp_down, 0)]

    def fill_attend_back(sent):
        kept["mlp_given"] = partner(half_share("mlp_other", after(there, sent), mlp_terms, False), CORE)
        grad_attended = rows_back(after(here, sent), mix_grad_mine, mix_grad_other, attn_out)
        kept["grads"] = attend.back(rank, queries, grad_attended, kept["log"], key_rows, value_rows)
        grad_query, grad_key, grad_value = kept["grads"]
        kept["query_sent"] = send_rows(grad_query)
        kept["kv_given"] = jnp.where(core == 0, grad_value, grad_key).astype(jnp.bfloat16)
        return (grad_query, kept["kv_given"], up_sent, kept["mlp_given"])

    def fill_scan_back(sent):
        given = partner(after(kept["kv_given"], sent), CORE)
        kept["up"] = weight_grad(
            "grad_up", core, [(two_pair, two_columns, [grad_up], listed(up_sent))], sent
        )
        kept["scan"] = scan.within_back(
            source_rows, after(grad_values, kept["up"][0]), small_rows, write_rows, read_rows
        )
        _, grad_key, grad_value = kept["grads"]
        own_part = jnp.where(core == 0, grad_key, grad_value)
        paired = (own_part + given.astype(jnp.float32)).reshape(ctx_count, tokens, AHEAD_DIM)
        kept["kv"] = [paired[0]] + [paired[shift].astype(jnp.bfloat16) for shift in range(1, ctx_count)]
        kept["mix_columns"] = both_halves([after(part, sent) for part in mix_sent])
        return (kept["scan"][0], kept["kv"], kept["mix_columns"], z_sent, kept["query_sent"])

    def fill_weights(sent):
        kept["kv_back"] = [
            moved(after(part, sent), "ctx", -shift) for shift, part in enumerate(kept["kv"]) if shift
        ]
        kept["mlp_mine"] = half_share("mlp_own", after(here, sent), mlp_terms, False, kept["mlp_given"])
        kept["mixer"] = weight_grad(
            "grad_mixer",
            core,
            [
                ((mix_grad_mine, mix_grad_other), kept["mix_columns"], [gated_rows, attended], outs_sent),
                (
                    input_one,
                    one_columns,
                    [grad_gate_ssm, kept["grads"][0]],
                    listed(z_sent, kept["query_sent"]),
                ),
            ],
            kept["mlp_mine"],
        )
        return (kept["mixer"][0],)

    leaving = chained(own_grad, running[:, -1], False, [fill_attend_back, fill_scan_back, fill_weights])
    grad_query = kept["grads"][0]
    grad_written, scan_sums, grad_b, grad_c = kept["scan"]
    grad_source, steps, grad_b, grad_c = scan.carried_back(
        source_rows, grad_values, small_rows, scan_sums, grad_written,
        write_rows, read_rows, entering, leaving, grad_b, grad_c,
    )
    source_sent = send_rows(grad_source)
    grad_bc = jnp.concatenate([grad_b, grad_c], axis=1)
    bc_sent = partner(cut(grad_bc, 1 - core, 2 * bc_share, 1).astype(jnp.bfloat16), CORE)
    bc_mine = cut(grad_bc, core, 2 * bc_share, 1) + bc_sent.astype(jnp.float32)
    bc_given = partner(cut(bc_mine, 1 - chip, bc_share, 1).astype(jnp.bfloat16), CHIP)
    grad_bc_low = (cut(bc_mine, chip, bc_share, 1) + bc_given.astype(jnp.float32)).astype(jnp.bfloat16)
    kv_sum = kept["kv"][0]
    for part in kept["kv_back"]:
        kv_sum = kv_sum + part.astype(jnp.float32)
    grad_kv_low = kv_sum.astype(jnp.bfloat16)
    grad_dt_pre = steps[:, 0:2].reshape(heads_local, tokens) * jax.nn.sigmoid(dt_pre)
    flow_rows = steps[:, 2:4].reshape(heads_local, tokens)
    grad_dt_bias = jnp.sum(grad_dt_pre, axis=1)
    grad_a_log = decay_rate * jnp.sum(dt_rows * flow_rows, axis=1)
    grad_d_skip = jnp.sum(scan_sums[:, 4, : 2 * head_width].reshape(heads_local, head_width), axis=1)
    grad_dt_low = grad_dt_pre.astype(jnp.bfloat16)
    grad_small = jnp.concatenate([grad_kv_low, grad_bc_low], axis=1)
    grad_dt_all = jnp.concatenate(
        [grad_small, jnp.pad(grad_dt_low.T, ((0, 0), (0, pad)))], axis=1
    )
    small_sent = send_rows(grad_small)
    terms = [
        (grad_gate_ssm, in_matrix, 0),
        (grad_source, in_matrix, 1),
        (grad_query, attn_q, 0),
        (grad_dt_all, weight_small, 0),
    ]
    mlp_theirs = partner(after(kept["mlp_mine"], grad_bc_low), CHIP)
    given = partner(half_share("one_other", after(there, source_sent, down_sum, gate_sum, kept["up"][1]), terms, True), CORE)
    one_back = half_share("one_own", after(here, mlp_theirs), terms, True, given)
    one_theirs = partner(one_back, CHIP)
    last_made, last_sum = weight_grad(
        "grad_last",
        core,
        [(input_one, one_columns, [grad_source, grad_small], listed(source_sent, small_sent))],
        one_back,
    )
    one_theirs = after(one_theirs, last_made, kept["mixer"][1])
    hidden_mine, gain_one_sum = norm_grad(
        "norm_one_back", here, hidden_rows, grad_middle, one_back, one_theirs, gain_one, (jnp.bfloat16,)
    )
    grad_hidden = gather_rows("gather_hidden", here, hidden_mine)
    step_share = matmul_low(after(grad_dt_low, hidden_mine), input_one).T
    grad_ssm_dt = scatter_sum(scatter_sum(step_share, "dp"), "ctx")
    mlp_total = wide(kept["mlp_mine"]) + wide(after(mlp_theirs, hidden_mine))
    block_out = middle + mlp_total
    output = gather_rows("gather_output", here, block_out.astype(jnp.bfloat16))
    squares = jnp.stack([jnp.sum(mix_squares), jnp.sum(mlp_total * mlp_total), jnp.sum(block_out * block_out)])
    def line(*parts):
        flat = jnp.concatenate(parts)
        return jnp.pad(flat, (0, model_width - flat.shape[0]))[None]

    halves = jnp.concatenate([gain_one_sum, gain_two_sum, line(squares)], axis=0)
    halves = halves + partner(halves, CORE)
    sums = jnp.concatenate([halves, line(grad_dt_bias, grad_a_log, grad_d_skip)], axis=0)
    sums = all_sum(all_sum(sums, "dp"), "ctx")

    grad_last = wide(after(last_sum, kept["mixer"][1], sums, grad_ssm_dt, output, grad_hidden))
    grad_little = grad_last[:, inner_local:]
    held = narrow(grad_little[:, : AHEAD_DIM + bc_share])
    pieces = jnp.stack([held] + [partner(held, stride) for stride in range(1, 4)])

    def of_rank(rank):
        return lax.dynamic_index_in_dim(pieces, tensor_rank ^ rank, 0, keepdims=False).astype(jnp.float32)

    by_rank = [of_rank(rank) for rank in range(4)]
    kv_rows = held.shape[0] // 4
    kv_parts = [cut(part[:, :AHEAD_DIM], tensor_rank, kv_rows, 0) for part in by_rank]
    grad_attn_kv = jnp.stack(
        [jnp.concatenate([kv_parts[kind], kv_parts[2 + kind]], axis=1) for kind in range(2)], axis=1
    )
    grad_ssm_bc = jnp.concatenate(
        [by_rank[2 * (place % 2) + place // 2][:, AHEAD_DIM:] for place in range(4)], axis=1
    ).reshape(-1, 2, state_width)

    place = lax.axis_index("dp") * ctx_count + ctx_rank
    share = model_width // (lax.axis_size("dp") * ctx_count)
    small = sums[3]
    counted = tokens * model_width * lax.axis_size("dp") * ctx_count
    grad_down = wide(down_sum)
    grad_gate_up = jnp.stack([wide(gate_sum), wide(kept["up"][1])], axis=1)
    grad_mixer = wide(after(kept["mixer"][1], grad_gate_up))
    outs_width = inner_local + heads_query * AHEAD_DIM
    grad_outs = grad_mixer[:, :outs_width]
    grad_first = grad_mixer[:, outs_width:]
    branch_rms = jnp.sqrt(sums[2, :3] / counted)
    return (
        output[None],
        grad_hidden[None],
        cut(sums[0], place, share, 0),
        jnp.stack([grad_first[:, :inner_local], grad_last[:, :inner_local]], axis=1),
        grad_ssm_bc,
        grad_ssm_dt,
        small[:heads_local],
        small[heads_local : 2 * heads_local],
        small[2 * heads_local : 3 * heads_local],
        grad_outs[:, :inner_local].T,
        grad_first[:, inner_local:],
        grad_attn_kv,
        grad_outs[:, inner_local:].T,
        cut(sums[1], place, share, 0),
        grad_gate_up,
        grad_down.T,
        branch_rms,
    )


def solution(mesh):
    return jax.shard_map(
        body,
        mesh=mesh,
        in_specs=(
            P("dp", "ctx", None),
            P("dp", "ctx", None),
            P(),
            P(None, None, "tensor"),
            P(),
            P(None, "tensor"),
            P("tensor"),
            P("tensor"),
            P("tensor"),
            P("tensor", None),
            P(None, "tensor"),
            P(),
            P("tensor", None),
            P(),
            P(None, None, "tensor"),
            P("tensor", None),
        ),
        out_specs=(
            P("dp", "ctx", None),
            P("dp", "ctx", None),
            P(("dp", "ctx")),
            P(("dp", "ctx"), None, "tensor"),
            P(("dp", "ctx"), None, None),
            P(("dp", "ctx"), "tensor"),
            P("tensor"),
            P("tensor"),
            P("tensor"),
            P("tensor", ("dp", "ctx")),
            P(("dp", "ctx"), "tensor"),
            P(("dp", "ctx", "tensor"), None, None),
            P("tensor", ("dp", "ctx")),
            P(("dp", "ctx")),
            P(("dp", "ctx"), None, "tensor"),
            P("tensor", ("dp", "ctx")),
            P(),
        ),
        check_vma=False,
    )
```
